32 devices in a mesh: fsdp: 4 (over x, core), seq: 8 (over z, y).
Axes of the slice: x: 2, y: 2, z: 4, core: 2. Of those that a mesh axis runs over, the one named last changes fastest.
Arguments:
- tokens: bfloat16 [4096, 2048], P(('fsdp', 'seq')), may hold values from -6 to 6
- cotangent: bfloat16 [4096, 2048], P(('fsdp', 'seq')), may hold values from -6 to 6
- expert_ids: int32 [4096, 8], P(('fsdp', 'seq')), may hold values from 0 to 15, all different within a row; in each aligned block of 128 rows (0 to 127, 128 to 255, ...) at most 85 rows name the same one
- attn_gain: bfloat16 [2048], P(('fsdp', 'seq')), may hold values from 0.5 to 1.5
- w_query: bfloat16 [2048, 4096], P(('fsdp', 'seq')), may hold values from -0.125 to 0.125
- w_key: bfloat16 [2048, 512], P(('fsdp', 'seq')), may hold values from -0.125 to 0.125
- w_value: bfloat16 [2048, 512], P(('fsdp', 'seq')), may hold values from -0.125 to 0.125
- query_gain: bfloat16 [128], P(('fsdp', 'seq')), may hold values from 0.5 to 1.5
- key_gain: bfloat16 [128], P(('fsdp', 'seq')), may hold values from 0.5 to 1.5
- w_output: bfloat16 [4096, 2048], P(('fsdp', 'seq')), may hold values from -0.75 to 0.75
- mlp_gain: bfloat16 [2048], P(('fsdp', 'seq')), may hold values from 0.5 to 1.5
- w_router: bfloat16 [2048, 16], P(('fsdp', 'seq')), may hold values from -0.0625 to 0.0625
- w_gate: bfloat16 [16, 2048, 768], P('seq', 'fsdp'), may hold values from -0.125 to 0.125
- w_up: bfloat16 [16, 2048, 768], P('seq', 'fsdp'), may hold values from -0.125 to 0.125
- w_down: bfloat16 [16, 768, 2048], P('seq', None, 'fsdp'), may hold values from -0.875 to 0.875
Outputs:
- layer_out: bfloat16 [4096, 2048], P(('fsdp', 'seq'))
- grad_tokens: bfloat16 [4096, 2048], P(('fsdp', 'seq'))
- grad_attn_gain: float32 [2048], P(('fsdp', 'seq'))
- grad_query: float32 [2048, 4096], P(('fsdp', 'seq'))
- grad_key: float32 [2048, 512], P(('fsdp', 'seq'))
- grad_value: float32 [2048, 512], P(('fsdp', 'seq'))
- grad_query_gain: float32 [128], P(('fsdp', 'seq'))
- grad_key_gain: float32 [128], P(('fsdp', 'seq'))
- grad_output: float32 [4096, 2048], P(('fsdp', 'seq'))
- grad_mlp_gain: float32 [2048], P(('fsdp', 'seq'))
- grad_router: float32 [2048, 16], P(('fsdp', 'seq'))
- grad_gate: float32 [16, 2048, 768], P('seq', 'fsdp')
- grad_up: float32 [16, 2048, 768], P('seq', 'fsdp')
- grad_down: float32 [16, 768, 2048], P('seq', None, 'fsdp')
The draws below stay inside these ranges and needn't reach their ends.
Inputs may be any that keep to these rules, and one draw needn't show every extreme that they name: `expert_ids`: each row names 8 different experts. In each aligned block of 128 rows (the rows of one device) no expert is named by more than 85 rows, a bound that some block reaches.
All inputs are finite; a program needn't handle non-finite values.
Results may differ from the reference program's by a relative error of at most 0.025.
Values may be sent and summed in bfloat16 or wider, within the bound.
No kernel may reach another device: no remote copies, remote signals or barrier semaphores. Data moves between devices by JAX's collectives and lax.ppermute only.
A program may use at most 320 MiB of HBM per device.

```python
import math
import jax
import jax.numpy as jnp
import numpy as np
from jax import lax

D = 2048
HEADS = 32
KV_HEADS = 4
HEAD_DIM = 128
FF = 768
TOP = 8
TOK_DEV = 128
EXPERTS = 16
SEQ_LEN = 1024
TOKENS = 4096
CAP = 85
N_FSDP = 4
N_SEQ = 8


def level_of(stream_key, dims, split, smallest, largest):
    def one(dim, parts):
        draws = jax.random.uniform(jax.random.fold_in(jax.random.fold_in(stream_key, 6), dim), (parts,), jnp.float32, smallest / len(split), largest / len(split))
        return jnp.repeat(jnp.exp(draws), dims[dim] // parts).reshape((-1,) + (1,) * (len(dims) - dim - 1))

    factor_of = one(*split[0])
    for cut in split[1:]:
        factor_of = factor_of * one(*cut)
    return factor_of


def assign_block(stream_key, own, number, rows, count, top, most, lean):
    sequence = jax.random.permutation(stream_key, count)
    packed, ordinary = portions_of(count, rows * top, most, lean, True), portions_of(count, rows * top, most, lean, False)
    places = jnp.arange(count)

    def named(tallies, rotation):
        used = int((tallies > 0).sum())
        fixed = max(1, used // 4)
        passed = fixed + (places - fixed + rotation * (used - fixed)) % max(1, count - fixed)
        return jnp.zeros((count,), jnp.int32).at[sequence[jnp.where(places < fixed, places, passed)]].set(jnp.asarray(tallies, jnp.int32))

    tallies = jnp.where(number % 4 == 0, named(packed, number // 4), named(ordinary, number - number // 4 - 1))
    mixed = jax.random.permutation(jax.random.fold_in(own, 3), count)
    donor, taker = mixed[0:count // 2 * 2:2], mixed[1:count // 2 * 2:2]
    room = jnp.minimum(tallies[donor] - 1, most - tallies[taker]) // 2
    room = jnp.where((donor == sequence[0]) | (taker == sequence[0]) | (tallies[taker] == 0), 0, jnp.maximum(room, 0))
    passed = jax.random.randint(jax.random.fold_in(own, 4), (count // 2,), 0, 1 << 20) % (room + 1)
    tallies = tallies.at[donor].add(-passed).at[taker].add(passed)
    members = jnp.searchsorted(jnp.cumsum(tallies), jnp.arange(rows * top), side="right").astype(jnp.int32)
    table = members.reshape(top, rows).T
    table = table[jax.random.permutation(jax.random.fold_in(own, 1), rows)]
    rotation = jax.random.randint(jax.random.fold_in(own, 2), (rows, 1), 0, top)
    return jnp.take_along_axis(table, (jnp.arange(top)[None, :] + rotation) % top, axis=1)


def portions_of(amount, total, most, skew, full):
    weights = [(1 << 20) // math.isqrt(standing ** skew) + 1 for standing in range(1, amount + 1)]
    largest = most if full else min(most, max(-(-total // amount), total * weights[0] // sum(weights)))
    least = 1 if total - largest >= amount - 1 else 0
    counts, surplus = [largest] + [least] * (amount - 1), total - largest - least * (amount - 1)
    while surplus > 0:
        candidates = [i for i in range(1, amount) if counts[i] < largest] or [i for i in range(1, amount) if counts[i] < most]
        mass, budget = sum([weights[i] for i in candidates]), surplus
        for i in candidates:
            addition = min(most - counts[i], max(1, budget * weights[i] // mass), surplus)
            counts[i] = counts[i] + addition
            surplus = surplus - addition
    return np.array(counts)


def bell_draw(own_key, shape, spread, most, cuts=(), kind=jnp.bfloat16):
    entries = jax.random.normal(own_key, shape, jnp.float32) * spread
    if len(cuts) > 0:
        entries = level_of(own_key, shape, cuts, -0.22, 0.18) * entries
    return jnp.clip(entries, min=-most, max=most).astype(kind)


def setup_inputs(seed: int = 0) -> dict:
    key_list = jax.random.split(jax.random.key(seed), 16)
    tokens = bell_draw(key_list[0], (TOKENS, D), 1.0, 6.0, ((0, 32),))
    cotangent = bell_draw(key_list[1], (TOKENS, D), 1.0, 6.0, ((0, 32),))
    expert_ids_keys = jax.random.split(jax.random.fold_in(key_list[2], 1), TOKENS // TOK_DEV)
    expert_ids_turns = jax.random.permutation(jax.random.fold_in(key_list[2], 3), TOKENS // TOK_DEV)
    expert_ids = jax.vmap(lambda own, number: assign_block(jax.random.fold_in(key_list[2], 2), own, number, TOK_DEV, EXPERTS, TOP, CAP, 2))(expert_ids_keys, expert_ids_turns).reshape((TOKENS, TOP))
    attn_gain = jnp.clip(1.0 + 0.1 * jax.random.normal(key_list[3], (D,), jnp.float32), 0.5, 1.5).astype(jnp.bfloat16)
    w_query = bell_draw(key_list[4], (D, HEADS * HEAD_DIM), D ** -0.5, 0.125, ((0, 32),))
    w_key = bell_draw(key_list[5], (D, KV_HEADS * HEAD_DIM), D ** -0.5, 0.125, ((0, 32),))
    w_value = bell_draw(key_list[6], (D, KV_HEADS * HEAD_DIM), D ** -0.5, 0.125, ((0, 32),))
    query_gain = jnp.clip(1.0 + 0.1 * jax.random.normal(key_list[7], (HEAD_DIM,), jnp.float32), 0.5, 1.5).astype(jnp.bfloat16)
    key_gain = jnp.clip(1.0 + 0.1 * jax.random.normal(key_list[8], (HEAD_DIM,), jnp.float32), 0.5, 1.5).astype(jnp.bfloat16)
    w_output = bell_draw(key_list[9], (HEADS * HEAD_DIM, D), (HEAD_DIM // 2) ** -0.5, 0.75, ((0, 32),))
    mlp_gain = jnp.clip(1.0 + 0.1 * jax.random.normal(key_list[10], (D,), jnp.float32), 0.5, 1.5).astype(jnp.bfloat16)
    w_router = bell_draw(key_list[11], (D, EXPERTS), (4 * D) ** -0.5, 0.0625, ((0, 32),))
    w_gate = bell_draw(key_list[12], (EXPERTS, D, FF), D ** -0.5, 0.125, ((0, 8), (1, 4)))
    w_up = bell_draw(key_list[13], (EXPERTS, D, FF), D ** -0.5, 0.125, ((0, 8), (1, 4)))
    w_down = bell_draw(key_list[14], (EXPERTS, FF, D), (FF // 16) ** -0.5, 0.875, ((0, 8), (2, 4)))
    return dict(tokens=tokens, cotangent=cotangent, expert_ids=expert_ids, attn_gain=attn_gain, w_query=w_query, w_key=w_key, w_value=w_value, query_gain=query_gain, key_gain=key_gain, w_output=w_output, mlp_gain=mlp_gain, w_router=w_router, w_gate=w_gate, w_up=w_up, w_down=w_down)


@jax.custom_vjp
def low(v):
    return lax.optimization_barrier(v.astype(jnp.bfloat16)).astype(jnp.float32)

@jax.custom_vjp
def low_back(v):
    return v

def low_keep(v):
    return (low(v), None)

def low_pass(kept, grad):
    return (grad,)

def back_keep(v):
    return (v, None)

def back_low(kept, grad):
    return (low(grad),)
low.defvjp(low_keep, low_pass)
low_back.defvjp(back_keep, back_low)
NORM_EPS = 1e-06
ROPE_BASE = 1000000.0
NEG_LARGE = -1e+30
HIGHEST = lax.Precision.HIGHEST

def norm_rows(values, gain):
    row_scale = lax.rsqrt(lax.optimization_barrier(jnp.mean(values * values, axis=-1, keepdims=True)) + NORM_EPS)
    return values * row_scale * gain

def rotary_tables(positions, head_size):
    half_size = head_size // 2
    frequency = jnp.exp(jnp.arange(half_size, dtype=jnp.float32) * (-2.0 * math.log(ROPE_BASE) / head_size))
    angles = positions[:, None] * frequency[None, :]
    return (jnp.cos(angles)[:, None, :], jnp.sin(angles)[:, None, :])

def rotate(values, cos_table, sine_table):
    half_size = values.shape[-1] // 2
    first_half = values[..., :half_size]
    second_half = values[..., half_size:]
    return jnp.concatenate([first_half * cos_table - second_half * sine_table, second_half * cos_table + first_half * sine_table], axis=-1)

def attend_block(query_blk, key_seq, value_seq, first_row):
    block_rows = query_blk.shape[0]
    seq_rows = key_seq.shape[0]
    scores = jnp.einsum('qchd,kcd->chqk', query_blk, key_seq, precision=HIGHEST) * (1.0 / math.sqrt(HEAD_DIM))
    scores = low_back(scores)
    causal = jnp.arange(seq_rows, dtype=jnp.int32)[None, :] <= (first_row + jnp.arange(block_rows, dtype=jnp.int32))[:, None]
    scores = jnp.where(causal, scores, NEG_LARGE)
    weights_low = low(jax.nn.softmax(scores, axis=-1))
    return jnp.einsum('chqk,kcd->qchd', weights_low, value_seq, precision=HIGHEST)

def attend_sequence(operands):
    query_seq, key_seq, value_seq = operands
    block_rows = min(512, SEQ_LEN)
    block_count = SEQ_LEN // block_rows
    blocks = query_seq.reshape((block_count, block_rows) + query_seq.shape[1:])
    firsts = jnp.arange(block_count, dtype=jnp.int32) * block_rows
    checked = jax.checkpoint(attend_block)
    outputs = lax.map(lambda operand_pair: checked(operand_pair[0], key_seq, value_seq, operand_pair[1]), (blocks, firsts))
    return outputs.reshape(query_seq.shape)

def expert_rows(source, row_index, live_rows, gate_mat, up_mat, down_mat):
    entered = low_back(source[row_index] * live_rows[:, None])
    gate_pre = low_back(jnp.dot(entered, gate_mat, precision=HIGHEST))
    up_pre = low_back(jnp.dot(entered, up_mat, precision=HIGHEST))
    active = low(jax.nn.silu(gate_pre) * up_pre)
    return low_back(low(jnp.dot(active, down_mat, precision=HIGHEST)))

def reference(tokens, cotangent, expert_ids, attn_gain, w_query, w_key, w_value, query_gain, key_gain, w_output, mlp_gain, w_router, w_gate, w_up, w_down):
    head_local = HEADS // N_SEQ
    copies = N_SEQ // KV_HEADS
    block_total = TOKENS // TOK_DEV
    route_rows = TOK_DEV * TOP
    ids_block = expert_ids.reshape(block_total, route_rows)
    onehot = (ids_block[:, :, None] == jnp.arange(EXPERTS, dtype=jnp.int32)[None, None, :]).astype(jnp.int32)
    slot_index = lax.optimization_barrier(jnp.sum((jnp.cumsum(onehot, axis=1) - 1) * onehot, axis=-1))
    places = ids_block * (block_total * CAP) + jnp.arange(block_total, dtype=jnp.int32)[:, None] * CAP + slot_index
    places = places.reshape(-1).astype(jnp.int32)
    routes = jnp.arange(TOKENS * TOP, dtype=jnp.int32)
    slot_count = EXPERTS * block_total * CAP
    route_of = jnp.zeros((slot_count,), jnp.int32).at[places].set(routes)
    live_slots = jnp.zeros((slot_count,), jnp.float32).at[places].set(1.0)
    token_of = (route_of // TOP).reshape(EXPERTS, block_total * CAP)
    route_of = route_of.reshape(EXPERTS, block_total * CAP)
    live_slots = live_slots.reshape(EXPERTS, block_total * CAP)
    positions = (jnp.arange(TOKENS, dtype=jnp.int32) % SEQ_LEN).astype(jnp.float32)
    cos_table, sine_table = rotary_tables(positions, HEAD_DIM)

    def whole_layer(inputs, gain_a, query_w, key_w, value_w, gain_q, gain_k, output_w, gain_m, router_w, gate_w, up_w, down_w):
        hidden = low(norm_rows(inputs, gain_a))
        query_heads = low_back(jnp.dot(hidden, query_w, precision=HIGHEST)).reshape(TOKENS, HEADS, HEAD_DIM)
        key_heads = low_back(jnp.dot(hidden, key_w, precision=HIGHEST)).reshape(TOKENS, KV_HEADS, HEAD_DIM)
        value_heads = low_back(jnp.dot(hidden, value_w, precision=HIGHEST)).reshape(TOKENS, KV_HEADS, HEAD_DIM)
        query_heads = low_back(low(rotate(norm_rows(query_heads, gain_q), cos_table, sine_table)))
        key_heads = low_back(jnp.repeat(low(rotate(norm_rows(key_heads, gain_k), cos_table, sine_table)), copies, axis=1))
        value_heads = low_back(jnp.repeat(low(value_heads), copies, axis=1))
        attended = lax.map(attend_sequence, (query_heads.reshape(N_FSDP, SEQ_LEN, N_SEQ, head_local, HEAD_DIM), key_heads.reshape(N_FSDP, SEQ_LEN, N_SEQ, HEAD_DIM), value_heads.reshape(N_FSDP, SEQ_LEN, N_SEQ, HEAD_DIM)))
        attended = low_back(low(attended.reshape(TOKENS, HEADS * HEAD_DIM)))
        middle = inputs + low_back(jnp.dot(attended, output_w, precision=HIGHEST))
        mixer_in = low(norm_rows(middle, gain_m))
        logits = low_back(jnp.dot(mixer_in, router_w, precision=HIGHEST))
        gate_share = jax.nn.softmax(jnp.take_along_axis(logits, expert_ids, axis=1), axis=-1).reshape(-1)
        checked = jax.checkpoint(expert_rows)
        produced = lax.map(lambda operands: checked(mixer_in, operands[0], operands[1], operands[2], operands[3], operands[4]), (token_of, live_slots, gate_w, up_w, down_w))
        weighted = produced * (gate_share[route_of] * live_slots)[:, :, None]
        expert_sum = jnp.zeros((TOKENS, D), jnp.float32).at[token_of.reshape(-1)].add(weighted.reshape(-1, D))
        return middle + expert_sum
    result, pullback = jax.vjp(whole_layer, tokens.astype(jnp.float32), attn_gain.astype(jnp.float32), w_query.astype(jnp.float32), w_key.astype(jnp.float32), w_value.astype(jnp.float32), query_gain.astype(jnp.float32), key_gain.astype(jnp.float32), w_output.astype(jnp.float32), mlp_gain.astype(jnp.float32), w_router.astype(jnp.float32), w_gate.astype(jnp.float32), w_up.astype(jnp.float32), w_down.astype(jnp.float32))
    gradients = pullback(cotangent.astype(jnp.float32))
    return (result.astype(jnp.bfloat16), gradients[0].astype(jnp.bfloat16), gradients[1], gradients[2], gradients[3], gradients[4], gradients[5], gradients[6], gradients[7], gradients[8], gradients[9], gradients[10], gradients[11], gradients[12])
```

```python
import math

import jax
import jax.numpy as jnp
from jax import lax
from jax.sharding import PartitionSpec as P

NORM_EPS = 1e-06
ROPE_BASE = 1000000.0
NEG_LARGE = -1e30
F32 = jnp.float32
BF16 = jnp.bfloat16
ALL = ("fsdp", "seq")


def dot(left, right, left_dim, right_dim):
    return lax.dot_general(
        left, right, (((left_dim,), (right_dim,)), ((), ())), preferred_element_type=F32
    )


def norm_parts(values):
    row_scale = lax.rsqrt(jnp.mean(values * values, axis=-1, keepdims=True) + NORM_EPS)
    return (values * row_scale, row_scale)


def norm_back(grad_normed, normed, row_scale):
    return row_scale * (
        grad_normed - normed * jnp.mean(grad_normed * normed, axis=-1, keepdims=True)
    )


def rotary_tables(positions, head_size):
    half_size = head_size // 2
    frequency = jnp.exp(
        jnp.arange(half_size, dtype=F32) * (-2.0 * math.log(ROPE_BASE) / head_size)
    )
    angles = positions[:, None] * frequency[None, :]
    return (jnp.cos(angles)[:, None, :], jnp.sin(angles)[:, None, :])


def rotate(values, cos_table, sine_table):
    half_size = values.shape[-1] // 2
    first_half = values[..., :half_size]
    second_half = values[..., half_size:]
    return jnp.concatenate(
        [
            first_half * cos_table - second_half * sine_table,
            second_half * cos_table + first_half * sine_table,
        ],
        axis=-1,
    )


def unrotate(gradient, cos_table, sine_table):
    return rotate(gradient, cos_table, -sine_table)


def after(value, *others):
    return lax.optimization_barrier((value, *others))[0]


def ring_order(size):
    if size % 4 or size < 8:
        return list(range(size))
    wide = size // 4
    walk = [(0, y) for y in range(wide)]
    for z in range(1, 4):
        walk += [(z, y) for y in (range(wide - 1, 0, -1) if z % 2 else range(1, wide))]
    walk += [(z, 0) for z in (3, 2, 1)]
    return [z * wide + y for z, y in walk]


class Ring:
    def __init__(self, size):
        self.size = size
        self.order = ring_order(size)
        place = [0] * size
        for i, member in enumerate(self.order):
            place[member] = i
        self.here = jnp.asarray(place, jnp.int32)[lax.axis_index("seq")]
        self.table = jnp.asarray(self.order, jnp.int32)
        self.up = [(self.order[i], self.order[(i + 1) % size]) for i in range(size)]
        self.down = [(self.order[i], self.order[(i - 1) % size]) for i in range(size)]

    def member(self, offset):
        return self.table[lax.rem(self.here + (offset + self.size), self.size)]

    def gather(self, block):
        size, rows = self.size, block.shape[0]
        whole = jnp.zeros((size * rows,) + block.shape[1:], block.dtype)
        tail = (0,) * (block.ndim - 1)

        def put(whole, piece, owner, shift=0):
            return lax.dynamic_update_slice(whole, piece, (owner * rows + shift,) + tail)

        whole = put(whole, block, self.member(0))
        from_left = from_right = block
        for step in range(1, size // 2):
            from_left = lax.ppermute(from_left, "seq", self.up)
            from_right = lax.ppermute(from_right, "seq", self.down)
            whole = put(whole, from_left, self.member(-step))
            whole = put(whole, from_right, self.member(step))
        half = rows // 2
        far = self.member(size // 2)
        whole = put(whole, lax.ppermute(from_left[:half], "seq", self.up), far)
        return put(whole, lax.ppermute(from_right[half:], "seq", self.down), far, half)

    def scatter(self, whole):
        size = self.size
        rows = whole.shape[0] // size
        half = rows // 2

        def piece(offset):
            return lax.dynamic_slice_in_dim(whole, self.member(offset) * rows, rows, 0)

        far = piece(size // 2).astype(BF16)
        left_half = lax.ppermute(far[:half], "seq", self.up)
        right_half = lax.ppermute(far[half:], "seq", self.down)
        blank = jnp.zeros((rows - half,) + whole.shape[1:], BF16)
        from_left = jnp.concatenate([left_half, blank], axis=0)
        from_right = jnp.concatenate([blank, right_half], axis=0)
        for step in range(size // 2 - 1, 0, -1):
            send_up = (piece(step) + from_left.astype(F32)).astype(BF16)
            send_down = (piece(-step) + from_right.astype(F32)).astype(BF16)
            from_left = lax.ppermute(send_up, "seq", self.up)
            from_right = lax.ppermute(send_down, "seq", self.down)
        return piece(0) + from_left.astype(F32) + from_right.astype(F32)


class Fsdp:
    def __init__(self, size):
        self.size = size
        self.across = size // 2
        index = lax.axis_index("fsdp")
        self.x = index // 2
        self.core = index % 2
        self.swap = [(i, i ^ 1) for i in range(size)]

    def shift(self, step):
        return [(x * 2 + c, (x + step) % self.across * 2 + c) for x in range(self.across) for c in (0, 1)]

    def gather(self, block, dim):
        width = block.shape[dim]
        shape = list(block.shape)
        shape[dim] = width * self.size
        whole = jnp.zeros(shape, block.dtype)
        for step in range(self.across):
            mine = lax.ppermute(block, "fsdp", self.shift(step)) if step else block
            owner = lax.rem(self.x - step + self.across, self.across) * 2
            other = lax.ppermute(mine, "fsdp", self.swap)
            whole = lax.dynamic_update_slice_in_dim(whole, mine, (owner + self.core) * width, dim)
            whole = lax.dynamic_update_slice_in_dim(whole, other, (owner + 1 - self.core) * width, dim)
        return whole

    def scatter(self, whole, dim):
        width = whole.shape[dim] // self.size

        def piece(x, core):
            return lax.dynamic_slice_in_dim(whole, (x * 2 + core) * width, width, dim)

        total = None
        for step in range(self.across):
            x = lax.rem(self.x + step, self.across)
            other = lax.ppermute(piece(x, 1 - self.core), "fsdp", self.swap)
            both = piece(x, self.core).astype(F32) + other.astype(F32)
            if step:
                both = lax.ppermute(both.astype(BF16), "fsdp", self.shift(step)).astype(F32)
            total = both if total is None else total + both
        return total


def doubling_gather(block, counts):
    me = lax.axis_index(ALL)
    bit = 1
    while bit < counts:
        other = lax.ppermute(block, ALL, [(i, i ^ bit) for i in range(counts)])
        low = (me & bit) == 0
        block = jnp.concatenate(
            [jnp.where(low, block, other), jnp.where(low, other, block)], axis=0
        )
        bit *= 2
    return block


def halving_scatter(block, counts):
    me = lax.axis_index(ALL)
    bit = counts // 2
    while bit:
        half = block.shape[0] // 2
        low = (me & bit) == 0
        keep = jnp.where(low, block[:half], block[half:])
        send = jnp.where(low, block[half:], block[:half])
        block = keep + lax.ppermute(send, ALL, [(i, i ^ bit) for i in range(counts)])
        bit //= 2
    return block


def on_device(
    tokens,
    cotangent,
    expert_ids,
    attn_gain,
    w_query,
    w_key,
    w_value,
    query_gain,
    key_gain,
    w_output,
    mlp_gain,
    w_router,
    w_gate,
    w_up,
    w_down,
):
    groups = lax.axis_size("seq")
    splits = lax.axis_size("fsdp")
    counts = groups * splits
    ring, fsdp = Ring(groups), Fsdp(splits)
    seat = lax.axis_index("seq")
    tok_rows, model_width = tokens.shape
    own_rows = w_query.shape[0]
    head_size = query_gain.shape[0] * counts
    heads_all = w_query.shape[1] // head_size
    kv_heads = w_key.shape[1] // head_size
    head_local = heads_all // groups
    copies = groups // kv_heads
    query_width = head_local * head_size
    experts_all = w_router.shape[1]
    local_experts, _, ff = w_gate.shape
    seq_rows = tok_rows * groups
    scale_qk = 1.0 / math.sqrt(head_size)

    tokens_all = ring.gather(tokens)

    packed = jnp.concatenate(
        [query_gain, key_gain, mlp_gain, w_router.reshape(-1)], axis=0
    )[None, :]
    packed = doubling_gather(packed, counts)
    cuts = [query_gain.shape[0], key_gain.shape[0], own_rows, own_rows * experts_all]
    ends = [sum(cuts[: i + 1]) for i in range(4)]
    gain_q = packed[:, : ends[0]].reshape(-1).astype(F32)
    gain_k = packed[:, ends[0] : ends[1]].reshape(-1).astype(F32)
    gain_mlp = packed[:, ends[1] : ends[2]].reshape(-1).astype(F32)
    router_w = packed[:, ends[2] :].reshape(model_width, experts_all)
    ids_all = lax.all_gather(expert_ids, "seq", axis=0, tiled=True)

    gain_rows = attn_gain.astype(F32)[:, None, None]
    weights_own = jnp.concatenate(
        [
            w_query.reshape(own_rows, groups, query_width),
            jnp.repeat(w_key.reshape(own_rows, kv_heads, head_size), copies, axis=1),
            jnp.repeat(w_value.reshape(own_rows, kv_heads, head_size), copies, axis=1),
        ],
        axis=2,
    )
    scaled = (weights_own.astype(F32) * gain_rows).astype(BF16)
    qkv_width = query_width + 2 * head_size
    qkv_w = lax.all_to_all(
        scaled.transpose(1, 0, 2), "seq", split_axis=0, concat_axis=0, tiled=True
    ).reshape(groups * own_rows, qkv_width)
    qkv_w = fsdp.gather(qkv_w, 0)

    me = lax.axis_index(ALL)
    out_rows = w_output.shape[0]
    chunk = model_width // splits
    held = jnp.zeros((splits * out_rows, chunk), BF16)
    my_split = lax.axis_index("fsdp")
    for step in range(splits):
        perm = [(b, ((b % splits + step) % splits) * groups + b // splits) for b in range(counts)]
        target = lax.rem(me + step, splits)
        piece = lax.dynamic_slice_in_dim(w_output, target * chunk, chunk, 1)
        piece = lax.ppermute(piece, ALL, perm)
        origin = lax.rem(my_split - step + splits, splits)
        held = lax.dynamic_update_slice_in_dim(held, piece, origin * out_rows, 0)
    output_w = fsdp.gather(held, 1)

    gate_w = fsdp.gather(w_gate, 1)
    up_w = fsdp.gather(w_up, 1)
    down_w = fsdp.gather(w_down, 2)

    positions = jnp.arange(seq_rows, dtype=jnp.int32).astype(F32)
    cos_table, sine_table = rotary_tables(positions, head_size)
    normed_all = norm_parts(tokens_all.astype(F32))[0].astype(BF16)
    qkv = jnp.dot(normed_all, qkv_w, preferred_element_type=F32)
    query_pre = qkv[:, :query_width].reshape(seq_rows, head_local, head_size)
    key_pre = qkv[:, query_width : query_width + head_size].reshape(seq_rows, 1, head_size)
    value_seq = qkv[:, query_width + head_size :].astype(BF16)
    query_hat, query_scale = norm_parts(query_pre)
    key_hat, key_scale = norm_parts(key_pre)
    query_seq = rotate(query_hat * gain_q, cos_table, sine_table).astype(BF16)
    key_seq = rotate(key_hat * gain_k, cos_table, sine_table).astype(BF16)[:, 0]

    block_rows = min(512, seq_rows)
    block_count = seq_rows // block_rows
    blocks = []

    def block_scores(query_blk, first):
        limit = first + block_rows
        scores = (
            jnp.einsum("qhd,kd->hqk", query_blk, key_seq[:limit], preferred_element_type=F32)
            * scale_qk
        )
        rows = first + jnp.arange(block_rows, dtype=jnp.int32)
        causal = jnp.arange(limit, dtype=jnp.int32)[None, :] <= rows[:, None]
        return jnp.where(causal[None], scores, NEG_LARGE)

    attended, log_sums = [], []
    for block in range(block_count):
        first = block * block_rows
        scores = block_scores(query_seq[first : first + block_rows], first)
        row_peak = jnp.max(scores, axis=-1, keepdims=True)
        exponent = jnp.exp(scores - row_peak)
        row_total = jnp.sum(exponent, axis=-1, keepdims=True)
        weights_low = (exponent / row_total).astype(BF16)
        attended.append(
            jnp.einsum(
                "hqk,kd->qhd",
                weights_low,
                value_seq[: first + block_rows],
                preferred_element_type=F32,
            )
            .astype(BF16)
            .reshape(block_rows, query_width)
        )
        log_sums.append(row_peak + jnp.log(row_total))
    attended = jnp.concatenate(attended, axis=0)

    inputs = tokens.astype(F32)
    middle = inputs + ring.scatter(jnp.dot(attended, output_w, preferred_element_type=F32))
    normed_m, scale_m = norm_parts(middle)
    mixer_in = (normed_m * gain_mlp).astype(BF16)

    mixer_all = ring.gather(mixer_in)
    cot_all = ring.gather(after(cotangent, tokens_all))

    def shares(rows_in, ids):
        logits = jnp.dot(rows_in, router_w, preferred_element_type=F32)
        chosen = jnp.sum(
            (ids[:, :, None] == jnp.arange(experts_all, dtype=jnp.int32)).astype(F32), axis=1
        )
        masked = jnp.where(chosen > 0, logits, NEG_LARGE)
        grown = jnp.exp(masked - jnp.max(masked, axis=-1, keepdims=True)) * chosen
        return grown / jnp.sum(grown, axis=-1, keepdims=True)

    share_own = shares(mixer_in, expert_ids)
    share_all = shares(mixer_all, ids_all)
    share = lax.dynamic_slice_in_dim(share_all, seat * local_experts, local_experts, 1).T[
        :, :, None
    ]

    gate_pre = jnp.einsum("td,edf->etf", mixer_all, gate_w, preferred_element_type=F32)
    up_pre = jnp.einsum("td,edf->etf", mixer_all, up_w, preferred_element_type=F32)
    down_back = jnp.einsum("td,efd->etf", cot_all, down_w, preferred_element_type=F32)
    sigmoid = jax.nn.sigmoid(gate_pre)
    silu_gate = gate_pre * sigmoid
    active = silu_gate * up_pre
    grad_share = jnp.sum(active * down_back, axis=-1)
    active_shared = (active * share).astype(BF16)
    grad_active = down_back * share
    grad_up_pre = (grad_active * silu_gate).astype(BF16)
    grad_gate_pre = (
        grad_active * up_pre * sigmoid * (1.0 + gate_pre * (1.0 - sigmoid))
    ).astype(BF16)
    grad_entered = jnp.einsum(
        "etf,edf->td", grad_gate_pre, gate_w, preferred_element_type=F32
    ) + jnp.einsum("etf,edf->td", grad_up_pre, up_w, preferred_element_type=F32)

    grad_share_own = lax.all_to_all(
        grad_share.reshape(local_experts, groups, tok_rows).transpose(1, 0, 2),
        "seq",
        split_axis=0,
        concat_axis=0,
        tiled=True,
    )
    grad_share_own = grad_share_own.reshape(experts_all, tok_rows).T
    grad_logits = (
        share_own
        * (grad_share_own - jnp.sum(share_own * grad_share_own, axis=-1, keepdims=True))
    ).astype(BF16)

    grad_mixer = ring.scatter(grad_entered) + dot(grad_logits, router_w, 1, 1)
    grad_router = dot(mixer_in, grad_logits, 0, 0)
    grad_gain_m = jnp.sum(grad_mixer * normed_m, axis=0)
    grad_out = cotangent.astype(F32)
    grad_middle = grad_out + norm_back(grad_mixer * gain_mlp, normed_m, scale_m)
    grad_branch = grad_middle.astype(BF16)
    branch_all = ring.gather(grad_branch)

    produced = jnp.einsum("etf,efd->td", active_shared, down_w, preferred_element_type=F32)
    layer_out = (middle + ring.scatter(after(produced, branch_all))).astype(BF16)

    grad_gate = jnp.einsum("td,etf->edf", mixer_all, grad_gate_pre, preferred_element_type=F32)
    grad_up = jnp.einsum("td,etf->edf", mixer_all, grad_up_pre, preferred_element_type=F32)
    grad_down = jnp.einsum("etf,td->efd", active_shared, cot_all, preferred_element_type=F32)
    grad_gate = fsdp.scatter(grad_gate.astype(BF16), 1)
    grad_up = fsdp.scatter(grad_up.astype(BF16), 1)
    grad_down = fsdp.scatter(grad_down.astype(BF16), 2)

    grad_attended = (
        dot(branch_all, output_w, 1, 1).astype(BF16).reshape(seq_rows, head_local, head_size)
    )
    grad_output = dot(attended, branch_all, 0, 0).astype(BF16)
    grad_key_seq = jnp.zeros((seq_rows, head_size), F32)
    grad_value_seq = jnp.zeros((seq_rows, head_size), F32)
    grad_query_seq = []
    for block in range(block_count):
        first = block * block_rows
        limit = first + block_rows
        query_blk = query_seq[first:limit]
        grad_blk = grad_attended[first:limit]
        probs = jnp.exp(block_scores(query_blk, first) - log_sums[block])
        value_part = jnp.einsum(
            "hqk,qhd->kd", probs.astype(BF16), grad_blk, preferred_element_type=F32
        )
        grad_probs = jnp.einsum(
            "qhd,kd->hqk", grad_blk, value_seq[:limit], preferred_element_type=F32
        )
        grad_scores = (
            probs * (grad_probs - jnp.sum(probs * grad_probs, axis=-1, keepdims=True))
        ).astype(BF16)
        grad_query_seq.append(
            jnp.einsum("hqk,kd->qhd", grad_scores, key_seq[:limit], preferred_element_type=F32)
            * scale_qk
        )
        key_part = (
            jnp.einsum("hqk,qhd->kd", grad_scores, query_blk, preferred_element_type=F32)
            * scale_qk
        )
        spare = ((0, seq_rows - limit), (0, 0))
        grad_key_seq = grad_key_seq + jnp.pad(key_part, spare)
        grad_value_seq = grad_value_seq + jnp.pad(value_part, spare)
    grad_query_seq = jnp.concatenate(grad_query_seq, axis=0)

    grad_query_norm = unrotate(grad_query_seq, cos_table, sine_table)
    grad_key_norm = unrotate(grad_key_seq[:, None, :], cos_table, sine_table)
    grad_gain_q = jnp.sum(grad_query_norm * query_hat, axis=(0, 1))
    grad_gain_k = jnp.sum(grad_key_norm * key_hat, axis=(0, 1))
    grad_qkv = jnp.concatenate(
        [
            norm_back(grad_query_norm * gain_q, query_hat, query_scale)
            .astype(BF16)
            .reshape(seq_rows, query_width),
            norm_back(grad_key_norm * gain_k, key_hat, key_scale)
            .astype(BF16)
            .reshape(seq_rows, head_size),
            grad_value_seq.astype(BF16),
        ],
        axis=1,
    )
    grad_normed = ring.scatter(dot(grad_qkv, qkv_w, 1, 1))
    normed_a, scale_a = norm_parts(inputs)
    grad_tokens = (grad_middle + norm_back(grad_normed, normed_a, scale_a)).astype(BF16)

    grad_qkv_w = fsdp.scatter(dot(normed_all, grad_qkv, 0, 0).astype(BF16), 0)
    grad_qkv_w = lax.all_to_all(
        grad_qkv_w.astype(BF16).reshape(groups, own_rows, qkv_width),
        "seq",
        split_axis=0,
        concat_axis=0,
        tiled=True,
    ).astype(F32)
    grad_gain_a = jnp.sum(grad_qkv_w * weights_own.transpose(1, 0, 2).astype(F32), axis=(0, 2))
    grad_qkv_w = grad_qkv_w * attn_gain.astype(F32)[None, :, None]
    grad_query_w = (
        grad_qkv_w[:, :, :query_width].transpose(1, 0, 2).reshape(own_rows, heads_all * head_size)
    )

    def merged(part):
        summed = jnp.sum(part.reshape(kv_heads, copies, own_rows, head_size), axis=1)
        return summed.transpose(1, 0, 2).reshape(own_rows, kv_heads * head_size)

    grad_key_w = merged(grad_qkv_w[:, :, query_width : query_width + head_size])
    grad_value_w = merged(grad_qkv_w[:, :, query_width + head_size :])

    grad_output = fsdp.scatter(grad_output, 1).astype(BF16)
    grad_output_w = jnp.zeros((out_rows, model_width), F32)
    for step in range(splits):
        perm = [(((b % splits + step) % splits) * groups + b // splits, b) for b in range(counts)]
        origin = lax.rem(my_split - step + splits, splits)
        piece = lax.dynamic_slice_in_dim(grad_output, origin * out_rows, out_rows, 0)
        piece = lax.ppermute(piece, ALL, perm).astype(F32)
        target = lax.rem(me + step, splits)
        grad_output_w = lax.dynamic_update_slice_in_dim(grad_output_w, piece, target * chunk, 1)

    small = jnp.concatenate(
        [grad_gain_m[:, None], grad_router], axis=1
    ).reshape(counts, own_rows, 1 + experts_all)
    small = halving_scatter(small, counts)[0]
    gains = jnp.concatenate(
        [grad_gain_q.reshape(counts, -1), grad_gain_k.reshape(counts, -1)], axis=1
    )
    gains = halving_scatter(gains, counts)[0]
    cut = query_gain.shape[0]
    return (
        layer_out,
        grad_tokens,
        grad_gain_a,
        grad_query_w,
        grad_key_w,
        grad_value_w,
        gains[:cut],
        gains[cut:],
        grad_output_w,
        small[:, 0],
        small[:, 1:],
        grad_gate,
        grad_up,
        grad_down,
    )


def solution(mesh):
    rows = P(("fsdp", "seq"), None)
    line = P(("fsdp", "seq"))
    wide = P("seq", "fsdp", None)
    deep = P("seq", None, "fsdp")
    in_specs = (
        rows, rows, rows, line, rows, rows, rows, line, line, rows, line, rows, wide, wide, deep,
    )
    out_specs = (
        rows, rows, line, rows, rows, rows, line, line, rows, line, rows, wide, wide, deep,
    )
    return jax.shard_map(
        on_device, mesh=mesh, in_specs=in_specs, out_specs=out_specs, check_vma=False
    )
```

```python
import math

import jax
import jax.numpy as jnp
import numpy as np
from jax import lax
from jax.experimental import pallas as pl
from jax.experimental.pallas import tpu as pltpu
from jax.sharding import PartitionSpec as P

NORM_EPS = 1e-06
ROPE_BASE = 1000000.0
NEG_LARGE = -1e30
F32 = jnp.float32
BF16 = jnp.bfloat16
ALL = ("fsdp", "seq")
VMEM_LIMIT = 40 * 1024 * 1024
LARGE_LIMIT = 56 * 1024 * 1024
SMALL_LIMIT = 16 * 1024 * 1024


def dot(left, right, left_dim, right_dim):
    return lax.dot_general(
        left, right, (((left_dim,), (right_dim,)), ((), ())), preferred_element_type=F32
    )


def norm_parts(values):
    row_scale = lax.rsqrt(jnp.mean(values * values, axis=-1, keepdims=True) + NORM_EPS)
    return (values * row_scale, row_scale)


def norm_back(grad_normed, normed, row_scale):
    return row_scale * (
        grad_normed - normed * jnp.mean(grad_normed * normed, axis=-1, keepdims=True)
    )


def rotary_tables(positions, head_size):
    half_size = head_size // 2
    frequency = jnp.exp(
        jnp.arange(half_size, dtype=F32) * (-2.0 * math.log(ROPE_BASE) / head_size)
    )
    angles = positions[:, None] * frequency[None, :]
    cosine, sine = jnp.cos(angles), jnp.sin(angles)
    return jnp.concatenate([cosine, cosine], axis=1), jnp.concatenate([-sine, sine], axis=1)


def swap_halves(values):
    return pltpu.roll(values, values.shape[-1] // 2, 1)


def params(limit=VMEM_LIMIT):
    return pltpu.CompilerParams(vmem_limit_bytes=limit)


def take_piece(step, pieces, halved, store):
    last = len(pieces) - (2 if halved else 0)
    for i in range(last):

        @pl.when(step == i)
        def _(i=i):
            store(0, pieces[i][...])

    if halved:

        @pl.when(step == last)
        def _():
            half = pieces[last].shape[0]
            store(0, pieces[last][...])
            store(half, pieces[last + 1][...])


def lay_kernel(count, halved, order_ref, *refs):
    def store(first, rows):
        refs[-1][first : first + rows.shape[0]] = rows

    take_piece(pl.program_id(0), refs[:count], halved, store)


def lay(pieces, order=None):
    halved = order is None
    members = len(pieces) - (1 if halved else 0)
    if halved:
        order = jnp.arange(members, dtype=jnp.int32)
    rows, cols = pieces[0].shape
    return pl.pallas_call(
        lambda *refs: lay_kernel(len(pieces), halved, *refs),
        grid_spec=pltpu.PrefetchScalarGridSpec(
            num_scalar_prefetch=1,
            grid=(members,),
            in_specs=[pl.BlockSpec(piece.shape, lambda i, order: (0, 0)) for piece in pieces],
            out_specs=pl.BlockSpec((rows, cols), lambda i, order: (order[i], 0)),
        ),
        out_shape=jax.ShapeDtypeStruct((members * rows, cols), pieces[0].dtype),
        compiler_params=params(),
        cost_estimate=pl.CostEstimate(
            flops=0, bytes_accessed=4 * members * rows * cols, transcendentals=0
        ),
    )(order, *pieces)


def project_kernel(heads, parts, count, order_ref, *refs):
    pieces, refs = refs[:count], refs[count:]
    weights, refs = refs[:parts], refs[parts:]
    cos_ref, sin_ref, gain_ref, n_ref, pre_ref, q_ref, k_ref, v_ref = refs
    size = cos_ref.shape[1]

    def store(first, rows):
        n_ref[first : first + rows.shape[0]] = norm_parts(rows.astype(F32))[0].astype(BF16)

    take_piece(pl.program_id(0), pieces, True, store)
    depth = weights[0].shape[0]
    projected = 0.0
    for part, w_ref in enumerate(weights):
        columns = pl.ds(pl.multiple_of(order_ref[part] * depth, depth), depth)
        projected += jnp.dot(n_ref[:, columns], w_ref[...], preferred_element_type=F32)
    pre_ref[...] = projected[:, : (heads + 1) * size]
    for head in range(heads + 1):
        row = 0 if head < heads else 1
        scaled = norm_parts(projected[:, head * size : (head + 1) * size])[0] * gain_ref[row : row + 1]
        turned = (scaled * cos_ref[...] + swap_halves(scaled) * sin_ref[...]).astype(BF16)
        if head < heads:
            q_ref[:, head * size : (head + 1) * size] = turned
        else:
            k_ref[...] = turned
    v_ref[...] = projected[:, (heads + 1) * size :].astype(BF16)


def project(pieces, weights, order, width, cos_table, sine_table, gains):
    block, depth = pieces[0].shape
    rows = block * (len(pieces) - 1)
    size = cos_table.shape[1]
    heads = width // size - 2
    spec = lambda cols: pl.BlockSpec((block, cols), lambda i, order: (i, 0))
    whole = lambda shape: pl.BlockSpec(shape, lambda i, order: (0, 0))
    return pl.pallas_call(
        lambda *refs: project_kernel(heads, len(weights), len(pieces), *refs),
        grid_spec=pltpu.PrefetchScalarGridSpec(
            num_scalar_prefetch=1,
            grid=(rows // block,),
            in_specs=[whole(piece.shape) for piece in pieces]
            + [whole((part.shape[0], width)) for part in weights]
            + [spec(size), spec(size), whole(gains.shape)],
            out_specs=[
                spec(depth), spec((heads + 1) * size), spec(heads * size), spec(size), spec(size),
            ],
        ),
        out_shape=[
            jax.ShapeDtypeStruct((rows, depth), BF16),
            jax.ShapeDtypeStruct((rows, (heads + 1) * size), F32),
            jax.ShapeDtypeStruct((rows, heads * size), BF16),
            jax.ShapeDtypeStruct((rows, size), BF16),
            jax.ShapeDtypeStruct((rows, size), BF16),
        ],
        compiler_params=params(LARGE_LIMIT),
        cost_estimate=pl.CostEstimate(
            flops=2 * rows * depth * width, bytes_accessed=16 << 20, transcendentals=0
        ),
    )(order, *pieces, *weights, cos_table, sine_table, gains)


def fetch(arrays, spots, buffers, sems):
    rows = buffers[0].shape[0]
    copies = [
        pltpu.make_async_copy(array.at[pl.ds(spot * rows, rows)], buffer, sems.at[i])
        for i, (array, spot, buffer) in enumerate(zip(arrays, spots, buffers))
    ]
    for copy in copies:
        copy.start()
    for copy in copies:
        copy.wait()


def ring_add_kernel(spots, up_hbm, down_hbm, left_ref, right_ref, up_ref, down_ref, up_buf, down_buf, sems):
    fetch((up_hbm, down_hbm), spots, (up_buf, down_buf), sems)
    rows, half = up_buf.shape[0], left_ref.shape[0]
    if half == rows:
        up_ref[...] = (up_buf[...].astype(F32) + left_ref[...].astype(F32)).astype(BF16)
        down_ref[...] = (down_buf[...].astype(F32) + right_ref[...].astype(F32)).astype(BF16)
        return
    up_ref[:half] = (up_buf[:half].astype(F32) + left_ref[...].astype(F32)).astype(BF16)
    up_ref[half:] = up_buf[half:]
    down_ref[:half] = down_buf[:half]
    down_ref[half:] = (down_buf[half:].astype(F32) + right_ref[...].astype(F32)).astype(BF16)


HBM = pl.BlockSpec(memory_space=pltpu.HBM)
VMEM = pl.BlockSpec(memory_space=pltpu.VMEM)


def ring_add(mine_up, mine_down, left, right, rows):
    width = left.shape[1]
    return pl.pallas_call(
        lambda *refs: ring_add_kernel((mine_up[1], mine_down[1]), *refs),
        in_specs=[HBM, HBM, VMEM, VMEM],
        out_specs=[VMEM, VMEM],
        out_shape=[jax.ShapeDtypeStruct((rows, width), BF16)] * 2,
        scratch_shapes=[pltpu.VMEM((rows, width), BF16)] * 2 + [pltpu.SemaphoreType.DMA((2,))],
        compiler_params=pltpu.CompilerParams(vmem_limit_bytes=SMALL_LIMIT),
        cost_estimate=pl.CostEstimate(
            flops=2 * rows * width, bytes_accessed=12 * rows * width, transcendentals=0
        ),
    )(mine_up[0], mine_down[0], left, right)


def summed(mine_ref, left_ref, right_ref):
    return mine_ref[...].astype(F32) + left_ref[...].astype(F32) + right_ref[...].astype(F32)


def enter_kernel(mine_ref, left_ref, right_ref, x_ref, gain_ref, middle_ref, mixer_ref):
    middle = x_ref[...].astype(F32) + summed(mine_ref, left_ref, right_ref)
    middle_ref[...] = middle
    mixer_ref[...] = (norm_parts(middle)[0] * gain_ref[...]).astype(BF16)


def mixer_back_kernel(
    mine_ref, left_ref, right_ref, logits_ref, router_ref, middle_ref, cot_ref, gain_ref, *refs
):
    grad_ref, branch_ref, gains_ref = refs
    grad_mixer = summed(mine_ref, left_ref, right_ref) + dot(logits_ref[...], router_ref[...], 1, 1)
    normed, row_scale = norm_parts(middle_ref[...])
    gains_ref[...] = jnp.sum(grad_mixer * normed, axis=0, keepdims=True)
    grad = cot_ref[...].astype(F32) + norm_back(grad_mixer * gain_ref[...], normed, row_scale)
    grad_ref[...] = grad
    branch_ref[...] = grad.astype(BF16)


def tokens_back_kernel(mine_ref, left_ref, right_ref, x_ref, grad_ref, out_ref):
    normed, row_scale = norm_parts(x_ref[...].astype(F32))
    grad = norm_back(summed(mine_ref, left_ref, right_ref), normed, row_scale)
    out_ref[...] = (grad_ref[...] + grad).astype(BF16)


def by_rows(kernel, landed, inputs, outs, sums=()):
    (mine, spot), left, right = landed
    rows, width = left.shape

    def whole(mine_hbm, *refs):
        refs, mine_ref, sems = refs[:-2], refs[-2], refs[-1]
        fetch((mine_hbm,), (spot,), (mine_ref,), sems)
        kernel(mine_ref, *refs)

    return pl.pallas_call(
        whole,
        in_specs=[HBM] + [VMEM] * (2 + len(inputs)),
        out_specs=[VMEM] * (len(outs) + len(sums)),
        out_shape=[jax.ShapeDtypeStruct((rows, width), kind) for kind in outs]
        + [jax.ShapeDtypeStruct(shape, F32) for shape in sums],
        scratch_shapes=[pltpu.VMEM((rows, width), BF16), pltpu.SemaphoreType.DMA((1,))],
        compiler_params=pltpu.CompilerParams(vmem_limit_bytes=SMALL_LIMIT),
        cost_estimate=pl.CostEstimate(
            flops=20 * rows * width, bytes_accessed=16 * rows * width, transcendentals=rows
        ),
    )(mine, left, right, *inputs)


def weights_back_kernel(held, copies, size, came_ref, own_ref, gain_ref, q_ref, k_ref, v_ref, gains_ref, small_ref):
    groups, rows, _ = came_ref.shape
    width = own_ref.shape[2]
    wide = width - 2 * size
    gains = jnp.zeros((rows, 1), F32)
    small = jnp.zeros(small_ref.shape, F32)
    gain = gain_ref[...]
    seen = set()
    for member, group in enumerate(held):
        came = came_ref[member].astype(F32)
        gains += jnp.sum(
            came[:, :width] * own_ref[member].astype(F32), axis=1, keepdims=True
        )
        small += came[:, width:]
        came = came[:, :width] * gain
        q_ref[:, group * wide : (group + 1) * wide] = came[:, :wide]
        lanes = slice(group // copies * size, (group // copies + 1) * size)
        if group // copies not in seen:
            k_ref[:, lanes] = came[:, wide : wide + size]
            v_ref[:, lanes] = came[:, wide + size :]
        else:
            k_ref[:, lanes] += came[:, wide : wide + size]
            v_ref[:, lanes] += came[:, wide + size :]
        seen.add(group // copies)
    gains_ref[...] = jnp.broadcast_to(gains, gains_ref.shape)
    small_ref[...] = small


def weights_back(came, own, gain, held, kv_heads, size):
    groups, rows, total = came.shape
    width = own.shape[2]
    shape = lambda cols: jax.ShapeDtypeStruct((rows, cols), F32)
    return pl.pallas_call(
        lambda *refs: weights_back_kernel(held, groups // kv_heads, size, *refs),
        out_shape=[
            shape(groups * (width - 2 * size)),
            shape(kv_heads * size),
            shape(kv_heads * size),
            shape(128),
            shape(total - width),
        ],
        compiler_params=params(),
        cost_estimate=pl.CostEstimate(
            flops=4 * groups * rows * width, bytes_accessed=4 << 20, transcendentals=0
        ),
    )(came, own, gain)


def output_back_kernel(count, order_ref, left_ref, *refs):
    pieces, outs, (rows_ref, sum_ref) = refs[:count], refs[count:-2], refs[-2:]
    step = pl.program_id(0)

    def store(first, rows):
        rows_ref[first : first + rows.shape[0]] = rows

    take_piece(step, pieces, True, store)

    @pl.when(step == 0)
    def _():
        sum_ref[...] = jnp.zeros_like(sum_ref)

    sum_ref[...] += dot(left_ref[...], rows_ref[...], 0, 0)

    @pl.when(step == pl.num_programs(0) - 1)
    def _():
        for i, out_ref in enumerate(outs):
            rows = out_ref.shape[0]
            first = pl.multiple_of(order_ref[i] * rows, rows)
            out_ref[...] = sum_ref[pl.ds(first, rows), :].astype(BF16)


def output_back(left, pieces, order):
    rows, width = left.shape
    block, cols = pieces[0].shape
    parts = order.shape[0]
    whole = lambda shape: pl.BlockSpec(shape, lambda i, order: (0, 0))
    return pl.pallas_call(
        lambda *refs: output_back_kernel(len(pieces), *refs),
        grid_spec=pltpu.PrefetchScalarGridSpec(
            num_scalar_prefetch=1,
            grid=(rows // block,),
            in_specs=[pl.BlockSpec((block, width), lambda i, order: (i, 0))]
            + [whole(piece.shape) for piece in pieces],
            out_specs=[whole((width // parts, cols))] * parts,
            scratch_shapes=[pltpu.VMEM((block, cols), BF16), pltpu.VMEM((width, cols), F32)],
        ),
        out_shape=[jax.ShapeDtypeStruct((width // parts, cols), BF16)] * parts,
        compiler_params=params(),
        cost_estimate=pl.CostEstimate(
            flops=2 * rows * width * cols, bytes_accessed=8 << 20, transcendentals=0
        ),
    )(order, left, *pieces)


def project_back_kernel(own_rows, order_ref, normed_ref, grad_ref, small_ref, gains_ref, *outs):
    width = grad_ref.shape[1]
    part = dot(normed_ref[...], grad_ref[...], 0, 0).astype(BF16)
    small = small_ref[...]
    size = small.shape[1]
    row = lax.broadcasted_iota(jnp.int32, small.shape, 0) % own_rows
    upper = lax.broadcasted_iota(jnp.int32, small.shape, 1) >= size // 2
    for i in range(2):
        gain = gains_ref[i : i + 1]
        for half, line in enumerate((pltpu.roll(gain, size // 2, 1), gain)):
            small = jnp.where(upper & (row == 2 * i + half), line, small)
    small = small.astype(BF16)
    for i, out_ref in enumerate(outs):

        @pl.when(pl.program_id(0) == i)
        def _(out_ref=out_ref):
            out_ref[:, :width] = part
            out_ref[:, width:] = small


def project_back(normed, grad, small, gains, own_rows, order):
    rows, depth = normed.shape
    width, extra = grad.shape[1], small.shape[1]
    parts = order.shape[0]
    block = depth // parts
    whole = lambda shape: pl.BlockSpec(shape, lambda i, order: (0, 0))
    return pl.pallas_call(
        lambda *refs: project_back_kernel(own_rows, *refs),
        grid_spec=pltpu.PrefetchScalarGridSpec(
            num_scalar_prefetch=1,
            grid=(parts,),
            in_specs=[
                pl.BlockSpec((rows, block), lambda i, order: (0, order[i])),
                whole(grad.shape),
                pl.BlockSpec((block, extra), lambda i, order: (order[i], 0)),
                whole(gains.shape),
            ],
            out_specs=[whole((block, width + extra))] * parts,
        ),
        out_shape=[jax.ShapeDtypeStruct((block, width + extra), BF16)] * parts,
        compiler_params=params(),
        cost_estimate=pl.CostEstimate(
            flops=2 * rows * depth * width, bytes_accessed=12 << 20, transcendentals=0
        ),
    )(order, normed, grad, small, gains)


def row_grads_kernel(first_ref, second_ref, first_grad_ref, second_grad_ref, out_ref):
    part = dot(first_ref[...], first_grad_ref[0], 0, 0)
    out_ref[0] = (part + dot(second_ref[...], second_grad_ref[0], 0, 0)).astype(BF16)


def row_grads(rows, grads):
    experts, _, ff = grads[0].shape
    depth = rows[0].shape[1]
    block = depth // 4
    return pl.pallas_call(
        row_grads_kernel,
        grid=(experts, 4),
        in_specs=[pl.BlockSpec((part.shape[0], block), lambda e, i: (0, i)) for part in rows]
        + [pl.BlockSpec((1,) + part.shape[1:], lambda e, i: (e, 0, 0)) for part in grads],
        out_specs=pl.BlockSpec((1, block, ff), lambda e, i: (e, i, 0)),
        out_shape=jax.ShapeDtypeStruct((experts, depth, ff), BF16),
        compiler_params=params(),
        cost_estimate=pl.CostEstimate(
            flops=2 * experts * sum(part.shape[0] for part in rows) * ff * depth,
            bytes_accessed=16 << 20,
            transcendentals=0,
        ),
    )(*rows, *grads)


def down_grads_kernel(order_ref, first_ref, second_ref, cot_ref, *outs):
    cut = first_ref.shape[1]
    part = dot(first_ref[0], cot_ref[:cut], 0, 0) + dot(second_ref[0], cot_ref[cut:], 0, 0)
    for i, out_ref in enumerate(outs):

        @pl.when(pl.program_id(0) == i)
        def _(out_ref=out_ref):
            out_ref[pl.program_id(1)] = part.astype(BF16)


def down_grads(active, cot, order):
    experts, _, ff = active[0].shape
    rows, depth = cot.shape
    parts = order.shape[0]
    block = depth // parts
    return pl.pallas_call(
        down_grads_kernel,
        grid_spec=pltpu.PrefetchScalarGridSpec(
            num_scalar_prefetch=1,
            grid=(parts, experts),
            in_specs=[
                pl.BlockSpec((1,) + part.shape[1:], lambda i, e, order: (e, 0, 0))
                for part in active
            ]
            + [pl.BlockSpec((rows, block), lambda i, e, order: (0, order[i]))],
            out_specs=[pl.BlockSpec((experts, ff, block), lambda i, e, order: (0, 0, 0))] * parts,
        ),
        out_shape=[jax.ShapeDtypeStruct((experts, ff, block), BF16)] * parts,
        compiler_params=params(),
        cost_estimate=pl.CostEstimate(
            flops=2 * experts * rows * ff * depth, bytes_accessed=16 << 20, transcendentals=0
        ),
    )(order, *active, cot)


def stack_heads(array, size):
    return jnp.concatenate(
        [array[:, i * size : (i + 1) * size] for i in range(array.shape[1] // size)], axis=0
    )


def attend_kernel(scale, q_ref, k_ref, v_ref, at_q_ref, at_k_ref, out_ref, p_ref):
    rows, size = q_ref.shape[0], k_ref.shape[1]
    heads = q_ref.shape[1] // size
    scores = dot(k_ref[...], stack_heads(q_ref[...], size), 1, 1) * scale
    at_q = jnp.concatenate([at_q_ref[...]] * heads, axis=1)
    scores = jnp.where(at_k_ref[...] <= at_q, scores, NEG_LARGE)
    grown = jnp.exp(scores - jnp.max(scores, axis=0, keepdims=True))
    probs = (grown * (1.0 / jnp.sum(grown, axis=0, keepdims=True))).astype(BF16)
    p_ref[...] = probs
    output = dot(v_ref[...].T, probs, 1, 0).T.astype(BF16)
    for head in range(heads):
        out_ref[:, head * size : (head + 1) * size] = output[head * rows : (head + 1) * rows]


def attend(query, key, value, places, scale, block):
    rows, width = query.shape
    size = key.shape[1]
    heads = width // size
    whole = lambda shape: pl.BlockSpec(shape, lambda i: (0, 0))
    return pl.pallas_call(
        lambda *refs: attend_kernel(scale, *refs),
        grid=(rows // block,),
        in_specs=[
            pl.BlockSpec((block, width), lambda i: (i, 0)),
            whole((rows, size)),
            whole((rows, size)),
            pl.BlockSpec((1, block), lambda i: (0, i)),
            whole((rows, 1)),
        ],
        out_specs=[
            pl.BlockSpec((block, width), lambda i: (i, 0)),
            pl.BlockSpec((rows, heads * block), lambda i: (0, i)),
        ],
        out_shape=[
            jax.ShapeDtypeStruct((rows, width), BF16),
            jax.ShapeDtypeStruct((rows, heads * rows), BF16),
        ],
        compiler_params=params(LARGE_LIMIT),
        cost_estimate=pl.CostEstimate(
            flops=4 * heads * rows * rows * size,
            bytes_accessed=12 << 20,
            transcendentals=heads * rows * rows,
        ),
    )(query, key, value, places[None, :], places[:, None])


def head_back(grad_turned, pre, gain, cosine, sine):
    grad = grad_turned * cosine - swap_halves(grad_turned) * sine
    normed, row_scale = norm_parts(pre)
    return (
        jnp.sum(grad * normed, axis=0, keepdims=True),
        norm_back(grad * gain, normed, row_scale).astype(BF16),
    )


def attend_back_kernel(scale, count, first, last, offset, *refs):
    pieces, refs = refs[:count], refs[count:]
    w_ref, p_ref, q_ref, k_ref, v_ref, pre_ref, cos_ref, sin_ref, gain_ref = refs[:9]
    refs = refs[9:]
    before, refs = (() if first else refs[:4]), (refs if first else refs[4:])
    out_ref, gains_ref, dk_ref, dv_ref, rows_ref = refs
    step = pl.program_id(0)
    rows, size = q_ref.shape[0], k_ref.shape[1]
    heads = q_ref.shape[1] // size

    def store(first, rows):
        rows_ref[first : first + rows.shape[0]] = rows

    take_piece(step, pieces, last, store)

    @pl.when(step == 0)
    def _():
        if first:
            dk_ref[...] = jnp.zeros_like(dk_ref)
            dv_ref[...] = jnp.zeros_like(dv_ref)
            gains_ref[...] = jnp.zeros_like(gains_ref)
        else:
            for now_ref, before_ref in zip((out_ref, gains_ref, dk_ref, dv_ref), before):
                now_ref[...] = before_ref[...]

    probs = p_ref[...]
    grads = stack_heads(dot(rows_ref[...], w_ref[...], 1, 1).astype(BF16), size)
    dv_ref[...] += dot(probs, grads, 1, 0)
    grad_probs = dot(v_ref[...], grads, 1, 1)
    probs = probs.astype(F32)
    grad_scores = (
        probs * (grad_probs - jnp.sum(probs * grad_probs, axis=0, keepdims=True))
    ).astype(BF16)
    dk_ref[...] += dot(grad_scores, stack_heads(q_ref[...], size), 1, 0)
    grad_query = dot(k_ref[...].T, grad_scores, 1, 0).T * scale
    start = pl.multiple_of((step + offset) * rows, rows)
    here = pl.ds(start, rows)
    cosine, sine = cos_ref[here, :], sin_ref[here, :]
    for head in range(heads):
        lanes = slice(head * size, (head + 1) * size)
        gain_part, part = head_back(
            grad_query[head * rows : (head + 1) * rows],
            pre_ref[here, lanes],
            gain_ref[0:1],
            cosine,
            sine,
        )
        gains_ref[0:1] += gain_part
        out_ref[here, lanes] = part

    if last:

        @pl.when(step == pl.num_programs(0) - 1)
        def _():
            gain_part, part = head_back(
                dk_ref[...] * scale,
                pre_ref[:, heads * size : (heads + 1) * size],
                gain_ref[1:2],
                cos_ref[...],
                sin_ref[...],
            )
            gains_ref[1:2] = gain_part
            out_ref[:, heads * size : (heads + 1) * size] = part
            out_ref[:, (heads + 1) * size :] = dv_ref[...].astype(BF16)


def attend_back(pieces, offset, before, weights, probs, query, key, value, pre, cos_table, sine_table, gains, scale):
    rows, width = query.shape
    size = key.shape[1]
    heads = width // size
    block, depth = pieces[0].shape
    first, last = before is None, before is not None
    steps = len(pieces) - (1 if last else 0)
    whole = lambda shape: pl.BlockSpec(shape, lambda i: (0, 0))
    shapes = [
        jax.ShapeDtypeStruct((rows, (heads + 2) * size), BF16),
        jax.ShapeDtypeStruct((8, size), F32),
        jax.ShapeDtypeStruct((rows, size), F32),
        jax.ShapeDtypeStruct((rows, size), F32),
    ]
    outs = [whole(shape.shape) for shape in shapes]
    return pl.pallas_call(
        lambda *refs: attend_back_kernel(scale, len(pieces), first, last, offset, *refs),
        grid=(steps,),
        in_specs=[whole(piece.shape) for piece in pieces]
        + [
            whole(weights.shape),
            pl.BlockSpec((rows, heads * block), lambda i: (0, i + offset)),
            pl.BlockSpec((block, width), lambda i: (i + offset, 0)),
            whole((rows, size)),
            whole((rows, size)),
            whole((rows, (heads + 1) * size)),
            whole((rows, size)),
            whole((rows, size)),
            whole(gains.shape),
        ]
        + ([] if first else outs),
        out_specs=outs,
        out_shape=shapes,
        scratch_shapes=[pltpu.VMEM((block, depth), BF16)],
        compiler_params=params(),
        cost_estimate=pl.CostEstimate(
            flops=(8 * heads * rows * size + 2 * depth * width) * steps * block,
            bytes_accessed=(3 << 20) * steps,
            transcendentals=0,
        ),
    )(*pieces, weights, probs, query, key, value, pre, cos_table, sine_table, gains, *(before or ()))


def after(value, *others):
    return lax.optimization_barrier((value, *others))[0]


def ring_order(size):
    if size % 4 or size < 8:
        return list(range(size))
    wide = size // 4
    walk = [(0, y) for y in range(wide)]
    for z in range(1, 4):
        walk += [(z, y) for y in (range(wide - 1, 0, -1) if z % 2 else range(1, wide))]
    walk += [(z, 0) for z in (3, 2, 1)]
    return [z * wide + y for z, y in walk]


def together(*values):
    return lax.optimization_barrier(values)


class Ring:
    def __init__(self, size):
        self.size = size
        self.steps = size // 2
        order = ring_order(size)
        self.up = [(order[i], order[(i + 1) % size]) for i in range(size)]
        self.down = [(order[i], order[(i - 1) % size]) for i in range(size)]
        self.offsets = [0]
        for step in range(1, self.steps):
            self.offsets += [-step, step]
        self.offsets += [self.steps]
        near = np.zeros((size, size), np.int32)
        for i, member in enumerate(order):
            near[member] = [order[(i + offset) % size] for offset in self.offsets]
        seat = lax.axis_index("seq")
        self.members = jnp.asarray(near)[seat]
        self.spots = jnp.asarray(np.argsort(near, axis=1).astype(np.int32))[seat]

    def swap(self, up, down):
        return lax.ppermute(up, "seq", self.up), lax.ppermute(down, "seq", self.down)

    def spot(self, offset):
        return self.offsets.index(offset)


class Gather:
    def __init__(self, ring, block):
        self.ring, self.step, self.pieces = ring, 0, [block]
        self.left = self.right = block
        self.ready = None

    def sends(self):
        if self.step + 1 < self.ring.steps:
            return self.left, self.right
        half = self.left.shape[0] // 2
        return self.left[:half], self.right[half:]

    def start(self):
        ready = self.ready or self.sends()
        self.step += 1
        self.ready = None
        return self.ring.swap(*ready)

    def end(self, left, right):
        self.left, self.right = left, right
        self.pieces += [left, right]


class Scatter:
    def __init__(self, ring, piece, rows):
        self.ring, self.step, self.piece, self.rows = ring, 0, piece, rows
        self.left = self.right = self.ready = None

    def sends(self):
        ring, rows = self.ring, self.rows
        if self.step == 0:
            whole, spot = self.piece(ring.spot(ring.steps))
            start, middle, end = spot * rows, spot * rows + rows // 2, (spot + 1) * rows
            return (
                lax.slice_in_dim(whole, start, middle, axis=0),
                lax.slice_in_dim(whole, middle, end, axis=0),
            )
        place = ring.steps - self.step
        mine_up, mine_down = self.piece(ring.spot(place)), self.piece(ring.spot(-place))
        return ring_add(mine_up, mine_down, self.left, self.right, rows)

    def start(self):
        ready = self.ready or self.sends()
        self.step += 1
        self.ready = None
        return self.ring.swap(*ready)

    def end(self, left, right):
        self.left, self.right = left, right

    def landed(self):
        return self.piece(0), self.left, self.right


def prepare(rings, *values):
    ready, values = together([ring.sends() for ring in rings], values)
    for ring, sends in zip(rings, ready):
        ring.ready = tuple(sends)
    return values


def window(rings, *values):
    moved = [ring.start() for ring in rings]
    moved, values = together(moved, values)
    for ring, (left, right) in zip(rings, moved):
        ring.end(left, right)
    return values


class Fsdp:
    def __init__(self, size):
        self.size = size
        self.across = size // 2

        def blocks(way):
            return np.asarray(
                [
                    [
                        (i // 2 + way * step) % self.across * 2 + (i % 2 ^ flip)
                        for step in range(self.across)
                        for flip in (0, 1)
                    ]
                    for i in range(size)
                ],
                np.int32,
            )

        index = lax.axis_index("fsdp")
        self.blocks = jnp.asarray(blocks(-1))[index]
        self.targets = jnp.asarray(blocks(1))[index]
        self.spots = jnp.asarray(np.argsort(blocks(-1), axis=1).astype(np.int32))[index]

    def swap(self, array):
        return lax.ppermute(array, "fsdp", [(i, i ^ 1) for i in range(self.size)])

    def shift(self, array, step):
        perm = [
            (x * 2 + c, (x + step) % self.across * 2 + c)
            for x in range(self.across)
            for c in (0, 1)
        ]
        return lax.ppermute(array, "fsdp", perm)

    def spread(self, block):
        return [self.shift(block, step) for step in range(1, self.across)]

    def swapped(self, block, others):
        return [part for mine in [block] + others for part in (mine, self.swap(mine))]

    def pair(self, parts):
        return [
            (parts[i].astype(F32) + self.swap(parts[i + 1]).astype(F32)).astype(BF16)
            for i in range(0, self.size, 2)
        ]

    def send(self, paired):
        return [self.shift(part, step) for step, part in enumerate(paired) if step]


def on_device(
    tokens,
    cotangent,
    expert_ids,
    attn_gain,
    w_query,
    w_key,
    w_value,
    query_gain,
    key_gain,
    w_output,
    mlp_gain,
    w_router,
    w_gate,
    w_up,
    w_down,
):
    groups = lax.axis_size("seq")
    splits = lax.axis_size("fsdp")
    counts = groups * splits
    ring, fsdp = Ring(groups), Fsdp(splits)
    seat = lax.axis_index("seq")
    me = lax.axis_index(ALL)
    tok_rows, model_width = tokens.shape
    top_k = expert_ids.shape[1]
    own_rows = w_query.shape[0]
    head_size = query_gain.shape[0] * counts
    heads_all = w_query.shape[1] // head_size
    kv_heads = w_key.shape[1] // head_size
    head_local = heads_all // groups
    copies = groups // kv_heads
    query_width = head_local * head_size
    qkv_width = query_width + 2 * head_size
    experts_all = w_router.shape[1]
    local_experts, _, ff = w_gate.shape
    seq_rows = tok_rows * groups
    scale_qk = 1.0 / math.sqrt(head_size)

    held_groups = [seat % splits * (groups // splits) + seat // splits for seat in range(groups)]
    exchange = [
        (j * groups + part * splits + i, i * groups + part * splits + j)
        for j in range(splits)
        for part in range(groups // splits)
        for i in range(splits)
    ]

    def by_member(weights, group_of):
        width = weights.shape[1] // (max(group_of) + 1)
        return [weights[:, group * width : (group + 1) * width] for group in group_of]

    kv_of = [group // copies for group in held_groups]
    weights_own = jnp.stack(
        [
            jnp.concatenate(parts, axis=1)
            for parts in zip(
                by_member(w_query, held_groups), by_member(w_key, kv_of), by_member(w_value, kv_of)
            )
        ]
    )
    scaled = (weights_own.astype(F32) * attn_gain.astype(F32)[None, :, None]).astype(BF16)

    def placed(gain):
        return lax.dynamic_update_slice(
            jnp.zeros((head_size,), BF16), gain, (me * gain.shape[0],)
        )

    others = jnp.concatenate(
        [mlp_gain, w_router.reshape(-1), expert_ids.T.reshape(-1).astype(BF16)]
    )
    extra = -(-(others.shape[0] + 2 * head_size) // (own_rows * head_size)) * head_size
    spread = jnp.zeros((2, extra), BF16).at[0, :head_size].set(placed(query_gain))
    spread = spread.at[1, :head_size].set(placed(key_gain))
    spare = (own_rows - 2) * extra - others.shape[0]
    others = jnp.pad(others, (0, spare)).reshape(own_rows - 2, extra)
    small = jnp.concatenate([spread, others], axis=0)[None]
    scaled = jnp.concatenate([scaled, jnp.repeat(small, groups, axis=0)], axis=2)
    places = (
        ring.members[:, None] * tok_rows + jnp.arange(tok_rows, dtype=jnp.int32)[None, :]
    ).reshape(seq_rows)
    tables = rotary_tables(places.astype(F32), head_size)

    gate_w = lax.all_gather(w_gate, "fsdp", axis=1, tiled=True)
    token_ring = Gather(ring, tokens)
    (scaled,) = window([token_ring], scaled)
    qkv = lax.all_to_all(scaled, "seq", split_axis=0, concat_axis=0, tiled=True).reshape(
        groups * own_rows, qkv_width + extra
    )
    qkv, w_output = window([token_ring], qkv, w_output)
    part_rows = groups * own_rows // 2
    first_half = fsdp.spread(qkv[:part_rows])
    for step in range(3, ring.steps):
        qkv, first_half, tables, places, w_output = window(
            [token_ring], qkv, first_half, tables, places, w_output
        )
    cos_table, sine_table = tables
    second_half = fsdp.spread(qkv[part_rows:])
    qkv, first_half, second_half, w_output, w_up, cotangent_sent = window(
        [token_ring], qkv, first_half, second_half, w_output, w_up, cotangent
    )
    up_w = lax.all_gather(w_up, "fsdp", axis=1, tiled=True)

    cot_ring = Gather(ring, cotangent_sent)
    qkv_parts = fsdp.swapped(
        qkv, [jnp.concatenate(pair, axis=0) for pair in zip(first_half, second_half)]
    )
    gains_qk = sum(
        jnp.sum(
            part.reshape(groups, own_rows, qkv_width + extra)[
                :, :2, qkv_width : qkv_width + head_size
            ].astype(F32),
            axis=0,
        )
        for part in qkv_parts
    )
    projected = project(
        token_ring.pieces, qkv_parts, fsdp.blocks, qkv_width, cos_table, sine_table, gains_qk
    )
    held = lax.ppermute(w_output, ALL, exchange)
    projected, held, qkv_parts = window([cot_ring], projected, held, qkv_parts)
    normed_all, qk_pre, query_seq, key_seq, value_seq = projected
    attended, probs = attend(query_seq, key_seq, value_seq, places, scale_qk, tok_rows)
    held_others = fsdp.spread(held)
    attended, probs, held, held_others = window([cot_ring], attended, probs, held, held_others)
    output_w = lay(fsdp.swapped(held, held_others), fsdp.blocks)
    branch = jnp.dot(attended, output_w, preferred_element_type=F32).astype(BF16)
    for step in range(3, ring.steps):
        branch, output_w, gate_w, w_down = window([cot_ring], branch, output_w, gate_w, w_down)
    down_w = lax.all_gather(w_down, "fsdp", axis=2, tiled=True)

    branch_ring = Scatter(ring, lambda spot: (branch, spot), tok_rows)
    (qkv_parts,) = window([branch_ring, cot_ring], qkv_parts)

    def small_arrays(parts):
        small = jnp.stack([part[:, qkv_width:].reshape(groups, -1) for part in parts])
        small = jnp.take(small, fsdp.spots, axis=0)[:, :, 2 * extra :]
        cuts = [own_rows, own_rows * experts_all, tok_rows * top_k]
        ends = [sum(cuts[: i + 1]) for i in range(3)]
        gain_mlp = small[:, :, : ends[0]].reshape(1, model_width).astype(F32)
        router_w = small[:, :, ends[0] : ends[1]].reshape(model_width, experts_all)
        ids_all = parts[0][:, qkv_width:].reshape(groups, -1)[:, 2 * extra :]
        ids_near = jnp.take(ids_all[:, ends[1] : ends[2]], ring.members, axis=0)
        ids_near = ids_near.astype(jnp.int32).reshape(groups, top_k, tok_rows)
        return gain_mlp, router_w, ids_near.transpose(1, 0, 2).reshape(top_k, -1)

    (gain_mlp, router_w, ids_near), qkv_parts, cot_pieces = window(
        [branch_ring], small_arrays(qkv_parts), qkv_parts, cot_ring.pieces
    )
    qkv_w, cot_all = lay(qkv_parts, fsdp.blocks), lay(cot_pieces)
    for step in range(3, ring.steps):
        qkv_w, cot_all = window([branch_ring], qkv_w, cot_all)
    (up_w,) = window([branch_ring], up_w)
    middle, mixer_in = by_rows(
        enter_kernel, branch_ring.landed(), [tokens, gain_mlp], [F32, BF16]
    )

    def shares(rows_in, ids):
        logits = jnp.dot(rows_in, router_w, preferred_element_type=F32)
        chosen = jnp.sum(
            (ids[:, :, None] == jnp.arange(experts_all, dtype=jnp.int32)).astype(F32), axis=0
        )
        masked = jnp.where(chosen > 0, logits, NEG_LARGE)
        grown = jnp.exp(masked - jnp.max(masked, axis=-1, keepdims=True)) * chosen
        return grown / jnp.sum(grown, axis=-1, keepdims=True)

    def expert_part(rows_in, first):
        last = first + rows_in.shape[0]
        share = lax.dynamic_slice_in_dim(
            shares(rows_in, ids_near[:, first:last]), seat * local_experts, local_experts, 1
        ).T[:, :, None]
        gate_pre = jnp.einsum("td,edf->etf", rows_in, gate_w, preferred_element_type=F32)
        up_pre = jnp.einsum("td,edf->etf", rows_in, up_w, preferred_element_type=F32)
        back = down_back[:, first:last]
        sigmoid = jax.nn.sigmoid(gate_pre)
        silu_gate = gate_pre * sigmoid
        active = silu_gate * up_pre
        grad_share = jnp.sum(active * back, axis=-1)
        active_shared = (active * share).astype(BF16)
        grad_active = back * share
        grad_up_pre = (grad_active * silu_gate).astype(BF16)
        grad_gate_pre = (
            grad_active * up_pre * sigmoid * (1.0 + gate_pre * (1.0 - sigmoid))
        ).astype(BF16)
        return grad_share, active_shared, grad_gate_pre, grad_up_pre

    def entered_part(part):
        entered = jnp.einsum(
            "etf,edf->td", part[2], gate_w, preferred_element_type=F32
        ) + jnp.einsum("etf,edf->td", part[3], up_w, preferred_element_type=F32)
        return entered.astype(BF16)

    cut = ring.steps // 2
    early = (2 * cut + 1) * tok_rows
    mixer_ring = Gather(ring, mixer_in)
    cot_all, down_w = window([mixer_ring], cot_all, down_w)
    down_back = jnp.einsum("td,efd->etf", cot_all, down_w, preferred_element_type=F32)
    (down_back,) = window([mixer_ring], down_back)
    for step in range(3, cut + 1):
        window([mixer_ring])
    early_rows = jnp.concatenate(mixer_ring.pieces, axis=0)
    early_part = expert_part(early_rows, 0)
    for step in range(cut + 1, ring.steps):
        (early_rows,) = window([mixer_ring], early_rows)
    early_part, early_rows = window([mixer_ring], early_part, early_rows)
    late_rows = jnp.concatenate(mixer_ring.pieces[2 * cut + 1 :], axis=0)
    late_part = expert_part(late_rows, early)
    late_entered = entered_part(late_part)
    late_entered, late_part, early_part, late_rows, early_rows = together(
        late_entered, late_part, early_part, late_rows, early_rows
    )

    def entered_piece(spot):
        if spot * tok_rows >= early:
            return late_entered, spot - early // tok_rows
        return early_entered, spot

    entered_ring = Scatter(ring, entered_piece, tok_rows)
    grad_share = jnp.concatenate([early_part[0], late_part[0]], axis=1)
    grad_share_own = lax.all_to_all(
        jnp.take(grad_share.reshape(local_experts, groups, tok_rows), ring.spots, axis=1).transpose(
            1, 0, 2
        ),
        "seq",
        split_axis=0,
        concat_axis=0,
        tiled=True,
    )
    early_entered = entered_part(early_part)
    window([entered_ring])
    early_entered, early_part, late_part, early_rows, late_rows = window(
        [entered_ring], early_entered, early_part, late_part, early_rows, late_rows
    )
    for step in range(3, ring.steps):
        early_part, late_part, early_rows, late_rows, grad_share_own = window(
            [entered_ring], early_part, late_part, early_rows, late_rows, grad_share_own
        )
    early_part, late_part, early_rows, late_rows, grad_share_own = prepare(
        [entered_ring], early_part, late_part, early_rows, late_rows, grad_share_own
    )
    grad_share_own = grad_share_own.reshape(experts_all, tok_rows).T
    share_own = shares(mixer_in, expert_ids.T)
    grad_logits = (
        share_own
        * (grad_share_own - jnp.sum(share_own * grad_share_own, axis=-1, keepdims=True))
    ).astype(BF16)
    grad_gate = row_grads((early_rows, late_rows), (early_part[2], late_part[2]))
    grad_gate, grad_logits, early_part, late_part, early_rows, late_rows = window(
        [entered_ring], grad_gate, grad_logits, early_part, late_part, early_rows, late_rows
    )
    grad_gate = lax.psum_scatter(grad_gate, "fsdp", scatter_dimension=1, tiled=True)
    grad_middle, grad_branch, grad_gain_m = by_rows(
        mixer_back_kernel,
        entered_ring.landed(),
        [grad_logits, router_w, middle, cotangent, gain_mlp],
        [F32, BF16],
        [(1, model_width)],
    )

    grads_ring = Gather(ring, grad_branch)
    early_part, late_part, early_rows, late_rows = prepare(
        [grads_ring], early_part, late_part, early_rows, late_rows
    )
    grad_up = row_grads((early_rows, late_rows), (early_part[3], late_part[3]))
    grad_up, early_active, late_active = window(
        [grads_ring], grad_up, early_part[1], late_part[1]
    )
    grad_up = lax.psum_scatter(grad_up, "fsdp", scatter_dimension=1, tiled=True)
    produced = [
        jnp.einsum("etf,efd->td", active, down_w, preferred_element_type=F32).astype(BF16)
        for active in (early_active, late_active)
    ]
    produced, early_active, late_active = window(
        [grads_ring], produced, early_active, late_active
    )
    for step in range(3, cut + 1):
        window([grads_ring])

    def two_parts(parts):
        def piece(spot):
            if spot * tok_rows >= early:
                return parts[1], spot - early // tok_rows
            return parts[0], spot

        return piece

    def back(pieces, offset, before):
        return attend_back(
            pieces,
            offset,
            before,
            output_w,
            probs,
            query_seq,
            key_seq,
            value_seq,
            qk_pre,
            cos_table,
            sine_table,
            gains_qk,
            scale_qk,
        )

    grads = back(grads_ring.pieces, 0, None)
    grad_small = jnp.concatenate([dot(mixer_in, grad_logits, 0, 0), grad_gain_m.T], axis=1)
    grad_small = jnp.pad(grad_small, ((0, 0), (0, head_size - grad_small.shape[1])))
    for step in range(cut + 1, ring.steps):
        (grad_small,) = window([grads_ring], grad_small)
    layer_ring = Scatter(ring, two_parts(produced), tok_rows)
    (grads,) = window([grads_ring, layer_ring], grads)
    grads = back(grads_ring.pieces[2 * cut + 1 :], 2 * cut + 1, grads)
    (grads,) = window([layer_ring], grads)

    grads, grad_small = prepare([layer_ring], grads, grad_small)
    grad_qkv = grads[0]
    paired = fsdp.pair(
        project_back(normed_all, grad_qkv, grad_small, grads[1], own_rows, fsdp.targets)
    )
    for step in range(3, ring.steps):
        paired, grad_qkv = window([layer_ring], paired, grad_qkv)
    paired, grad_qkv, early_active, late_active = prepare(
        [layer_ring], paired, grad_qkv, early_active, late_active
    )
    sent = fsdp.send(paired)
    grad_hidden = dot(grad_qkv, qkv_w[:, :qkv_width], 1, 1).astype(BF16)
    grad_hidden, paired, branch_pieces, early_active, late_active = window(
        [layer_ring], grad_hidden, paired, grads_ring.pieces, early_active, late_active
    )
    (produced, spot), left, right = layer_ring.landed()
    layer_out = (
        middle
        + lax.slice_in_dim(produced, 0, tok_rows, axis=0).astype(F32)
        + left.astype(F32)
        + right.astype(F32)
    ).astype(BF16)

    hidden_ring = Scatter(ring, lambda spot: (grad_hidden, spot), tok_rows)
    branch_pieces, paired = prepare([hidden_ring], branch_pieces, paired)
    paired_output = fsdp.pair(output_back(attended, branch_pieces, fsdp.targets))
    paired, sent, paired_output, early_active, late_active = window(
        [hidden_ring], paired, sent, paired_output, early_active, late_active
    )
    total = paired[0].astype(F32) + sum(part.astype(F32) for part in sent)
    grad_qkv_w = lax.all_to_all(
        total.astype(BF16).reshape(groups, own_rows, qkv_width + head_size),
        "seq",
        split_axis=0,
        concat_axis=0,
        tiled=True,
    )
    sent_output = fsdp.send(paired_output)
    early_active, late_active, paired_output = prepare(
        [hidden_ring], early_active, late_active, paired_output
    )
    paired_down = fsdp.pair(down_grads((early_active, late_active), cot_all, fsdp.targets))
    paired_output, sent_output, paired_down = window(
        [hidden_ring], paired_output, sent_output, paired_down
    )
    total = paired_output[0].astype(F32) + sum(part.astype(F32) for part in sent_output)
    grad_output_w = lax.ppermute(total.astype(BF16), ALL, exchange)
    sent_down = fsdp.send(paired_down)

    def corner(array):
        return lax.slice(array, (0,) * array.ndim, (1,) * (array.ndim - 2) + (8, 128))

    grad_gate, grad_up = prepare([hidden_ring], grad_gate, grad_up)
    grad_gate, grad_up = grad_gate.astype(F32), grad_up.astype(F32)
    for step in range(3, ring.steps):
        grad_qkv_w, grad_output_w, _ = window(
            [hidden_ring], grad_qkv_w, grad_output_w, [corner(grad_gate), corner(grad_up)]
        )
    grad_output_w, paired_down, sent_down = prepare(
        [hidden_ring], grad_output_w, paired_down, sent_down
    )
    grad_output_w = grad_output_w.astype(F32)
    grad_down = paired_down[0].astype(F32) + sum(part.astype(F32) for part in sent_down)
    window([hidden_ring], [corner(grad_output_w), corner(grad_down), corner(layer_out)])
    (grad_tokens,) = by_rows(
        tokens_back_kernel, hidden_ring.landed(), [tokens, grad_middle], [BF16]
    )
    grad_query_w, grad_key_w, grad_value_w, grad_gain_a, small = weights_back(
        grad_qkv_w,
        weights_own,
        attn_gain.astype(F32)[:, None],
        held_groups,
        kv_heads,
        head_size,
    )
    gains = small[:4, head_size // 2 :].reshape(2, head_size)
    cut = query_gain.shape[0]
    gains = lax.dynamic_slice(gains, (0, me * cut), (2, cut))
    return (
        layer_out,
        grad_tokens,
        grad_gain_a[:, 0],
        grad_query_w,
        grad_key_w,
        grad_value_w,
        gains[0],
        gains[1],
        grad_output_w,
        small[:, experts_all],
        small[:, :experts_all],
        grad_gate,
        grad_up,
        grad_down,
    )


def solution(mesh):
    rows = P(("fsdp", "seq"), None)
    line = P(("fsdp", "seq"))
    wide = P("seq", "fsdp", None)
    deep = P("seq", None, "fsdp")
    in_specs = (
        rows, rows, rows, line, rows, rows, rows, line, line, rows, line, rows, wide, wide, deep,
    )
    out_specs = (
        rows, rows, line, rows, rows, rows, line, line, rows, line, rows, wide, wide, deep,
    )
    return jax.shard_map(
        on_device, mesh=mesh, in_specs=in_specs, out_specs=out_specs, check_vma=False
    )
```

```python
import math

import jax
import jax.numpy as jnp
import numpy as np
from jax import lax
from jax.experimental import pallas as pl
from jax.experimental.pallas import tpu as pltpu
from jax.sharding import PartitionSpec as P

NORM_EPS = 1e-06
ROPE_BASE = 1000000.0
NEG_LARGE = -1e30
F32 = jnp.float32
BF16 = jnp.bfloat16
ALL = ("fsdp", "seq")
VMEM_LIMIT = 40 * 1024 * 1024
LARGE_LIMIT = 56 * 1024 * 1024
SMALL_LIMIT = 16 * 1024 * 1024


def dot(left, right, left_dim, right_dim):
    return lax.dot_general(
        left, right, (((left_dim,), (right_dim,)), ((), ())), preferred_element_type=F32
    )


def norm_parts(values):
    row_scale = lax.rsqrt(jnp.mean(values * values, axis=-1, keepdims=True) + NORM_EPS)
    return (values * row_scale, row_scale)


def norm_back(grad_normed, normed, row_scale):
    return row_scale * (
        grad_normed - normed * jnp.mean(grad_normed * normed, axis=-1, keepdims=True)
    )


def rotary_tables(positions, head_size):
    half_size = head_size // 2
    frequency = jnp.exp(
        jnp.arange(half_size, dtype=F32) * (-2.0 * math.log(ROPE_BASE) / head_size)
    )
    angles = positions[:, None] * frequency[None, :]
    cosine, sine = jnp.cos(angles), jnp.sin(angles)
    return jnp.concatenate([cosine, cosine], axis=1), jnp.concatenate([-sine, sine], axis=1)


def swap_halves(values):
    return pltpu.roll(values, values.shape[-1] // 2, 1)


def params(limit=VMEM_LIMIT):
    return pltpu.CompilerParams(vmem_limit_bytes=limit)


def take_piece(step, pieces, halved, store):
    last = len(pieces) - (2 if halved else 0)
    for i in range(last):

        @pl.when(step == i)
        def _(i=i):
            store(0, pieces[i][...])

    if halved:

        @pl.when(step == last)
        def _():
            half = pieces[last].shape[0]
            store(0, pieces[last][...])
            store(half, pieces[last + 1][...])


def lay_kernel(count, halved, order_ref, *refs):
    def store(first, rows):
        refs[-1][first : first + rows.shape[0]] = rows

    take_piece(pl.program_id(0), refs[:count], halved, store)


def lay(pieces, order=None):
    halved = order is None
    members = len(pieces) - (1 if halved else 0)
    if halved:
        order = jnp.arange(members, dtype=jnp.int32)
    rows, cols = pieces[0].shape
    return pl.pallas_call(
        lambda *refs: lay_kernel(len(pieces), halved, *refs),
        grid_spec=pltpu.PrefetchScalarGridSpec(
            num_scalar_prefetch=1,
            grid=(members,),
            in_specs=[pl.BlockSpec(piece.shape, lambda i, order: (0, 0)) for piece in pieces],
            out_specs=pl.BlockSpec((rows, cols), lambda i, order: (order[i], 0)),
        ),
        out_shape=jax.ShapeDtypeStruct((members * rows, cols), pieces[0].dtype),
        compiler_params=params(),
        cost_estimate=pl.CostEstimate(
            flops=0, bytes_accessed=4 * members * rows * cols, transcendentals=0
        ),
    )(order, *pieces)


def project_kernel(heads, parts, count, order_ref, *refs):
    pieces, refs = refs[:count], refs[count:]
    weights, refs = refs[:parts], refs[parts:]
    cos_ref, sin_ref, gain_ref, n_ref, pre_ref, q_ref, k_ref, v_ref = refs
    size = cos_ref.shape[1]

    def store(first, rows):
        n_ref[first : first + rows.shape[0]] = norm_parts(rows.astype(F32))[0].astype(BF16)

    take_piece(pl.program_id(0), pieces, True, store)
    depth = weights[0].shape[0]
    projected = 0.0
    for part, w_ref in enumerate(weights):
        columns = pl.ds(pl.multiple_of(order_ref[part] * depth, depth), depth)
        projected += jnp.dot(n_ref[:, columns], w_ref[...], preferred_element_type=F32)
    pre_ref[...] = projected[:, : (heads + 1) * size]
    for head in range(heads + 1):
        row = 0 if head < heads else 1
        scaled = norm_parts(projected[:, head * size : (head + 1) * size])[0] * gain_ref[row : row + 1]
        turned = (scaled * cos_ref[...] + swap_halves(scaled) * sin_ref[...]).astype(BF16)
        if head < heads:
            q_ref[:, head * size : (head + 1) * size] = turned
        else:
            k_ref[...] = turned
    v_ref[...] = projected[:, (heads + 1) * size :].astype(BF16)


def project(pieces, weights, order, width, cos_table, sine_table, gains):
    block, depth = pieces[0].shape
    rows = block * (len(pieces) - 1)
    size = cos_table.shape[1]
    heads = width // size - 2
    spec = lambda cols: pl.BlockSpec((block, cols), lambda i, order: (i, 0))
    whole = lambda shape: pl.BlockSpec(shape, lambda i, order: (0, 0))
    return pl.pallas_call(
        lambda *refs: project_kernel(heads, len(weights), len(pieces), *refs),
        grid_spec=pltpu.PrefetchScalarGridSpec(
            num_scalar_prefetch=1,
            grid=(rows // block,),
            in_specs=[whole(piece.shape) for piece in pieces]
            + [whole((part.shape[0], width)) for part in weights]
            + [spec(size), spec(size), whole(gains.shape)],
            out_specs=[
                spec(depth), spec((heads + 1) * size), spec(heads * size), spec(size), spec(size),
            ],
        ),
        out_shape=[
            jax.ShapeDtypeStruct((rows, depth), BF16),
            jax.ShapeDtypeStruct((rows, (heads + 1) * size), F32),
            jax.ShapeDtypeStruct((rows, heads * size), BF16),
            jax.ShapeDtypeStruct((rows, size), BF16),
            jax.ShapeDtypeStruct((rows, size), BF16),
        ],
        compiler_params=params(LARGE_LIMIT),
        cost_estimate=pl.CostEstimate(
            flops=2 * rows * depth * width, bytes_accessed=16 << 20, transcendentals=0
        ),
    )(order, *pieces, *weights, cos_table, sine_table, gains)


def fetch(arrays, spots, buffers, sems):
    copies = [
        pltpu.make_async_copy(
            array.at[pl.ds(spot * buffer.shape[0], buffer.shape[0])], buffer, sems.at[i]
        )
        for i, (array, spot, buffer) in enumerate(zip(arrays, spots, buffers))
    ]
    for copy in copies:
        copy.start()
    for copy in copies:
        copy.wait()


def ring_add_kernel(spots, up_hbm, down_hbm, left_ref, right_ref, up_ref, down_ref, up_buf, down_buf, sems):
    fetch((up_hbm, down_hbm), spots, (up_buf, down_buf), sems)
    rows, half = up_buf.shape[0], left_ref.shape[0]
    if half == rows:
        up_ref[...] = (up_buf[...].astype(F32) + left_ref[...].astype(F32)).astype(BF16)
        down_ref[...] = (down_buf[...].astype(F32) + right_ref[...].astype(F32)).astype(BF16)
        return
    up_ref[:half] = (up_buf[:half].astype(F32) + left_ref[...].astype(F32)).astype(BF16)
    up_ref[half:] = up_buf[half:]
    down_ref[:half] = down_buf[:half]
    down_ref[half:] = (down_buf[half:].astype(F32) + right_ref[...].astype(F32)).astype(BF16)


HBM = pl.BlockSpec(memory_space=pltpu.HBM)
VMEM = pl.BlockSpec(memory_space=pltpu.VMEM)


def ring_add(mine_up, mine_down, left, right, rows):
    width = left.shape[1]
    return pl.pallas_call(
        lambda *refs: ring_add_kernel((mine_up[1], mine_down[1]), *refs),
        in_specs=[HBM, HBM, VMEM, VMEM],
        out_specs=[VMEM, VMEM],
        out_shape=[jax.ShapeDtypeStruct((rows, width), BF16)] * 2,
        scratch_shapes=[pltpu.VMEM((rows, width), BF16)] * 2 + [pltpu.SemaphoreType.DMA((2,))],
        compiler_params=pltpu.CompilerParams(vmem_limit_bytes=SMALL_LIMIT),
        cost_estimate=pl.CostEstimate(
            flops=2 * rows * width, bytes_accessed=12 * rows * width, transcendentals=0
        ),
    )(mine_up[0], mine_down[0], left, right)


def summed(mine_ref, left_ref, right_ref):
    return mine_ref[...].astype(F32) + left_ref[...].astype(F32) + right_ref[...].astype(F32)


def enter_kernel(mine_ref, left_ref, right_ref, x_ref, gain_ref, middle_ref, mixer_ref):
    middle = x_ref[...].astype(F32) + summed(mine_ref, left_ref, right_ref)
    middle_ref[...] = middle
    mixer_ref[...] = (norm_parts(middle)[0] * gain_ref[...]).astype(BF16)


def mixer_back_kernel(
    mine_ref, left_ref, right_ref, middle_ref, cot_ref, logits_ref, router_ref, gain_ref, *refs
):
    grad_ref, branch_ref, gains_ref = refs
    grad_mixer = summed(mine_ref, left_ref, right_ref) + dot(logits_ref[...], router_ref[...], 1, 1)
    normed, row_scale = norm_parts(middle_ref[...])
    gains_ref[...] = jnp.sum(grad_mixer * normed, axis=0, keepdims=True)
    grad = cot_ref[...].astype(F32) + norm_back(grad_mixer * gain_ref[...], normed, row_scale)
    grad_ref[...] = grad
    branch_ref[...] = grad.astype(BF16)


def tokens_back_kernel(mine_ref, left_ref, right_ref, x_ref, grad_ref, out_ref):
    normed, row_scale = norm_parts(x_ref[...].astype(F32))
    grad = norm_back(summed(mine_ref, left_ref, right_ref), normed, row_scale)
    out_ref[...] = (grad_ref[...] + grad).astype(BF16)


def by_rows(kernel, landed, lines, inputs, outs, sums=()):
    (mine, spot), left, right = landed
    rows, width = left.shape
    count = 1 + len(lines)

    def whole(*refs):
        arrays, refs = refs[:count], refs[count:]
        refs, buffers, sems = refs[: -count - 1], refs[-count - 1 : -1], refs[-1]
        fetch(arrays, (spot,) + (0,) * len(lines), buffers, sems)
        kernel(buffers[0], *refs[:2], *buffers[1:], *refs[2:])

    return pl.pallas_call(
        whole,
        in_specs=[HBM] * count + [VMEM] * (2 + len(inputs)),
        out_specs=[VMEM] * (len(outs) + len(sums)),
        out_shape=[jax.ShapeDtypeStruct((rows, width), kind) for kind in outs]
        + [jax.ShapeDtypeStruct(shape, F32) for shape in sums],
        scratch_shapes=[pltpu.VMEM((rows, array.shape[1]), array.dtype) for array in [mine] + lines]
        + [pltpu.SemaphoreType.DMA((count,))],
        compiler_params=pltpu.CompilerParams(vmem_limit_bytes=SMALL_LIMIT),
        cost_estimate=pl.CostEstimate(
            flops=20 * rows * width, bytes_accessed=16 * rows * width, transcendentals=rows
        ),
    )(mine, *lines, left, right, *inputs)


def weights_back_kernel(held, copies, size, came_ref, own_ref, gain_ref, q_ref, k_ref, v_ref, gains_ref, small_ref):
    groups, rows, _ = came_ref.shape
    width = own_ref.shape[2]
    wide = width - 2 * size
    gains = jnp.zeros((rows, 1), F32)
    small = jnp.zeros(small_ref.shape, F32)
    gain = gain_ref[...]
    seen = set()
    for member, group in enumerate(held):
        came = came_ref[member].astype(F32)
        gains += jnp.sum(
            came[:, :width] * own_ref[member].astype(F32), axis=1, keepdims=True
        )
        small += came[:, width:]
        came = came[:, :width] * gain
        q_ref[:, group * wide : (group + 1) * wide] = came[:, :wide]
        lanes = slice(group // copies * size, (group // copies + 1) * size)
        if group // copies not in seen:
            k_ref[:, lanes] = came[:, wide : wide + size]
            v_ref[:, lanes] = came[:, wide + size :]
        else:
            k_ref[:, lanes] += came[:, wide : wide + size]
            v_ref[:, lanes] += came[:, wide + size :]
        seen.add(group // copies)
    gains_ref[...] = jnp.broadcast_to(gains, gains_ref.shape)
    small_ref[...] = small


def weights_back(came, own, gain, held, kv_heads, size):
    groups, rows, total = came.shape
    width = own.shape[2]
    shape = lambda cols: jax.ShapeDtypeStruct((rows, cols), F32)
    return pl.pallas_call(
        lambda *refs: weights_back_kernel(held, groups // kv_heads, size, *refs),
        out_shape=[
            shape(groups * (width - 2 * size)),
            shape(kv_heads * size),
            shape(kv_heads * size),
            shape(128),
            shape(total - width),
        ],
        compiler_params=params(),
        cost_estimate=pl.CostEstimate(
            flops=4 * groups * rows * width, bytes_accessed=4 << 20, transcendentals=0
        ),
    )(came, own, gain)


def output_back_kernel(count, order_ref, left_ref, *refs):
    pieces, outs, (rows_ref, turned_ref, sum_ref) = refs[:count], refs[count:-3], refs[-3:]

    @pl.when(pl.program_id(0) == 0)
    def _():
        turned_ref[...] = left_ref[...].T

    first = 0
    for piece in pieces:
        rows_ref[first : first + piece.shape[0]] = piece[...]
        first += piece.shape[0]
    sum_ref[...] = jnp.dot(turned_ref[...], rows_ref[...], preferred_element_type=F32)
    for i, out_ref in enumerate(outs):
        rows = out_ref.shape[0]
        first = pl.multiple_of(order_ref[i] * rows, rows)
        out_ref[...] = sum_ref[pl.ds(first, rows), :].astype(BF16)


def output_back(left, pieces, order):
    rows, width = left.shape
    cols = pieces[0].shape[1]
    parts = order.shape[0]
    block = cols // 4
    return pl.pallas_call(
        lambda *refs: output_back_kernel(len(pieces), *refs),
        grid_spec=pltpu.PrefetchScalarGridSpec(
            num_scalar_prefetch=1,
            grid=(4,),
            in_specs=[pl.BlockSpec((rows, width), lambda i, order: (0, 0))]
            + [pl.BlockSpec((piece.shape[0], block), lambda i, order: (0, i)) for piece in pieces],
            out_specs=[pl.BlockSpec((width // parts, block), lambda i, order: (0, i))] * parts,
            scratch_shapes=[
                pltpu.VMEM((rows, block), BF16),
                pltpu.VMEM((width, rows), BF16),
                pltpu.VMEM((width, block), F32),
            ],
        ),
        out_shape=[jax.ShapeDtypeStruct((width // parts, cols), BF16)] * parts,
        compiler_params=params(),
        cost_estimate=pl.CostEstimate(
            flops=2 * rows * width * cols, bytes_accessed=8 << 20, transcendentals=0
        ),
    )(order, left, *pieces)


def project_back_kernel(
    own_rows, place, order_ref, normed_ref, grad_ref, small_ref, line_ref, gains_ref, *outs
):
    width = grad_ref.shape[1]
    part = dot(normed_ref[...], grad_ref[...], 0, 0).astype(BF16)
    small = small_ref[...]
    size = small.shape[1]
    row = lax.broadcasted_iota(jnp.int32, small.shape, 0) % own_rows
    lane = lax.broadcasted_iota(jnp.int32, small.shape, 1)
    small = jnp.where(lane == place, jnp.broadcast_to(line_ref[...], (size, small.shape[0])).T, small)
    upper = lane >= size // 2
    for i in range(2):
        gain = gains_ref[i : i + 1]
        for half, line in enumerate((pltpu.roll(gain, size // 2, 1), gain)):
            small = jnp.where(upper & (row == 2 * i + half), line, small)
    small = small.astype(BF16)
    for i, out_ref in enumerate(outs):

        @pl.when(pl.program_id(0) == i)
        def _(out_ref=out_ref):
            out_ref[:, :width] = part
            out_ref[:, width:] = small


def project_back(normed, grad, small, line, place, gains, own_rows, order):
    rows, depth = normed.shape
    width, extra = grad.shape[1], small.shape[1]
    parts = order.shape[0]
    block = depth // parts
    whole = lambda shape: pl.BlockSpec(shape, lambda i, order: (0, 0))
    return pl.pallas_call(
        lambda *refs: project_back_kernel(own_rows, place, *refs),
        grid_spec=pltpu.PrefetchScalarGridSpec(
            num_scalar_prefetch=1,
            grid=(parts,),
            in_specs=[
                pl.BlockSpec((rows, block), lambda i, order: (0, order[i])),
                whole(grad.shape),
                pl.BlockSpec((block, extra), lambda i, order: (order[i], 0)),
                pl.BlockSpec((1, block), lambda i, order: (0, order[i])),
                whole(gains.shape),
            ],
            out_specs=[whole((block, width + extra))] * parts,
        ),
        out_shape=[jax.ShapeDtypeStruct((block, width + extra), BF16)] * parts,
        compiler_params=params(),
        cost_estimate=pl.CostEstimate(
            flops=2 * rows * depth * width, bytes_accessed=12 << 20, transcendentals=0
        ),
    )(order, normed, grad, small, line, gains)


def row_grads_kernel(first_ref, second_ref, *refs):
    count = len(refs) // 3
    grads, outs = refs[: 2 * count], refs[2 * count :]
    first, second = first_ref[...].T, second_ref[...].T
    for i, out_ref in enumerate(outs):
        for expert in range(out_ref.shape[0]):
            part = dot(first, grads[2 * i][expert], 1, 0)
            part += dot(second, grads[2 * i + 1][expert], 1, 0)
            out_ref[expert] = part.astype(BF16)


def row_grads(rows, *grads):
    experts, _, ff = grads[0][0].shape
    depth = rows[0].shape[1]
    block = depth // 8
    return pl.pallas_call(
        row_grads_kernel,
        grid=(8,),
        in_specs=[pl.BlockSpec((part.shape[0], block), lambda i: (0, i)) for part in rows]
        + [pl.BlockSpec(part.shape, lambda i: (0, 0, 0)) for pair in grads for part in pair],
        out_specs=[pl.BlockSpec((experts, block, ff), lambda i: (0, i, 0))] * len(grads),
        out_shape=[jax.ShapeDtypeStruct((experts, depth, ff), BF16)] * len(grads),
        compiler_params=params(LARGE_LIMIT),
        cost_estimate=pl.CostEstimate(
            flops=2 * len(grads) * experts * sum(part.shape[0] for part in rows) * ff * depth,
            bytes_accessed=24 << 20,
            transcendentals=0,
        ),
    )(*rows, *(part for pair in grads for part in pair))


def down_grads_kernel(order_ref, first_ref, second_ref, cot_ref, *refs):
    outs, turned_ref = refs[:-1], refs[-1]
    expert, step = pl.program_id(0), pl.program_id(1)
    cut = first_ref.shape[1]

    @pl.when(step == 0)
    def _():
        turned_ref[:, :cut] = first_ref[0].T
        turned_ref[:, cut:] = second_ref[0].T

    part = jnp.dot(turned_ref[...], cot_ref[...], preferred_element_type=F32).astype(BF16)
    for i, out_ref in enumerate(outs):

        @pl.when(step == i)
        def _(out_ref=out_ref):
            out_ref[expert] = part


def down_grads(active, cot, order):
    experts, _, ff = active[0].shape
    rows, depth = cot.shape
    parts = order.shape[0]
    block = depth // parts
    return pl.pallas_call(
        down_grads_kernel,
        grid_spec=pltpu.PrefetchScalarGridSpec(
            num_scalar_prefetch=1,
            grid=(experts, parts),
            in_specs=[
                pl.BlockSpec((1,) + part.shape[1:], lambda e, i, order: (e, 0, 0))
                for part in active
            ]
            + [pl.BlockSpec((rows, block), lambda e, i, order: (0, order[i]))],
            out_specs=[pl.BlockSpec((experts, ff, block), lambda e, i, order: (0, 0, 0))] * parts,
            scratch_shapes=[pltpu.VMEM((ff, rows), BF16)],
        ),
        out_shape=[jax.ShapeDtypeStruct((experts, ff, block), BF16)] * parts,
        compiler_params=params(),
        cost_estimate=pl.CostEstimate(
            flops=2 * experts * rows * ff * depth, bytes_accessed=16 << 20, transcendentals=0
        ),
    )(order, *active, cot)


def split_rows(result, outs):
    first = 0
    for out_ref in outs:
        out_ref[...] = result[first : first + out_ref.shape[0]].astype(BF16)
        first += out_ref.shape[0]


def split_shapes(rows, block, cols, halved):
    heights = [block] * (rows // block)
    if halved:
        heights[-1:] = [block // 2, block // 2]
    return [jax.ShapeDtypeStruct((height, cols), BF16) for height in heights]


def rows_dot(left, right, right_dim, block):
    rows, depth = left.shape
    cols = right.shape[1 - right_dim]
    each = cols // 4
    shapes = split_shapes(rows, block, cols, True)
    if right_dim:
        spec = pl.BlockSpec((each, depth), lambda i: (i, 0))
    else:
        spec = pl.BlockSpec((depth, each), lambda i: (0, i))
    return pl.pallas_call(
        lambda left_ref, right_ref, *outs: split_rows(
            dot(left_ref[...], right_ref[...], 1, right_dim), outs
        ),
        grid=(4,),
        in_specs=[pl.BlockSpec((rows, depth), lambda i: (0, 0)), spec],
        out_specs=[pl.BlockSpec((shape.shape[0], each), lambda i: (0, i)) for shape in shapes],
        out_shape=shapes,
        compiler_params=params(),
        cost_estimate=pl.CostEstimate(
            flops=2 * rows * depth * cols, bytes_accessed=8 << 20, transcendentals=0
        ),
    )(left, right)


def entered_kernel(first_ref, second_ref, first_w_ref, second_w_ref, *outs):
    total = 0.0
    for expert in range(first_ref.shape[0]):
        total += dot(first_ref[expert], first_w_ref[expert], 1, 1)
        total += dot(second_ref[expert], second_w_ref[expert], 1, 1)
    split_rows(total, outs)


def entered_rows(first, second, first_w, second_w, block):
    experts, rows, ff = first.shape
    depth = first_w.shape[1]
    each = depth // 8
    whole = pl.BlockSpec(first.shape, lambda i: (0, 0, 0))
    weight = pl.BlockSpec((experts, each, ff), lambda i: (0, i, 0))
    shapes = split_shapes(rows, block, depth, False)
    return pl.pallas_call(
        entered_kernel,
        grid=(8,),
        in_specs=[whole, whole, weight, weight],
        out_specs=[pl.BlockSpec((block, each), lambda i: (0, i))] * len(shapes),
        out_shape=shapes,
        compiler_params=params(LARGE_LIMIT),
        cost_estimate=pl.CostEstimate(
            flops=4 * experts * rows * ff * depth, bytes_accessed=20 << 20, transcendentals=0
        ),
    )(first, second, first_w, second_w)


def stack_heads(array, size):
    return jnp.concatenate(
        [array[:, i * size : (i + 1) * size] for i in range(array.shape[1] // size)], axis=0
    )


def attend_kernel(scale, q_ref, k_ref, v_ref, at_q_ref, at_k_ref, out_ref, p_ref):
    rows, size = q_ref.shape[0], k_ref.shape[1]
    heads = q_ref.shape[1] // size
    scores = dot(k_ref[...], stack_heads(q_ref[...], size), 1, 1) * scale
    at_q = jnp.concatenate([at_q_ref[...]] * heads, axis=1)
    scores = jnp.where(at_k_ref[...] <= at_q, scores, NEG_LARGE)
    grown = jnp.exp(scores - jnp.max(scores, axis=0, keepdims=True))
    probs = (grown * (1.0 / jnp.sum(grown, axis=0, keepdims=True))).astype(BF16)
    p_ref[...] = probs
    output = dot(v_ref[...].T, probs, 1, 0).T.astype(BF16)
    for head in range(heads):
        out_ref[:, head * size : (head + 1) * size] = output[head * rows : (head + 1) * rows]


def attend(query, key, value, places, scale, block):
    rows, width = query.shape
    size = key.shape[1]
    heads = width // size
    whole = lambda shape: pl.BlockSpec(shape, lambda i: (0, 0))
    return pl.pallas_call(
        lambda *refs: attend_kernel(scale, *refs),
        grid=(rows // block,),
        in_specs=[
            pl.BlockSpec((block, width), lambda i: (i, 0)),
            whole((rows, size)),
            whole((rows, size)),
            pl.BlockSpec((1, block), lambda i: (0, i)),
            whole((rows, 1)),
        ],
        out_specs=[
            pl.BlockSpec((block, width), lambda i: (i, 0)),
            pl.BlockSpec((rows, heads * block), lambda i: (0, i)),
        ],
        out_shape=[
            jax.ShapeDtypeStruct((rows, width), BF16),
            jax.ShapeDtypeStruct((rows, heads * rows), BF16),
        ],
        compiler_params=params(LARGE_LIMIT),
        cost_estimate=pl.CostEstimate(
            flops=4 * heads * rows * rows * size,
            bytes_accessed=12 << 20,
            transcendentals=heads * rows * rows,
        ),
    )(query, key, value, places[None, :], places[:, None])


def head_back(grad_turned, pre, gain, cosine, sine):
    grad = grad_turned * cosine - swap_halves(grad_turned) * sine
    normed, row_scale = norm_parts(pre)
    return (
        jnp.sum(grad * normed, axis=0, keepdims=True),
        norm_back(grad * gain, normed, row_scale).astype(BF16),
    )


def attend_back_kernel(scale, count, first, last, offset, *refs):
    pieces, refs = refs[:count], refs[count:]
    w_ref, p_ref, q_ref, k_ref, v_ref, pre_ref, cos_ref, sin_ref, gain_ref = refs[:9]
    refs = refs[9:]
    before, refs = (() if first else refs[:4]), (refs if first else refs[4:])
    out_ref, gains_ref, dk_ref, dv_ref, rows_ref = refs
    step = pl.program_id(0)
    rows, size = q_ref.shape[0], k_ref.shape[1]
    heads = q_ref.shape[1] // size

    def store(first, rows):
        rows_ref[first : first + rows.shape[0]] = rows

    take_piece(step, pieces, last, store)

    @pl.when(step == 0)
    def _():
        if first:
            dk_ref[...] = jnp.zeros_like(dk_ref)
            dv_ref[...] = jnp.zeros_like(dv_ref)
            gains_ref[...] = jnp.zeros_like(gains_ref)
        else:
            for now_ref, before_ref in zip((out_ref, gains_ref, dk_ref, dv_ref), before):
                now_ref[...] = before_ref[...]

    probs = p_ref[...]
    grads = stack_heads(dot(rows_ref[...], w_ref[...], 1, 1).astype(BF16), size)
    dv_ref[...] += dot(probs, grads, 1, 0)
    grad_probs = dot(v_ref[...], grads, 1, 1)
    probs = probs.astype(F32)
    grad_scores = (
        probs * (grad_probs - jnp.sum(probs * grad_probs, axis=0, keepdims=True))
    ).astype(BF16)
    dk_ref[...] += dot(grad_scores, stack_heads(q_ref[...], size), 1, 0)
    grad_query = dot(k_ref[...].T, grad_scores, 1, 0).T * scale
    start = pl.multiple_of((step + offset) * rows, rows)
    here = pl.ds(start, rows)
    cosine, sine = cos_ref[here, :], sin_ref[here, :]
    for head in range(heads):
        lanes = slice(head * size, (head + 1) * size)
        gain_part, part = head_back(
            grad_query[head * rows : (head + 1) * rows],
            pre_ref[here, lanes],
            gain_ref[0:1],
            cosine,
            sine,
        )
        gains_ref[0:1] += gain_part
        out_ref[here, lanes] = part

    if last:

        @pl.when(step == pl.num_programs(0) - 1)
        def _():
            gain_part, part = head_back(
                dk_ref[...] * scale,
                pre_ref[:, heads * size : (heads + 1) * size],
                gain_ref[1:2],
                cos_ref[...],
                sin_ref[...],
            )
            gains_ref[1:2] = gain_part
            out_ref[:, heads * size : (heads + 1) * size] = part
            out_ref[:, (heads + 1) * size :] = dv_ref[...].astype(BF16)


def attend_back(pieces, offset, before, weights, probs, query, key, value, pre, cos_table, sine_table, gains, scale):
    rows, width = query.shape
    size = key.shape[1]
    heads = width // size
    block, depth = pieces[0].shape
    first, last = before is None, before is not None
    steps = len(pieces) - (1 if last else 0)
    whole = lambda shape: pl.BlockSpec(shape, lambda i: (0, 0))
    shapes = [
        jax.ShapeDtypeStruct((rows, (heads + 2) * size), BF16),
        jax.ShapeDtypeStruct((8, size), F32),
        jax.ShapeDtypeStruct((rows, size), F32),
        jax.ShapeDtypeStruct((rows, size), F32),
    ]
    outs = [whole(shape.shape) for shape in shapes]
    return pl.pallas_call(
        lambda *refs: attend_back_kernel(scale, len(pieces), first, last, offset, *refs),
        grid=(steps,),
        in_specs=[whole(piece.shape) for piece in pieces]
        + [
            whole(weights.shape),
            pl.BlockSpec((rows, heads * block), lambda i: (0, i + offset)),
            pl.BlockSpec((block, width), lambda i: (i + offset, 0)),
            whole((rows, size)),
            whole((rows, size)),
            whole((rows, (heads + 1) * size)),
            whole((rows, size)),
            whole((rows, size)),
            whole(gains.shape),
        ]
        + ([] if first else outs),
        out_specs=outs,
        out_shape=shapes,
        scratch_shapes=[pltpu.VMEM((block, depth), BF16)],
        compiler_params=params(),
        cost_estimate=pl.CostEstimate(
            flops=(8 * heads * rows * size + 2 * depth * width) * steps * block,
            bytes_accessed=(3 << 20) * steps,
            transcendentals=0,
        ),
    )(*pieces, weights, probs, query, key, value, pre, cos_table, sine_table, gains, *(before or ()))


def after(value, *others):
    return lax.optimization_barrier((value, *others))[0]


def ring_order(size):
    if size % 4 or size < 8:
        return list(range(size))
    wide = size // 4
    walk = [(0, y) for y in range(wide)]
    for z in range(1, 4):
        walk += [(z, y) for y in (range(wide - 1, 0, -1) if z % 2 else range(1, wide))]
    walk += [(z, 0) for z in (3, 2, 1)]
    return [z * wide + y for z, y in walk]


def together(*values):
    return lax.optimization_barrier(values)


class Ring:
    def __init__(self, size):
        self.size = size
        self.steps = size // 2
        order = ring_order(size)
        self.up = [(order[i], order[(i + 1) % size]) for i in range(size)]
        self.down = [(order[i], order[(i - 1) % size]) for i in range(size)]
        self.offsets = [0]
        for step in range(1, self.steps):
            self.offsets += [-step, step]
        self.offsets += [self.steps]
        near = np.zeros((size, size), np.int32)
        for i, member in enumerate(order):
            near[member] = [order[(i + offset) % size] for offset in self.offsets]
        seat = lax.axis_index("seq")
        self.members = jnp.asarray(near)[seat]
        self.spots = jnp.asarray(np.argsort(near, axis=1).astype(np.int32))[seat]

    def swap(self, up, down):
        return lax.ppermute(up, "seq", self.up), lax.ppermute(down, "seq", self.down)

    def spot(self, offset):
        return self.offsets.index(offset)


class Gather:
    def __init__(self, ring, block):
        self.ring, self.step, self.pieces = ring, 0, [block]
        self.left = self.right = block
        self.ready = None

    def sends(self):
        if self.step + 1 < self.ring.steps:
            return self.left, self.right
        half = self.left.shape[0] // 2
        return self.left[:half], self.right[half:]

    def start(self):
        ready = self.ready or self.sends()
        self.step += 1
        self.ready = None
        return self.ring.swap(*ready)

    def end(self, left, right):
        self.left, self.right = left, right
        self.pieces += [left, right]


class Scatter:
    def __init__(self, ring, piece, rows, far=None):
        self.ring, self.step, self.piece, self.rows, self.far = ring, 0, piece, rows, far
        self.left = self.right = self.ready = None

    def sends(self):
        ring, rows = self.ring, self.rows
        if self.step == 0 and self.far:
            return self.far
        if self.step == 0:
            whole, spot = self.piece(ring.spot(ring.steps))
            start, middle, end = spot * rows, spot * rows + rows // 2, (spot + 1) * rows
            return (
                lax.slice_in_dim(whole, start, middle, axis=0),
                lax.slice_in_dim(whole, middle, end, axis=0),
            )
        place = ring.steps - self.step
        mine_up, mine_down = self.piece(ring.spot(place)), self.piece(ring.spot(-place))
        return ring_add(mine_up, mine_down, self.left, self.right, rows)

    def start(self):
        ready = self.ready or self.sends()
        self.step += 1
        self.ready = None
        return self.ring.swap(*ready)

    def end(self, left, right):
        self.left, self.right = left, right

    def landed(self):
        return self.piece(0), self.left, self.right


def prepare(rings, *values):
    ready, values = together([ring.sends() for ring in rings], values)
    for ring, sends in zip(rings, ready):
        ring.ready = tuple(sends)
    return values


def window(rings, *values):
    moved = [ring.start() for ring in rings]
    moved, values = together(moved, values)
    for ring, (left, right) in zip(rings, moved):
        ring.end(left, right)
    return values


class Fsdp:
    def __init__(self, size):
        self.size = size
        self.across = size // 2

        def blocks(way):
            return np.asarray(
                [
                    [
                        (i // 2 + way * step) % self.across * 2 + (i % 2 ^ flip)
                        for step in range(self.across)
                        for flip in (0, 1)
                    ]
                    for i in range(size)
                ],
                np.int32,
            )

        index = lax.axis_index("fsdp")
        self.blocks = jnp.asarray(blocks(-1))[index]
        self.targets = jnp.asarray(blocks(1))[index]
        self.spots = jnp.asarray(np.argsort(blocks(-1), axis=1).astype(np.int32))[index]

    def swap(self, array):
        return lax.ppermute(array, "fsdp", [(i, i ^ 1) for i in range(self.size)])

    def shift(self, array, step):
        perm = [
            (x * 2 + c, (x + step) % self.across * 2 + c)
            for x in range(self.across)
            for c in (0, 1)
        ]
        return lax.ppermute(array, "fsdp", perm)

    def spread(self, block):
        return [self.shift(block, step) for step in range(1, self.across)]

    def swapped(self, block, others):
        return [part for mine in [block] + others for part in (mine, self.swap(mine))]

    def pair(self, parts):
        return [
            (parts[i].astype(F32) + self.swap(parts[i + 1]).astype(F32)).astype(BF16)
            for i in range(0, self.size, 2)
        ]

    def send(self, paired):
        return [self.shift(part, step) for step, part in enumerate(paired) if step]


def on_device(
    tokens,
    cotangent,
    expert_ids,
    attn_gain,
    w_query,
    w_key,
    w_value,
    query_gain,
    key_gain,
    w_output,
    mlp_gain,
    w_router,
    w_gate,
    w_up,
    w_down,
):
    groups = lax.axis_size("seq")
    splits = lax.axis_size("fsdp")
    counts = groups * splits
    ring, fsdp = Ring(groups), Fsdp(splits)
    seat = lax.axis_index("seq")
    me = lax.axis_index(ALL)
    tok_rows, model_width = tokens.shape
    top_k = expert_ids.shape[1]
    own_rows = w_query.shape[0]
    head_size = query_gain.shape[0] * counts
    heads_all = w_query.shape[1] // head_size
    kv_heads = w_key.shape[1] // head_size
    head_local = heads_all // groups
    copies = groups // kv_heads
    query_width = head_local * head_size
    qkv_width = query_width + 2 * head_size
    experts_all = w_router.shape[1]
    local_experts, _, ff = w_gate.shape
    seq_rows = tok_rows * groups
    scale_qk = 1.0 / math.sqrt(head_size)

    held_groups = [seat % splits * (groups // splits) + seat // splits for seat in range(groups)]
    exchange = [
        (j * groups + part * splits + i, i * groups + part * splits + j)
        for j in range(splits)
        for part in range(groups // splits)
        for i in range(splits)
    ]

    def by_member(weights, group_of):
        width = weights.shape[1] // (max(group_of) + 1)
        return [weights[:, group * width : (group + 1) * width] for group in group_of]

    kv_of = [group // copies for group in held_groups]
    weights_own = jnp.stack(
        [
            jnp.concatenate(parts, axis=1)
            for parts in zip(
                by_member(w_query, held_groups), by_member(w_key, kv_of), by_member(w_value, kv_of)
            )
        ]
    )
    scaled = (weights_own.astype(F32) * attn_gain.astype(F32)[None, :, None]).astype(BF16)

    def placed(gain):
        return lax.dynamic_update_slice(
            jnp.zeros((head_size,), BF16), gain, (me * gain.shape[0],)
        )

    others = jnp.concatenate(
        [mlp_gain, w_router.reshape(-1), expert_ids.T.reshape(-1).astype(BF16)]
    )
    extra = -(-(others.shape[0] + 2 * head_size) // (own_rows * head_size)) * head_size
    spread = jnp.zeros((2, extra), BF16).at[0, :head_size].set(placed(query_gain))
    spread = spread.at[1, :head_size].set(placed(key_gain))
    spare = (own_rows - 2) * extra - others.shape[0]
    others = jnp.pad(others, (0, spare)).reshape(own_rows - 2, extra)
    small = jnp.concatenate([spread, others], axis=0)[None]
    scaled = jnp.concatenate([scaled, jnp.repeat(small, groups, axis=0)], axis=2)
    places = (
        ring.members[:, None] * tok_rows + jnp.arange(tok_rows, dtype=jnp.int32)[None, :]
    ).reshape(seq_rows)
    tables = rotary_tables(places.astype(F32), head_size)

    gate_w = lax.all_gather(w_gate, "fsdp", axis=1, tiled=True)
    token_ring = Gather(ring, tokens)
    (scaled,) = window([token_ring], scaled)
    qkv = lax.all_to_all(scaled, "seq", split_axis=0, concat_axis=0, tiled=True).reshape(
        groups * own_rows, qkv_width + extra
    )
    qkv, w_output = window([token_ring], qkv, w_output)
    part_rows = groups * own_rows // 2
    first_half = fsdp.spread(qkv[:part_rows])
    for step in range(3, ring.steps):
        qkv, first_half, tables, places, w_output = window(
            [token_ring], qkv, first_half, tables, places, w_output
        )
    cos_table, sine_table = tables
    second_half = fsdp.spread(qkv[part_rows:])
    qkv, first_half, second_half, w_output, cotangent_sent = window(
        [token_ring], qkv, first_half, second_half, w_output, cotangent
    )

    cot_ring = Gather(ring, cotangent_sent)
    qkv_parts = fsdp.swapped(
        qkv, [jnp.concatenate(pair, axis=0) for pair in zip(first_half, second_half)]
    )
    gains_qk = sum(
        jnp.sum(
            part.reshape(groups, own_rows, qkv_width + extra)[
                :, :2, qkv_width : qkv_width + head_size
            ].astype(F32),
            axis=0,
        )
        for part in qkv_parts
    )
    projected = project(
        token_ring.pieces, qkv_parts, fsdp.blocks, qkv_width, cos_table, sine_table, gains_qk
    )
    held = lax.ppermute(w_output, ALL, exchange)
    projected, held, qkv_parts = window([cot_ring], projected, held, qkv_parts)
    normed_all, qk_pre, query_seq, key_seq, value_seq = projected
    attended, probs = attend(query_seq, key_seq, value_seq, places, scale_qk, tok_rows)
    held_others = fsdp.spread(held)
    attended, probs, held, held_others, w_up = window(
        [cot_ring], attended, probs, held, held_others, w_up
    )
    up_w = lax.all_gather(w_up, "fsdp", axis=1, tiled=True)
    output_w = lay(fsdp.swapped(held, held_others), fsdp.blocks)
    branch = rows_dot(attended, output_w, 0, tok_rows)
    for step in range(3, ring.steps):
        branch, output_w, gate_w, w_down = window([cot_ring], branch, output_w, gate_w, w_down)
    down_w = lax.all_gather(w_down, "fsdp", axis=2, tiled=True)

    branch_ring = Scatter(ring, lambda spot: (branch[spot], 0), tok_rows, tuple(branch[-2:]))
    (qkv_parts,) = window([branch_ring, cot_ring], qkv_parts)

    def small_arrays(parts):
        small = jnp.stack([part[:, qkv_width:].reshape(groups, -1) for part in parts])
        small = jnp.take(small, fsdp.spots, axis=0)[:, :, 2 * extra :]
        cuts = [own_rows, own_rows * experts_all, tok_rows * top_k]
        ends = [sum(cuts[: i + 1]) for i in range(3)]
        gain_mlp = small[:, :, : ends[0]].reshape(1, model_width).astype(F32)
        router_w = small[:, :, ends[0] : ends[1]].reshape(model_width, experts_all)
        ids_all = parts[0][:, qkv_width:].reshape(groups, -1)[:, 2 * extra :]
        ids_near = jnp.take(ids_all[:, ends[1] : ends[2]], ring.members, axis=0)
        ids_near = ids_near.astype(jnp.int32).reshape(groups, top_k, tok_rows)
        return gain_mlp, router_w, ids_near.transpose(1, 0, 2).reshape(top_k, -1)

    (gain_mlp, router_w, ids_near), qkv_parts, cot_pieces = window(
        [branch_ring], small_arrays(qkv_parts), qkv_parts, cot_ring.pieces
    )
    qkv_w, cot_all = lay(qkv_parts, fsdp.blocks), lay(cot_pieces)
    for step in range(3, ring.steps):
        qkv_w, cot_all = window([branch_ring], qkv_w, cot_all)
    (up_w,) = window([branch_ring], up_w)
    middle, mixer_in = by_rows(
        enter_kernel, branch_ring.landed(), [tokens], [gain_mlp], [F32, BF16]
    )

    def shares(rows_in, ids):
        logits = jnp.dot(rows_in, router_w, preferred_element_type=F32)
        chosen = jnp.sum(
            (ids[:, :, None] == jnp.arange(experts_all, dtype=jnp.int32)).astype(F32), axis=0
        )
        masked = jnp.where(chosen > 0, logits, NEG_LARGE)
        grown = jnp.exp(masked - jnp.max(masked, axis=-1, keepdims=True)) * chosen
        return grown / jnp.sum(grown, axis=-1, keepdims=True)

    def gate_part(rows_in, first):
        last = first + rows_in.shape[0]
        share = lax.dynamic_slice_in_dim(
            shares(rows_in, ids_near[:, first:last]), seat * local_experts, local_experts, 1
        ).T[:, :, None]
        return share, jnp.einsum("td,edf->etf", rows_in, gate_w, preferred_element_type=F32)

    def expert_part(rows_in, first, share, gate_pre):
        last = first + rows_in.shape[0]
        up_pre = jnp.einsum("td,edf->etf", rows_in, up_w, preferred_element_type=F32)
        back = down_back[:, first:last]
        sigmoid = jax.nn.sigmoid(gate_pre)
        silu_gate = gate_pre * sigmoid
        active = silu_gate * up_pre
        grad_share = jnp.sum(active * back, axis=-1)
        active_shared = (active * share).astype(BF16)
        grad_active = back * share
        grad_up_pre = (grad_active * silu_gate).astype(BF16)
        grad_gate_pre = (
            grad_active * up_pre * sigmoid * (1.0 + gate_pre * (1.0 - sigmoid))
        ).astype(BF16)
        return grad_share, active_shared, grad_gate_pre, grad_up_pre

    def entered_part(part):
        entered = jnp.einsum(
            "etf,edf->td", part[2], gate_w, preferred_element_type=F32
        ) + jnp.einsum("etf,edf->td", part[3], up_w, preferred_element_type=F32)
        return entered.astype(BF16)

    cut = ring.steps // 2
    early = (2 * cut + 1) * tok_rows
    mixer_ring = Gather(ring, mixer_in)
    (cot_all,) = window([mixer_ring], cot_all)
    cot_all, down_w = prepare([mixer_ring], cot_all, down_w)
    down_back = jnp.einsum("td,efd->etf", cot_all, down_w, preferred_element_type=F32)
    (down_back,) = window([mixer_ring], down_back)
    for step in range(3, cut + 1):
        window([mixer_ring])
    early_rows = jnp.concatenate(mixer_ring.pieces, axis=0)
    early_share, early_gate = gate_part(early_rows, 0)
    for step in range(cut + 1, ring.steps):
        early_rows, early_share, early_gate = window(
            [mixer_ring], early_rows, early_share, early_gate
        )
    early_part = expert_part(early_rows, 0, early_share, early_gate)
    early_part, early_rows = window([mixer_ring], early_part, early_rows)
    late_rows = jnp.concatenate(mixer_ring.pieces[2 * cut + 1 :], axis=0)
    late_part = expert_part(late_rows, early, *gate_part(late_rows, early))
    late_entered = entered_part(late_part)
    late_entered, late_part, early_part, late_rows, early_rows = together(
        late_entered, late_part, early_part, late_rows, early_rows
    )

    def entered_piece(spot):
        if spot * tok_rows >= early:
            return late_entered, spot - early // tok_rows
        return early_entered[spot], 0

    entered_ring = Scatter(ring, entered_piece, tok_rows)
    grad_share = jnp.concatenate([early_part[0], late_part[0]], axis=1)
    grad_share_own = lax.all_to_all(
        jnp.take(grad_share.reshape(local_experts, groups, tok_rows), ring.spots, axis=1).transpose(
            1, 0, 2
        ),
        "seq",
        split_axis=0,
        concat_axis=0,
        tiled=True,
    )
    early_entered = entered_rows(
        early_part[2], early_part[3], gate_w, up_w, tok_rows
    )
    window([entered_ring])
    early_entered, early_part, late_part, early_rows, late_rows = window(
        [entered_ring], early_entered, early_part, late_part, early_rows, late_rows
    )
    early_part, late_part, early_rows, late_rows = prepare(
        [entered_ring], early_part, late_part, early_rows, late_rows
    )
    (grad_gate,) = row_grads((early_rows, late_rows), (early_part[2], late_part[2]))
    for step in range(3, ring.steps):
        grad_gate, early_part, late_part, early_rows, late_rows, grad_share_own = window(
            [entered_ring], grad_gate, early_part, late_part, early_rows, late_rows, grad_share_own
        )
    grad_gate = lax.psum_scatter(grad_gate, "fsdp", scatter_dimension=1, tiled=True)
    early_part, late_part, early_rows, late_rows, grad_share_own = prepare(
        [entered_ring], early_part, late_part, early_rows, late_rows, grad_share_own
    )
    grad_share_own = grad_share_own.reshape(experts_all, tok_rows).T
    share_own = shares(mixer_in, expert_ids.T)
    grad_logits = (
        share_own
        * (grad_share_own - jnp.sum(share_own * grad_share_own, axis=-1, keepdims=True))
    ).astype(BF16)
    (grad_up,) = row_grads((early_rows, late_rows), (early_part[3], late_part[3]))
    grad_up, grad_logits, early_active, late_active = window(
        [entered_ring], grad_up, grad_logits, early_part[1], late_part[1]
    )
    grad_up = lax.psum_scatter(grad_up, "fsdp", scatter_dimension=1, tiled=True)
    grad_middle, grad_branch, grad_gain_m = by_rows(
        mixer_back_kernel,
        entered_ring.landed(),
        [middle, cotangent],
        [grad_logits, router_w, gain_mlp],
        [F32, BF16],
        [(1, model_width)],
    )

    grads_ring = Gather(ring, grad_branch)
    early_active, late_active = prepare([grads_ring], early_active, late_active)
    produced = [
        jnp.einsum("etf,efd->td", active, down_w, preferred_element_type=F32).astype(BF16)
        for active in (early_active, late_active)
    ]
    produced, early_active, late_active = window(
        [grads_ring], produced, early_active, late_active
    )
    early_active, late_active = prepare([grads_ring], early_active, late_active)
    down_parts = down_grads((early_active, late_active), cot_all, fsdp.targets)
    (down_parts,) = window([grads_ring], down_parts)
    paired_down = fsdp.pair(down_parts)
    for step in range(3, cut + 1):
        window([grads_ring])

    def two_parts(parts):
        def piece(spot):
            if spot * tok_rows >= early:
                return parts[1], spot - early // tok_rows
            return parts[0], spot

        return piece

    def back(pieces, offset, before):
        return attend_back(
            pieces,
            offset,
            before,
            output_w,
            probs,
            query_seq,
            key_seq,
            value_seq,
            qk_pre,
            cos_table,
            sine_table,
            gains_qk,
            scale_qk,
        )

    grads = back(grads_ring.pieces, 0, None)
    grad_small = dot(mixer_in, jnp.pad(grad_logits, ((0, 0), (0, head_size - experts_all))), 0, 0)
    for step in range(cut + 1, ring.steps):
        grad_small, paired_down = window([grads_ring], grad_small, paired_down)
    layer_ring = Scatter(ring, two_parts(produced), tok_rows)
    (grads,) = window([grads_ring, layer_ring], grads)
    grads = back(grads_ring.pieces[2 * cut + 1 :], 2 * cut + 1, grads)
    (grads,) = window([layer_ring], grads)

    grads, grad_small, branch_pieces = prepare(
        [layer_ring], grads, grad_small, grads_ring.pieces
    )
    grad_qkv = grads[0]
    grad_parts = project_back(
        normed_all, grad_qkv, grad_small, grad_gain_m, experts_all, grads[1], own_rows, fsdp.targets
    )
    output_parts = output_back(attended, branch_pieces, fsdp.targets)
    for step in range(3, ring.steps):
        grad_parts, grad_qkv, output_parts = window(
            [layer_ring], grad_parts, grad_qkv, output_parts
        )
    paired = fsdp.pair(grad_parts)
    sent = fsdp.send(paired)
    paired_output = fsdp.pair(output_parts)
    grad_hidden = rows_dot(grad_qkv, qkv_w, 1, tok_rows)
    grad_hidden, paired, sent, paired_output = window(
        [layer_ring], grad_hidden, paired, sent, paired_output
    )
    (produced, spot), left, right = layer_ring.landed()
    layer_out = (
        middle
        + lax.slice_in_dim(produced, 0, tok_rows, axis=0).astype(F32)
        + left.astype(F32)
        + right.astype(F32)
    ).astype(BF16)

    hidden_ring = Scatter(
        ring, lambda spot: (grad_hidden[spot], 0), tok_rows, tuple(grad_hidden[-2:])
    )
    total = paired[0].astype(F32) + sum(part.astype(F32) for part in sent)
    grad_qkv_w = lax.all_to_all(
        total.astype(BF16).reshape(groups, own_rows, qkv_width + head_size),
        "seq",
        split_axis=0,
        concat_axis=0,
        tiled=True,
    )
    sent_output = fsdp.send(paired_output)
    paired_output, sent_output, paired_down = window(
        [hidden_ring], paired_output, sent_output, paired_down
    )
    paired_output, sent_output, paired_down = prepare(
        [hidden_ring], paired_output, sent_output, paired_down
    )
    total = paired_output[0].astype(F32) + sum(part.astype(F32) for part in sent_output)
    grad_output_w = lax.ppermute(total.astype(BF16), ALL, exchange)
    sent_down = fsdp.send(paired_down)
    grad_qkv_w, grad_output_w, grad_gate, grad_up = window(
        [hidden_ring], grad_qkv_w, grad_output_w, grad_gate, grad_up
    )

    def corner(array):
        return lax.slice(array, (0,) * array.ndim, (1,) * (array.ndim - 2) + (8, 128))

    grad_gate, grad_up, grad_output_w = prepare([hidden_ring], grad_gate, grad_up, grad_output_w)
    grad_gate, grad_up = grad_gate.astype(F32), grad_up.astype(F32)
    grad_output_w = grad_output_w.astype(F32)
    corners = [corner(array) for array in (grad_gate, grad_up, grad_output_w, layer_out)]
    for step in range(3, ring.steps):
        paired_down, corners = window([hidden_ring], paired_down, corners)
    (paired_down,) = prepare([hidden_ring], paired_down)
    grad_down = paired_down[0].astype(F32) + sum(part.astype(F32) for part in sent_down)
    window([hidden_ring], [corner(grad_down)])
    (grad_tokens,) = by_rows(
        tokens_back_kernel, hidden_ring.landed(), [tokens, grad_middle], [], [BF16]
    )
    grad_query_w, grad_key_w, grad_value_w, grad_gain_a, small = weights_back(
        grad_qkv_w,
        weights_own,
        attn_gain.astype(F32)[:, None],
        held_groups,
        kv_heads,
        head_size,
    )
    gains = small[:4, head_size // 2 :].reshape(2, head_size)
    cut = query_gain.shape[0]
    gains = lax.dynamic_slice(gains, (0, me * cut), (2, cut))
    return (
        layer_out,
        grad_tokens,
        grad_gain_a[:, 0],
        grad_query_w,
        grad_key_w,
        grad_value_w,
        gains[0],
        gains[1],
        grad_output_w,
        small[:, experts_all],
        small[:, :experts_all],
        grad_gate,
        grad_up,
        grad_down,
    )


def solution(mesh):
    rows = P(("fsdp", "seq"), None)
    line = P(("fsdp", "seq"))
    wide = P("seq", "fsdp", None)
    deep = P("seq", None, "fsdp")
    in_specs = (
        rows, rows, rows, line, rows, rows, rows, line, line, rows, line, rows, wide, wide, deep,
    )
    out_specs = (
        rows, rows, line, rows, rows, rows, line, line, rows, line, rows, wide, wide, deep,
    )
    return jax.shard_map(
        on_device, mesh=mesh, in_specs=in_specs, out_specs=out_specs, check_vma=False
    )
```

```python
import math

import jax
import jax.numpy as jnp
import numpy as np
from jax import lax
from jax.experimental import pallas as pl
from jax.experimental.pallas import tpu as pltpu
from jax.sharding import PartitionSpec as P

NORM_EPS = 1e-06
ROPE_BASE = 1000000.0
NEG_LARGE = -1e30
F32 = jnp.float32
BF16 = jnp.bfloat16
ALL = ("fsdp", "seq")
VMEM_LIMIT = 40 * 1024 * 1024
LARGE_LIMIT = 56 * 1024 * 1024
SMALL_LIMIT = 16 * 1024 * 1024


def dot(left, right, left_dim, right_dim):
    return lax.dot_general(
        left, right, (((left_dim,), (right_dim,)), ((), ())), preferred_element_type=F32
    )


def norm_parts(values):
    row_scale = lax.rsqrt(jnp.mean(values * values, axis=-1, keepdims=True) + NORM_EPS)
    return (values * row_scale, row_scale)


def norm_back(grad_normed, normed, row_scale):
    return row_scale * (
        grad_normed - normed * jnp.mean(grad_normed * normed, axis=-1, keepdims=True)
    )


def rotary_tables(positions, head_size):
    half_size = head_size // 2
    frequency = jnp.exp(
        jnp.arange(half_size, dtype=F32) * (-2.0 * math.log(ROPE_BASE) / head_size)
    )
    angles = positions[:, None] * frequency[None, :]
    cosine, sine = jnp.cos(angles), jnp.sin(angles)
    return jnp.concatenate([cosine, cosine], axis=1), jnp.concatenate([-sine, sine], axis=1)


def swap_halves(values):
    return pltpu.roll(values, values.shape[-1] // 2, 1)


def params(limit=VMEM_LIMIT):
    return pltpu.CompilerParams(vmem_limit_bytes=limit)


def take_piece(step, pieces, halved, store):
    last = len(pieces) - (2 if halved else 0)
    for i in range(last):

        @pl.when(step == i)
        def _(i=i):
            store(0, pieces[i][...])

    if halved:

        @pl.when(step == last)
        def _():
            half = pieces[last].shape[0]
            store(0, pieces[last][...])
            store(half, pieces[last + 1][...])


def lay_kernel(count, halved, order_ref, *refs):
    def store(first, rows):
        refs[-1][first : first + rows.shape[0]] = rows

    take_piece(pl.program_id(0), refs[:count], halved, store)


def lay(pieces, order=None):
    halved = order is None
    members = len(pieces) - (1 if halved else 0)
    if halved:
        order = jnp.arange(members, dtype=jnp.int32)
    rows, cols = pieces[0].shape
    return pl.pallas_call(
        lambda *refs: lay_kernel(len(pieces), halved, *refs),
        grid_spec=pltpu.PrefetchScalarGridSpec(
            num_scalar_prefetch=1,
            grid=(members,),
            in_specs=[pl.BlockSpec(piece.shape, lambda i, order: (0, 0)) for piece in pieces],
            out_specs=pl.BlockSpec((rows, cols), lambda i, order: (order[i], 0)),
        ),
        out_shape=jax.ShapeDtypeStruct((members * rows, cols), pieces[0].dtype),
        compiler_params=params(),
        cost_estimate=pl.CostEstimate(
            flops=0, bytes_accessed=4 * members * rows * cols, transcendentals=0
        ),
    )(order, *pieces)


def project_kernel(heads, parts, count, order_ref, *refs):
    pieces, refs = refs[:count], refs[count:]
    weights, refs = refs[:parts], refs[parts:]
    cos_ref, sin_ref, gain_ref, n_ref, pre_ref, q_ref, k_ref, v_ref = refs
    size = cos_ref.shape[1]

    def store(first, rows):
        n_ref[first : first + rows.shape[0]] = norm_parts(rows.astype(F32))[0].astype(BF16)

    take_piece(pl.program_id(0), pieces, True, store)
    depth = weights[0].shape[0]
    projected = 0.0
    for part, w_ref in enumerate(weights):
        columns = pl.ds(pl.multiple_of(order_ref[part] * depth, depth), depth)
        projected += jnp.dot(n_ref[:, columns], w_ref[...], preferred_element_type=F32)
    pre_ref[...] = projected[:, : (heads + 1) * size]
    for head in range(heads + 1):
        row = 0 if head < heads else 1
        scaled = norm_parts(projected[:, head * size : (head + 1) * size])[0] * gain_ref[row : row + 1]
        turned = (scaled * cos_ref[...] + swap_halves(scaled) * sin_ref[...]).astype(BF16)
        if head < heads:
            q_ref[:, head * size : (head + 1) * size] = turned
        else:
            k_ref[...] = turned
    v_ref[...] = projected[:, (heads + 1) * size :].astype(BF16)


def project(pieces, weights, order, width, cos_table, sine_table, gains):
    block, depth = pieces[0].shape
    rows = block * (len(pieces) - 1)
    size = cos_table.shape[1]
    heads = width // size - 2
    spec = lambda cols: pl.BlockSpec((block, cols), lambda i, order: (i, 0))
    whole = lambda shape: pl.BlockSpec(shape, lambda i, order: (0, 0))
    return pl.pallas_call(
        lambda *refs: project_kernel(heads, len(weights), len(pieces), *refs),
        grid_spec=pltpu.PrefetchScalarGridSpec(
            num_scalar_prefetch=1,
            grid=(rows // block,),
            in_specs=[whole(piece.shape) for piece in pieces]
            + [whole((part.shape[0], width)) for part in weights]
            + [spec(size), spec(size), whole(gains.shape)],
            out_specs=[
                spec(depth), spec((heads + 1) * size), spec(heads * size), spec(size), spec(size),
            ],
        ),
        out_shape=[
            jax.ShapeDtypeStruct((rows, depth), BF16),
            jax.ShapeDtypeStruct((rows, (heads + 1) * size), F32),
            jax.ShapeDtypeStruct((rows, heads * size), BF16),
            jax.ShapeDtypeStruct((rows, size), BF16),
            jax.ShapeDtypeStruct((rows, size), BF16),
        ],
        compiler_params=params(LARGE_LIMIT),
        cost_estimate=pl.CostEstimate(
            flops=2 * rows * depth * width, bytes_accessed=16 << 20, transcendentals=0
        ),
    )(order, *pieces, *weights, cos_table, sine_table, gains)


def fetch(arrays, spots, buffers, sems):
    copies = [
        pltpu.make_async_copy(
            array.at[pl.ds(spot * buffer.shape[0], buffer.shape[0])], buffer, sems.at[i]
        )
        for i, (array, spot, buffer) in enumerate(zip(arrays, spots, buffers))
    ]
    for copy in copies:
        copy.start()
    for copy in copies:
        copy.wait()


def ring_add_kernel(spots, up_hbm, down_hbm, left_ref, right_ref, up_ref, down_ref, up_buf, down_buf, sems):
    fetch((up_hbm, down_hbm), spots, (up_buf, down_buf), sems)
    rows, half = up_buf.shape[0], left_ref.shape[0]
    if half == rows:
        up_ref[...] = (up_buf[...].astype(F32) + left_ref[...].astype(F32)).astype(BF16)
        down_ref[...] = (down_buf[...].astype(F32) + right_ref[...].astype(F32)).astype(BF16)
        return
    up_ref[:half] = (up_buf[:half].astype(F32) + left_ref[...].astype(F32)).astype(BF16)
    up_ref[half:] = up_buf[half:]
    down_ref[:half] = down_buf[:half]
    down_ref[half:] = (down_buf[half:].astype(F32) + right_ref[...].astype(F32)).astype(BF16)


HBM = pl.BlockSpec(memory_space=pltpu.HBM)
VMEM = pl.BlockSpec(memory_space=pltpu.VMEM)


def ring_add(mine_up, mine_down, left, right, rows):
    width = left.shape[1]
    return pl.pallas_call(
        lambda *refs: ring_add_kernel((mine_up[1], mine_down[1]), *refs),
        in_specs=[HBM, HBM, VMEM, VMEM],
        out_specs=[VMEM, VMEM],
        out_shape=[jax.ShapeDtypeStruct((rows, width), BF16)] * 2,
        scratch_shapes=[pltpu.VMEM((rows, width), BF16)] * 2 + [pltpu.SemaphoreType.DMA((2,))],
        compiler_params=pltpu.CompilerParams(vmem_limit_bytes=SMALL_LIMIT),
        cost_estimate=pl.CostEstimate(
            flops=2 * rows * width, bytes_accessed=12 * rows * width, transcendentals=0
        ),
    )(mine_up[0], mine_down[0], left, right)


def summed(mine_ref, left_ref, right_ref):
    return mine_ref[...].astype(F32) + left_ref[...].astype(F32) + right_ref[...].astype(F32)


def enter_kernel(mine_ref, left_ref, right_ref, x_ref, gain_ref, middle_ref, mixer_ref):
    middle = x_ref[...].astype(F32) + summed(mine_ref, left_ref, right_ref)
    middle_ref[...] = middle
    mixer_ref[...] = (norm_parts(middle)[0] * gain_ref[...]).astype(BF16)


def mixer_back_kernel(
    mine_ref, left_ref, right_ref, middle_ref, cot_ref, logits_ref, router_ref, gain_ref, *refs
):
    grad_ref, branch_ref, gains_ref = refs
    grad_mixer = summed(mine_ref, left_ref, right_ref) + dot(logits_ref[...], router_ref[...], 1, 1)
    normed, row_scale = norm_parts(middle_ref[...])
    gains_ref[...] = jnp.sum(grad_mixer * normed, axis=0, keepdims=True)
    grad = cot_ref[...].astype(F32) + norm_back(grad_mixer * gain_ref[...], normed, row_scale)
    grad_ref[...] = grad
    branch_ref[...] = grad.astype(BF16)


def tokens_back_kernel(mine_ref, left_ref, right_ref, x_ref, grad_ref, out_ref):
    normed, row_scale = norm_parts(x_ref[...].astype(F32))
    grad = norm_back(summed(mine_ref, left_ref, right_ref), normed, row_scale)
    out_ref[...] = (grad_ref[...] + grad).astype(BF16)


def by_rows(kernel, landed, lines, inputs, outs, sums=()):
    (mine, spot), left, right = landed
    rows, width = left.shape
    count = 1 + len(lines)

    def whole(*refs):
        arrays, refs = refs[:count], refs[count:]
        refs, buffers, sems = refs[: -count - 1], refs[-count - 1 : -1], refs[-1]
        fetch(arrays, (spot,) + (0,) * len(lines), buffers, sems)
        kernel(buffers[0], *refs[:2], *buffers[1:], *refs[2:])

    return pl.pallas_call(
        whole,
        in_specs=[HBM] * count + [VMEM] * (2 + len(inputs)),
        out_specs=[VMEM] * (len(outs) + len(sums)),
        out_shape=[jax.ShapeDtypeStruct((rows, width), kind) for kind in outs]
        + [jax.ShapeDtypeStruct(shape, F32) for shape in sums],
        scratch_shapes=[pltpu.VMEM((rows, array.shape[1]), array.dtype) for array in [mine] + lines]
        + [pltpu.SemaphoreType.DMA((count,))],
        compiler_params=pltpu.CompilerParams(vmem_limit_bytes=SMALL_LIMIT),
        cost_estimate=pl.CostEstimate(
            flops=20 * rows * width, bytes_accessed=16 * rows * width, transcendentals=rows
        ),
    )(mine, *lines, left, right, *inputs)


def weights_back_kernel(held, copies, size, came_ref, own_ref, gain_ref, q_ref, k_ref, v_ref, gains_ref, small_ref):
    groups, rows, _ = came_ref.shape
    width = own_ref.shape[2]
    wide = width - 2 * size
    gains = jnp.zeros((rows, 1), F32)
    small = jnp.zeros(small_ref.shape, F32)
    gain = gain_ref[...]
    seen = set()
    for member, group in enumerate(held):
        came = came_ref[member].astype(F32)
        gains += jnp.sum(
            came[:, :width] * own_ref[member].astype(F32), axis=1, keepdims=True
        )
        small += came[:, width:]
        came = came[:, :width] * gain
        q_ref[:, group * wide : (group + 1) * wide] = came[:, :wide]
        lanes = slice(group // copies * size, (group // copies + 1) * size)
        if group // copies not in seen:
            k_ref[:, lanes] = came[:, wide : wide + size]
            v_ref[:, lanes] = came[:, wide + size :]
        else:
            k_ref[:, lanes] += came[:, wide : wide + size]
            v_ref[:, lanes] += came[:, wide + size :]
        seen.add(group // copies)
    gains_ref[...] = jnp.broadcast_to(gains, gains_ref.shape)
    small_ref[...] = small


def weights_back(came, own, gain, held, kv_heads, size):
    groups, rows, total = came.shape
    width = own.shape[2]
    shape = lambda cols: jax.ShapeDtypeStruct((rows, cols), F32)
    return pl.pallas_call(
        lambda *refs: weights_back_kernel(held, groups // kv_heads, size, *refs),
        out_shape=[
            shape(groups * (width - 2 * size)),
            shape(kv_heads * size),
            shape(kv_heads * size),
            shape(128),
            shape(total - width),
        ],
        compiler_params=params(),
        cost_estimate=pl.CostEstimate(
            flops=4 * groups * rows * width, bytes_accessed=4 << 20, transcendentals=0
        ),
    )(came, own, gain)


def output_back_kernel(count, order_ref, left_ref, *refs):
    pieces, outs, (rows_ref, turned_ref, sum_ref) = refs[:count], refs[count:-3], refs[-3:]

    @pl.when(pl.program_id(0) == 0)
    def _():
        turned_ref[...] = left_ref[...].T

    first = 0
    for piece in pieces:
        rows_ref[first : first + piece.shape[0]] = piece[...]
        first += piece.shape[0]
    sum_ref[...] = jnp.dot(turned_ref[...], rows_ref[...], preferred_element_type=F32)
    for i, out_ref in enumerate(outs):
        rows = out_ref.shape[0]
        first = pl.multiple_of(order_ref[i] * rows, rows)
        out_ref[...] = sum_ref[pl.ds(first, rows), :].astype(BF16)


def output_back(left, pieces, order):
    rows, width = left.shape
    cols = pieces[0].shape[1]
    parts = order.shape[0]
    block = cols // 4
    return pl.pallas_call(
        lambda *refs: output_back_kernel(len(pieces), *refs),
        grid_spec=pltpu.PrefetchScalarGridSpec(
            num_scalar_prefetch=1,
            grid=(4,),
            in_specs=[pl.BlockSpec((rows, width), lambda i, order: (0, 0))]
            + [pl.BlockSpec((piece.shape[0], block), lambda i, order: (0, i)) for piece in pieces],
            out_specs=[pl.BlockSpec((width // parts, block), lambda i, order: (0, i))] * parts,
            scratch_shapes=[
                pltpu.VMEM((rows, block), BF16),
                pltpu.VMEM((width, rows), BF16),
                pltpu.VMEM((width, block), F32),
            ],
        ),
        out_shape=[jax.ShapeDtypeStruct((width // parts, cols), BF16)] * parts,
        compiler_params=params(),
        cost_estimate=pl.CostEstimate(
            flops=2 * rows * width * cols, bytes_accessed=8 << 20, transcendentals=0
        ),
    )(order, left, *pieces)


def project_back_kernel(
    own_rows, place, order_ref, normed_ref, grad_ref, small_ref, line_ref, gains_ref, *outs
):
    width = grad_ref.shape[1]
    part = dot(normed_ref[...], grad_ref[...], 0, 0).astype(BF16)
    small = small_ref[...]
    size = small.shape[1]
    row = lax.broadcasted_iota(jnp.int32, small.shape, 0) % own_rows
    lane = lax.broadcasted_iota(jnp.int32, small.shape, 1)
    small = jnp.where(lane == place, jnp.broadcast_to(line_ref[...], (size, small.shape[0])).T, small)
    upper = lane >= size // 2
    for i in range(2):
        gain = gains_ref[i : i + 1]
        for half, line in enumerate((pltpu.roll(gain, size // 2, 1), gain)):
            small = jnp.where(upper & (row == 2 * i + half), line, small)
    small = small.astype(BF16)
    for i, out_ref in enumerate(outs):

        @pl.when(pl.program_id(0) == i)
        def _(out_ref=out_ref):
            out_ref[:, :width] = part
            out_ref[:, width:] = small


def project_back(normed, grad, small, line, place, gains, own_rows, order):
    rows, depth = normed.shape
    width, extra = grad.shape[1], small.shape[1]
    parts = order.shape[0]
    block = depth // parts
    whole = lambda shape: pl.BlockSpec(shape, lambda i, order: (0, 0))
    return pl.pallas_call(
        lambda *refs: project_back_kernel(own_rows, place, *refs),
        grid_spec=pltpu.PrefetchScalarGridSpec(
            num_scalar_prefetch=1,
            grid=(parts,),
            in_specs=[
                pl.BlockSpec((rows, block), lambda i, order: (0, order[i])),
                whole(grad.shape),
                pl.BlockSpec((block, extra), lambda i, order: (order[i], 0)),
                pl.BlockSpec((1, block), lambda i, order: (0, order[i])),
                whole(gains.shape),
            ],
            out_specs=[whole((block, width + extra))] * parts,
        ),
        out_shape=[jax.ShapeDtypeStruct((block, width + extra), BF16)] * parts,
        compiler_params=params(),
        cost_estimate=pl.CostEstimate(
            flops=2 * rows * depth * width, bytes_accessed=12 << 20, transcendentals=0
        ),
    )(order, normed, grad, small, line, gains)


def row_grads_kernel(first_ref, second_ref, *refs):
    count = len(refs) // 3
    grads, outs = refs[: 2 * count], refs[2 * count :]
    first, second = first_ref[...].T, second_ref[...].T
    for i, out_ref in enumerate(outs):
        for expert in range(out_ref.shape[0]):
            part = dot(first, grads[2 * i][expert], 1, 0)
            part += dot(second, grads[2 * i + 1][expert], 1, 0)
            out_ref[expert] = part.astype(BF16)


def row_grads(rows, *grads):
    experts, _, ff = grads[0][0].shape
    depth = rows[0].shape[1]
    block = depth // 8
    return pl.pallas_call(
        row_grads_kernel,
        grid=(8,),
        in_specs=[pl.BlockSpec((part.shape[0], block), lambda i: (0, i)) for part in rows]
        + [pl.BlockSpec(part.shape, lambda i: (0, 0, 0)) for pair in grads for part in pair],
        out_specs=[pl.BlockSpec((experts, block, ff), lambda i: (0, i, 0))] * len(grads),
        out_shape=[jax.ShapeDtypeStruct((experts, depth, ff), BF16)] * len(grads),
        compiler_params=params(LARGE_LIMIT),
        cost_estimate=pl.CostEstimate(
            flops=2 * len(grads) * experts * sum(part.shape[0] for part in rows) * ff * depth,
            bytes_accessed=24 << 20,
            transcendentals=0,
        ),
    )(*rows, *(part for pair in grads for part in pair))


def down_grads_kernel(order_ref, first_ref, second_ref, cot_ref, *refs):
    outs, turned_ref = refs[:-1], refs[-1]
    expert, step = pl.program_id(0), pl.program_id(1)
    cut = first_ref.shape[1]

    @pl.when(step == 0)
    def _():
        turned_ref[:, :cut] = first_ref[0].T
        turned_ref[:, cut:] = second_ref[0].T

    part = jnp.dot(turned_ref[...], cot_ref[...], preferred_element_type=F32).astype(BF16)
    for i, out_ref in enumerate(outs):

        @pl.when(step == i)
        def _(out_ref=out_ref):
            out_ref[expert] = part


def down_grads(active, cot, order):
    experts, _, ff = active[0].shape
    rows, depth = cot.shape
    parts = order.shape[0]
    block = depth // parts
    return pl.pallas_call(
        down_grads_kernel,
        grid_spec=pltpu.PrefetchScalarGridSpec(
            num_scalar_prefetch=1,
            grid=(experts, parts),
            in_specs=[
                pl.BlockSpec((1,) + part.shape[1:], lambda e, i, order: (e, 0, 0))
                for part in active
            ]
            + [pl.BlockSpec((rows, block), lambda e, i, order: (0, order[i]))],
            out_specs=[pl.BlockSpec((experts, ff, block), lambda e, i, order: (0, 0, 0))] * parts,
            scratch_shapes=[pltpu.VMEM((ff, rows), BF16)],
        ),
        out_shape=[jax.ShapeDtypeStruct((experts, ff, block), BF16)] * parts,
        compiler_params=params(),
        cost_estimate=pl.CostEstimate(
            flops=2 * experts * rows * ff * depth, bytes_accessed=16 << 20, transcendentals=0
        ),
    )(order, *active, cot)


def split_rows(result, outs):
    first = 0
    for out_ref in outs:
        out_ref[...] = result[first : first + out_ref.shape[0]].astype(BF16)
        first += out_ref.shape[0]


def split_shapes(rows, block, cols, halved):
    heights = [block] * (rows // block)
    if halved:
        heights[-1:] = [block // 2, block // 2]
    return [jax.ShapeDtypeStruct((height, cols), BF16) for height in heights]


def rows_dot(left, right, right_dim, block):
    rows, depth = left.shape
    cols = right.shape[1 - right_dim]
    each = cols // 4
    shapes = split_shapes(rows, block, cols, True)
    if right_dim:
        spec = pl.BlockSpec((each, depth), lambda i: (i, 0))
    else:
        spec = pl.BlockSpec((depth, each), lambda i: (0, i))
    return pl.pallas_call(
        lambda left_ref, right_ref, *outs: split_rows(
            dot(left_ref[...], right_ref[...], 1, right_dim), outs
        ),
        grid=(4,),
        in_specs=[pl.BlockSpec((rows, depth), lambda i: (0, 0)), spec],
        out_specs=[pl.BlockSpec((shape.shape[0], each), lambda i: (0, i)) for shape in shapes],
        out_shape=shapes,
        compiler_params=params(),
        cost_estimate=pl.CostEstimate(
            flops=2 * rows * depth * cols, bytes_accessed=8 << 20, transcendentals=0
        ),
    )(left, right)


def entered_kernel(first_ref, second_ref, first_w_ref, second_w_ref, *outs):
    total = 0.0
    for expert in range(first_ref.shape[0]):
        total += dot(first_ref[expert], first_w_ref[expert], 1, 1)
        total += dot(second_ref[expert], second_w_ref[expert], 1, 1)
    split_rows(total, outs)


def entered_rows(first, second, first_w, second_w, block):
    experts, rows, ff = first.shape
    depth = first_w.shape[1]
    each = depth // 8
    whole = pl.BlockSpec(first.shape, lambda i: (0, 0, 0))
    weight = pl.BlockSpec((experts, each, ff), lambda i: (0, i, 0))
    shapes = split_shapes(rows, block, depth, False)
    return pl.pallas_call(
        entered_kernel,
        grid=(8,),
        in_specs=[whole, whole, weight, weight],
        out_specs=[pl.BlockSpec((block, each), lambda i: (0, i))] * len(shapes),
        out_shape=shapes,
        compiler_params=params(LARGE_LIMIT),
        cost_estimate=pl.CostEstimate(
            flops=4 * experts * rows * ff * depth, bytes_accessed=20 << 20, transcendentals=0
        ),
    )(first, second, first_w, second_w)


def stack_heads(array, size):
    return jnp.concatenate(
        [array[:, i * size : (i + 1) * size] for i in range(array.shape[1] // size)], axis=0
    )


def attend_kernel(scale, q_ref, k_ref, v_ref, at_q_ref, at_k_ref, out_ref, p_ref):
    rows, size = q_ref.shape[0], k_ref.shape[1]
    heads = q_ref.shape[1] // size
    scores = dot(k_ref[...], stack_heads(q_ref[...], size), 1, 1) * scale
    at_q = jnp.concatenate([at_q_ref[...]] * heads, axis=1)
    scores = jnp.where(at_k_ref[...] <= at_q, scores, NEG_LARGE)
    grown = jnp.exp(scores - jnp.max(scores, axis=0, keepdims=True))
    probs = (grown * (1.0 / jnp.sum(grown, axis=0, keepdims=True))).astype(BF16)
    p_ref[...] = probs
    output = dot(v_ref[...].T, probs, 1, 0).T.astype(BF16)
    for head in range(heads):
        out_ref[:, head * size : (head + 1) * size] = output[head * rows : (head + 1) * rows]


def attend(query, key, value, places, scale, block):
    rows, width = query.shape
    size = key.shape[1]
    heads = width // size
    whole = lambda shape: pl.BlockSpec(shape, lambda i: (0, 0))
    return pl.pallas_call(
        lambda *refs: attend_kernel(scale, *refs),
        grid=(rows // block,),
        in_specs=[
            pl.BlockSpec((block, width), lambda i: (i, 0)),
            whole((rows, size)),
            whole((rows, size)),
            pl.BlockSpec((1, block), lambda i: (0, i)),
            whole((rows, 1)),
        ],
        out_specs=[
            pl.BlockSpec((block, width), lambda i: (i, 0)),
            pl.BlockSpec((rows, heads * block), lambda i: (0, i)),
        ],
        out_shape=[
            jax.ShapeDtypeStruct((rows, width), BF16),
            jax.ShapeDtypeStruct((rows, heads * rows), BF16),
        ],
        compiler_params=params(LARGE_LIMIT),
        cost_estimate=pl.CostEstimate(
            flops=4 * heads * rows * rows * size,
            bytes_accessed=12 << 20,
            transcendentals=heads * rows * rows,
        ),
    )(query, key, value, places[None, :], places[:, None])


def head_back(grad_turned, pre, gain, cosine, sine):
    grad = grad_turned * cosine - swap_halves(grad_turned) * sine
    normed, row_scale = norm_parts(pre)
    return (
        jnp.sum(grad * normed, axis=0, keepdims=True),
        norm_back(grad * gain, normed, row_scale).astype(BF16),
    )


def attend_back_kernel(scale, count, first, last, offset, *refs):
    pieces, refs = refs[:count], refs[count:]
    w_ref, p_ref, q_ref, k_ref, v_ref, pre_ref, cos_ref, sin_ref, gain_ref = refs[:9]
    refs = refs[9:]
    before, refs = (() if first else refs[:4]), (refs if first else refs[4:])
    out_ref, gains_ref, dk_ref, dv_ref, rows_ref = refs
    step = pl.program_id(0)
    rows, size = q_ref.shape[0], k_ref.shape[1]
    heads = q_ref.shape[1] // size

    def store(first, rows):
        rows_ref[first : first + rows.shape[0]] = rows

    take_piece(step, pieces, last, store)

    @pl.when(step == 0)
    def _():
        if first:
            dk_ref[...] = jnp.zeros_like(dk_ref)
            dv_ref[...] = jnp.zeros_like(dv_ref)
            gains_ref[...] = jnp.zeros_like(gains_ref)
        else:
            for now_ref, before_ref in zip((out_ref, gains_ref, dk_ref, dv_ref), before):
                now_ref[...] = before_ref[...]

    probs = p_ref[...]
    grads = stack_heads(dot(rows_ref[...], w_ref[...], 1, 1).astype(BF16), size)
    dv_ref[...] += dot(probs, grads, 1, 0)
    grad_probs = dot(v_ref[...], grads, 1, 1)
    probs = probs.astype(F32)
    grad_scores = (
        probs * (grad_probs - jnp.sum(probs * grad_probs, axis=0, keepdims=True))
    ).astype(BF16)
    dk_ref[...] += dot(grad_scores, stack_heads(q_ref[...], size), 1, 0)
    grad_query = dot(k_ref[...].T, grad_scores, 1, 0).T * scale
    start = pl.multiple_of((step + offset) * rows, rows)
    here = pl.ds(start, rows)
    cosine, sine = cos_ref[here, :], sin_ref[here, :]
    for head in range(heads):
        lanes = slice(head * size, (head + 1) * size)
        gain_part, part = head_back(
            grad_query[head * rows : (head + 1) * rows],
            pre_ref[here, lanes],
            gain_ref[0:1],
            cosine,
            sine,
        )
        gains_ref[0:1] += gain_part
        out_ref[here, lanes] = part

    if last:

        @pl.when(step == pl.num_programs(0) - 1)
        def _():
            gain_part, part = head_back(
                dk_ref[...] * scale,
                pre_ref[:, heads * size : (heads + 1) * size],
                gain_ref[1:2],
                cos_ref[...],
                sin_ref[...],
            )
            gains_ref[1:2] = gain_part
            out_ref[:, heads * size : (heads + 1) * size] = part
            out_ref[:, (heads + 1) * size :] = dv_ref[...].astype(BF16)


def attend_back(pieces, offset, before, weights, probs, query, key, value, pre, cos_table, sine_table, gains, scale):
    rows, width = query.shape
    size = key.shape[1]
    heads = width // size
    block, depth = pieces[0].shape
    first, last = before is None, before is not None
    steps = len(pieces) - (1 if last else 0)
    whole = lambda shape: pl.BlockSpec(shape, lambda i: (0, 0))
    shapes = [
        jax.ShapeDtypeStruct((rows, (heads + 2) * size), BF16),
        jax.ShapeDtypeStruct((8, size), F32),
        jax.ShapeDtypeStruct((rows, size), F32),
        jax.ShapeDtypeStruct((rows, size), F32),
    ]
    outs = [whole(shape.shape) for shape in shapes]
    return pl.pallas_call(
        lambda *refs: attend_back_kernel(scale, len(pieces), first, last, offset, *refs),
        grid=(steps,),
        in_specs=[whole(piece.shape) for piece in pieces]
        + [
            whole(weights.shape),
            pl.BlockSpec((rows, heads * block), lambda i: (0, i + offset)),
            pl.BlockSpec((block, width), lambda i: (i + offset, 0)),
            whole((rows, size)),
            whole((rows, size)),
            whole((rows, (heads + 1) * size)),
            whole((rows, size)),
            whole((rows, size)),
            whole(gains.shape),
        ]
        + ([] if first else outs),
        out_specs=outs,
        out_shape=shapes,
        scratch_shapes=[pltpu.VMEM((block, depth), BF16)],
        compiler_params=params(),
        cost_estimate=pl.CostEstimate(
            flops=(8 * heads * rows * size + 2 * depth * width) * steps * block,
            bytes_accessed=(3 << 20) * steps,
            transcendentals=0,
        ),
    )(*pieces, weights, probs, query, key, value, pre, cos_table, sine_table, gains, *(before or ()))


def after(value, *others):
    return lax.optimization_barrier((value, *others))[0]


def ring_order(size):
    if size % 4 or size < 8:
        return list(range(size))
    wide = size // 4
    walk = [(0, y) for y in range(wide)]
    for z in range(1, 4):
        walk += [(z, y) for y in (range(wide - 1, 0, -1) if z % 2 else range(1, wide))]
    walk += [(z, 0) for z in (3, 2, 1)]
    return [z * wide + y for z, y in walk]


def together(*values):
    return lax.optimization_barrier(values)


class Ring:
    def __init__(self, size):
        self.size = size
        self.steps = size // 2
        order = ring_order(size)
        self.up = [(order[i], order[(i + 1) % size]) for i in range(size)]
        self.down = [(order[i], order[(i - 1) % size]) for i in range(size)]
        self.offsets = [0]
        for step in range(1, self.steps):
            self.offsets += [-step, step]
        self.offsets += [self.steps]
        near = np.zeros((size, size), np.int32)
        for i, member in enumerate(order):
            near[member] = [order[(i + offset) % size] for offset in self.offsets]
        seat = lax.axis_index("seq")
        self.members = jnp.asarray(near)[seat]
        self.spots = jnp.asarray(np.argsort(near, axis=1).astype(np.int32))[seat]

    def swap(self, up, down):
        return lax.ppermute(up, "seq", self.up), lax.ppermute(down, "seq", self.down)

    def spot(self, offset):
        return self.offsets.index(offset)


class Gather:
    def __init__(self, ring, block):
        self.ring, self.step, self.pieces = ring, 0, [block]
        self.left = self.right = block
        self.ready = None

    def sends(self):
        if self.step + 1 < self.ring.steps:
            return self.left, self.right
        half = self.left.shape[0] // 2
        return self.left[:half], self.right[half:]

    def start(self):
        ready = self.ready or self.sends()
        self.step += 1
        self.ready = None
        return self.ring.swap(*ready)

    def end(self, left, right):
        self.left, self.right = left, right
        self.pieces += [left, right]


class Scatter:
    def __init__(self, ring, piece, rows, far=None):
        self.ring, self.step, self.piece, self.rows, self.far = ring, 0, piece, rows, far
        self.left = self.right = self.ready = None

    def sends(self):
        ring, rows = self.ring, self.rows
        if self.step == 0 and self.far:
            return self.far
        if self.step == 0:
            whole, spot = self.piece(ring.spot(ring.steps))
            start, middle, end = spot * rows, spot * rows + rows // 2, (spot + 1) * rows
            return (
                lax.slice_in_dim(whole, start, middle, axis=0),
                lax.slice_in_dim(whole, middle, end, axis=0),
            )
        place = ring.steps - self.step
        mine_up, mine_down = self.piece(ring.spot(place)), self.piece(ring.spot(-place))
        return ring_add(mine_up, mine_down, self.left, self.right, rows)

    def start(self):
        ready = self.ready or self.sends()
        self.step += 1
        self.ready = None
        return self.ring.swap(*ready)

    def end(self, left, right):
        self.left, self.right = left, right

    def landed(self):
        return self.piece(0), self.left, self.right


def prepare(rings, *values):
    ready, values = together([ring.sends() for ring in rings], values)
    for ring, sends in zip(rings, ready):
        ring.ready = tuple(sends)
    return values


def window(rings, *values):
    moved = [ring.start() for ring in rings]
    moved, values = together(moved, values)
    for ring, (left, right) in zip(rings, moved):
        ring.end(left, right)
    return values


class Fsdp:
    def __init__(self, size):
        self.size = size
        self.across = size // 2

        def blocks(way):
            return np.asarray(
                [
                    [
                        (i // 2 + way * step) % self.across * 2 + (i % 2 ^ flip)
                        for step in range(self.across)
                        for flip in (0, 1)
                    ]
                    for i in range(size)
                ],
                np.int32,
            )

        index = lax.axis_index("fsdp")
        self.blocks = jnp.asarray(blocks(-1))[index]
        self.targets = jnp.asarray(blocks(1))[index]
        self.spots = jnp.asarray(np.argsort(blocks(-1), axis=1).astype(np.int32))[index]

    def swap(self, array):
        return lax.ppermute(array, "fsdp", [(i, i ^ 1) for i in range(self.size)])

    def shift(self, array, step):
        perm = [
            (x * 2 + c, (x + step) % self.across * 2 + c)
            for x in range(self.across)
            for c in (0, 1)
        ]
        return lax.ppermute(array, "fsdp", perm)

    def spread(self, block):
        return [self.shift(block, step) for step in range(1, self.across)]

    def swapped(self, block, others):
        return [part for mine in [block] + others for part in (mine, self.swap(mine))]

    def pair(self, parts):
        return [
            (parts[i].astype(F32) + self.swap(parts[i + 1]).astype(F32)).astype(BF16)
            for i in range(0, self.size, 2)
        ]

    def send(self, paired):
        return [self.shift(part, step) for step, part in enumerate(paired) if step]


def on_device(
    tokens,
    cotangent,
    expert_ids,
    attn_gain,
    w_query,
    w_key,
    w_value,
    query_gain,
    key_gain,
    w_output,
    mlp_gain,
    w_router,
    w_gate,
    w_up,
    w_down,
):
    groups = lax.axis_size("seq")
    splits = lax.axis_size("fsdp")
    counts = groups * splits
    ring, fsdp = Ring(groups), Fsdp(splits)
    seat = lax.axis_index("seq")
    me = lax.axis_index(ALL)
    tok_rows, model_width = tokens.shape
    top_k = expert_ids.shape[1]
    own_rows = w_query.shape[0]
    head_size = query_gain.shape[0] * counts
    heads_all = w_query.shape[1] // head_size
    kv_heads = w_key.shape[1] // head_size
    head_local = heads_all // groups
    copies = groups // kv_heads
    query_width = head_local * head_size
    qkv_width = query_width + 2 * head_size
    experts_all = w_router.shape[1]
    local_experts, _, ff = w_gate.shape
    seq_rows = tok_rows * groups
    scale_qk = 1.0 / math.sqrt(head_size)

    held_groups = [seat % splits * (groups // splits) + seat // splits for seat in range(groups)]
    exchange = [
        (j * groups + part * splits + i, i * groups + part * splits + j)
        for j in range(splits)
        for part in range(groups // splits)
        for i in range(splits)
    ]

    def by_member(weights, group_of):
        width = weights.shape[1] // (max(group_of) + 1)
        return [weights[:, group * width : (group + 1) * width] for group in group_of]

    kv_of = [group // copies for group in held_groups]
    weights_own = jnp.stack(
        [
            jnp.concatenate(parts, axis=1)
            for parts in zip(
                by_member(w_query, held_groups), by_member(w_key, kv_of), by_member(w_value, kv_of)
            )
        ]
    )
    scaled = (weights_own.astype(F32) * attn_gain.astype(F32)[None, :, None]).astype(BF16)

    def placed(gain):
        return lax.dynamic_update_slice(
            jnp.zeros((head_size,), BF16), gain, (me * gain.shape[0],)
        )

    others = jnp.concatenate(
        [mlp_gain, w_router.reshape(-1), expert_ids.T.reshape(-1).astype(BF16)]
    )
    extra = -(-(others.shape[0] + 2 * head_size) // (own_rows * head_size)) * head_size
    spread = jnp.zeros((2, extra), BF16).at[0, :head_size].set(placed(query_gain))
    spread = spread.at[1, :head_size].set(placed(key_gain))
    spare = (own_rows - 2) * extra - others.shape[0]
    others = jnp.pad(others, (0, spare)).reshape(own_rows - 2, extra)
    small = jnp.concatenate([spread, others], axis=0)[None]
    scaled = jnp.concatenate([scaled, jnp.repeat(small, groups, axis=0)], axis=2)
    places = (
        ring.members[:, None] * tok_rows + jnp.arange(tok_rows, dtype=jnp.int32)[None, :]
    ).reshape(seq_rows)
    tables = rotary_tables(places.astype(F32), head_size)

    gate_w = lax.all_gather(w_gate, "fsdp", axis=1, tiled=True)
    token_ring = Gather(ring, tokens)
    (scaled,) = window([token_ring], scaled)
    qkv = lax.all_to_all(scaled, "seq", split_axis=0, concat_axis=0, tiled=True).reshape(
        groups * own_rows, qkv_width + extra
    )
    qkv, w_output = window([token_ring], qkv, w_output)
    part_rows = groups * own_rows // 2
    first_half = fsdp.spread(qkv[:part_rows])
    for step in range(3, ring.steps):
        qkv, first_half, tables, places, w_output = window(
            [token_ring], qkv, first_half, tables, places, w_output
        )
    cos_table, sine_table = tables
    second_half = fsdp.spread(qkv[part_rows:])
    qkv, first_half, second_half, w_output, cotangent_sent = window(
        [token_ring], qkv, first_half, second_half, w_output, cotangent
    )

    cot_ring = Gather(ring, cotangent_sent)
    qkv_parts = fsdp.swapped(
        qkv, [jnp.concatenate(pair, axis=0) for pair in zip(first_half, second_half)]
    )
    gains_qk = sum(
        jnp.sum(
            part.reshape(groups, own_rows, qkv_width + extra)[
                :, :2, qkv_width : qkv_width + head_size
            ].astype(F32),
            axis=0,
        )
        for part in qkv_parts
    )
    projected = project(
        token_ring.pieces, qkv_parts, fsdp.blocks, qkv_width, cos_table, sine_table, gains_qk
    )
    held = lax.ppermute(w_output, ALL, exchange)
    projected, held, qkv_parts = window([cot_ring], projected, held, qkv_parts)
    normed_all, qk_pre, query_seq, key_seq, value_seq = projected
    attended, probs = attend(query_seq, key_seq, value_seq, places, scale_qk, tok_rows)
    held_others = fsdp.spread(held)
    attended, probs, held, held_others, w_up = window(
        [cot_ring], attended, probs, held, held_others, w_up
    )
    up_w = lax.all_gather(w_up, "fsdp", axis=1, tiled=True)
    output_w = lay(fsdp.swapped(held, held_others), fsdp.blocks)
    branch = rows_dot(attended, output_w, 0, tok_rows)
    for step in range(3, ring.steps):
        branch, output_w, gate_w, w_down = window([cot_ring], branch, output_w, gate_w, w_down)
    down_w = lax.all_gather(w_down, "fsdp", axis=2, tiled=True)

    branch_ring = Scatter(ring, lambda spot: (branch[spot], 0), tok_rows, tuple(branch[-2:]))
    (qkv_parts,) = window([branch_ring, cot_ring], qkv_parts)

    def small_arrays(parts):
        small = jnp.stack([part[:, qkv_width:].reshape(groups, -1) for part in parts])
        small = jnp.take(small, fsdp.spots, axis=0)[:, :, 2 * extra :]
        cuts = [own_rows, own_rows * experts_all, tok_rows * top_k]
        ends = [sum(cuts[: i + 1]) for i in range(3)]
        gain_mlp = small[:, :, : ends[0]].reshape(1, model_width).astype(F32)
        router_w = small[:, :, ends[0] : ends[1]].reshape(model_width, experts_all)
        ids_all = parts[0][:, qkv_width:].reshape(groups, -1)[:, 2 * extra :]
        ids_near = jnp.take(ids_all[:, ends[1] : ends[2]], ring.members, axis=0)
        ids_near = ids_near.astype(jnp.int32).reshape(groups, top_k, tok_rows)
        return gain_mlp, router_w, ids_near.transpose(1, 0, 2).reshape(top_k, -1)

    (gain_mlp, router_w, ids_near), qkv_parts, cot_pieces = window(
        [branch_ring], small_arrays(qkv_parts), qkv_parts, cot_ring.pieces
    )
    qkv_w, cot_all = lay(qkv_parts, fsdp.blocks), lay(cot_pieces)
    for step in range(3, ring.steps):
        qkv_w, cot_all = window([branch_ring], qkv_w, cot_all)
    (up_w,) = window([branch_ring], up_w)
    middle, mixer_in = by_rows(
        enter_kernel, branch_ring.landed(), [tokens], [gain_mlp], [F32, BF16]
    )

    def shares(rows_in, ids):
        logits = jnp.dot(rows_in, router_w, preferred_element_type=F32)
        chosen = jnp.sum(
            (ids[:, :, None] == jnp.arange(experts_all, dtype=jnp.int32)).astype(F32), axis=0
        )
        masked = jnp.where(chosen > 0, logits, NEG_LARGE)
        grown = jnp.exp(masked - jnp.max(masked, axis=-1, keepdims=True)) * chosen
        return grown / jnp.sum(grown, axis=-1, keepdims=True)

    def gate_part(rows_in, first):
        last = first + rows_in.shape[0]
        share = lax.dynamic_slice_in_dim(
            shares(rows_in, ids_near[:, first:last]), seat * local_experts, local_experts, 1
        ).T[:, :, None]
        return share, jnp.einsum("td,edf->etf", rows_in, gate_w, preferred_element_type=F32)

    def expert_part(rows_in, first, share, gate_pre):
        last = first + rows_in.shape[0]
        up_pre = jnp.einsum("td,edf->etf", rows_in, up_w, preferred_element_type=F32)
        back = down_back[:, first:last]
        sigmoid = jax.nn.sigmoid(gate_pre)
        silu_gate = gate_pre * sigmoid
        active = silu_gate * up_pre
        grad_share = jnp.sum(active * back, axis=-1)
        active_shared = (active * share).astype(BF16)
        grad_active = back * share
        grad_up_pre = (grad_active * silu_gate).astype(BF16)
        grad_gate_pre = (
            grad_active * up_pre * sigmoid * (1.0 + gate_pre * (1.0 - sigmoid))
        ).astype(BF16)
        return grad_share, active_shared, grad_gate_pre, grad_up_pre

    def entered_part(part):
        entered = jnp.einsum(
            "etf,edf->td", part[2], gate_w, preferred_element_type=F32
        ) + jnp.einsum("etf,edf->td", part[3], up_w, preferred_element_type=F32)
        return entered.astype(BF16)

    cut = ring.steps // 2
    early = (2 * cut + 1) * tok_rows
    mixer_ring = Gather(ring, mixer_in)
    (cot_all,) = window([mixer_ring], cot_all)
    cot_all, down_w = prepare([mixer_ring], cot_all, down_w)
    down_back = jnp.einsum("td,efd->etf", cot_all, down_w, preferred_element_type=F32)
    (down_back,) = window([mixer_ring], down_back)
    for step in range(3, cut + 1):
        window([mixer_ring])
    early_rows = jnp.concatenate(mixer_ring.pieces, axis=0)
    early_share, early_gate = gate_part(early_rows, 0)
    for step in range(cut + 1, ring.steps):
        early_rows, early_share, early_gate = window(
            [mixer_ring], early_rows, early_share, early_gate
        )
    early_part = expert_part(early_rows, 0, early_share, early_gate)
    early_part, early_rows = window([mixer_ring], early_part, early_rows)
    late_rows = jnp.concatenate(mixer_ring.pieces[2 * cut + 1 :], axis=0)
    late_part = expert_part(late_rows, early, *gate_part(late_rows, early))
    late_entered = entered_part(late_part)
    late_entered, late_part, early_part, late_rows, early_rows = together(
        late_entered, late_part, early_part, late_rows, early_rows
    )

    def entered_piece(spot):
        if spot * tok_rows >= early:
            return late_entered, spot - early // tok_rows
        return early_entered[spot], 0

    entered_ring = Scatter(ring, entered_piece, tok_rows)
    grad_share = jnp.concatenate([early_part[0], late_part[0]], axis=1)
    grad_share_own = lax.all_to_all(
        jnp.take(grad_share.reshape(local_experts, groups, tok_rows), ring.spots, axis=1).transpose(
            1, 0, 2
        ),
        "seq",
        split_axis=0,
        concat_axis=0,
        tiled=True,
    )
    early_entered = entered_rows(
        early_part[2], early_part[3], gate_w, up_w, tok_rows
    )
    window([entered_ring])
    early_entered, early_part, late_part, early_rows, late_rows = window(
        [entered_ring], early_entered, early_part, late_part, early_rows, late_rows
    )
    early_part, late_part, early_rows, late_rows = prepare(
        [entered_ring], early_part, late_part, early_rows, late_rows
    )
    (grad_gate,) = row_grads((early_rows, late_rows), (early_part[2], late_part[2]))
    for step in range(3, ring.steps):
        grad_gate, early_part, late_part, early_rows, late_rows, grad_share_own = window(
            [entered_ring], grad_gate, early_part, late_part, early_rows, late_rows, grad_share_own
        )
    grad_gate = lax.psum_scatter(grad_gate, "fsdp", scatter_dimension=1, tiled=True)
    early_part, late_part, early_rows, late_rows, grad_share_own = prepare(
        [entered_ring], early_part, late_part, early_rows, late_rows, grad_share_own
    )
    grad_share_own = grad_share_own.reshape(experts_all, tok_rows).T
    share_own = shares(mixer_in, expert_ids.T)
    grad_logits = (
        share_own
        * (grad_share_own - jnp.sum(share_own * grad_share_own, axis=-1, keepdims=True))
    ).astype(BF16)
    (grad_up,) = row_grads((early_rows, late_rows), (early_part[3], late_part[3]))
    grad_up, grad_logits, early_active, late_active = window(
        [entered_ring], grad_up, grad_logits, early_part[1], late_part[1]
    )
    grad_up = lax.psum_scatter(grad_up, "fsdp", scatter_dimension=1, tiled=True)
    grad_middle, grad_branch, grad_gain_m = by_rows(
        mixer_back_kernel,
        entered_ring.landed(),
        [middle, cotangent],
        [grad_logits, router_w, gain_mlp],
        [F32, BF16],
        [(1, model_width)],
    )

    grads_ring = Gather(ring, grad_branch)
    early_active, late_active = prepare([grads_ring], early_active, late_active)
    produced = [
        jnp.einsum("etf,efd->td", active, down_w, preferred_element_type=F32).astype(BF16)
        for active in (early_active, late_active)
    ]
    produced, early_active, late_active = window(
        [grads_ring], produced, early_active, late_active
    )
    early_active, late_active = prepare([grads_ring], early_active, late_active)
    down_parts = down_grads((early_active, late_active), cot_all, fsdp.targets)
    (down_parts,) = window([grads_ring], down_parts)
    paired_down = fsdp.pair(down_parts)
    for step in range(3, cut + 1):
        window([grads_ring])

    def two_parts(parts):
        def piece(spot):
            if spot * tok_rows >= early:
                return parts[1], spot - early // tok_rows
            return parts[0], spot

        return piece

    def back(pieces, offset, before):
        return attend_back(
            pieces,
            offset,
            before,
            output_w,
            probs,
            query_seq,
            key_seq,
            value_seq,
            qk_pre,
            cos_table,
            sine_table,
            gains_qk,
            scale_qk,
        )

    grads = back(grads_ring.pieces, 0, None)
    grad_small = dot(mixer_in, jnp.pad(grad_logits, ((0, 0), (0, head_size - experts_all))), 0, 0)
    for step in range(cut + 1, ring.steps):
        grad_small, paired_down = window([grads_ring], grad_small, paired_down)
    layer_ring = Scatter(ring, two_parts(produced), tok_rows)
    (grads,) = window([grads_ring, layer_ring], grads)
    grads = back(grads_ring.pieces[2 * cut + 1 :], 2 * cut + 1, grads)
    (grads,) = window([layer_ring], grads)

    grads, grad_small, branch_pieces = prepare(
        [layer_ring], grads, grad_small, grads_ring.pieces
    )
    grad_qkv = grads[0]
    grad_parts = project_back(
        normed_all, grad_qkv, grad_small, grad_gain_m, experts_all, grads[1], own_rows, fsdp.targets
    )
    output_parts = output_back(attended, branch_pieces, fsdp.targets)
    for step in range(3, ring.steps):
        grad_parts, grad_qkv, output_parts = window(
            [layer_ring], grad_parts, grad_qkv, output_parts
        )
    paired = fsdp.pair(grad_parts)
    paired, grad_qkv, output_parts = together(paired, grad_qkv, output_parts)
    sent = fsdp.send(paired)
    paired_output = fsdp.pair(output_parts)
    grad_hidden = rows_dot(grad_qkv, qkv_w, 1, tok_rows)
    grad_hidden, paired_output = window([layer_ring], grad_hidden, paired_output)
    (produced, spot), left, right = layer_ring.landed()
    layer_out = (
        middle
        + lax.slice_in_dim(produced, 0, tok_rows, axis=0).astype(F32)
        + left.astype(F32)
        + right.astype(F32)
    ).astype(BF16)

    hidden_ring = Scatter(
        ring, lambda spot: (grad_hidden[spot], 0), tok_rows, tuple(grad_hidden[-2:])
    )
    paired, sent, paired_output, paired_down = window(
        [hidden_ring], paired, sent, paired_output, paired_down
    )
    paired, sent, paired_output, paired_down = prepare(
        [hidden_ring], paired, sent, paired_output, paired_down
    )
    total = paired[0].astype(F32) + sum(part.astype(F32) for part in sent)
    grad_qkv_w = lax.all_to_all(
        total.astype(BF16).reshape(groups, own_rows, qkv_width + head_size),
        "seq",
        split_axis=0,
        concat_axis=0,
        tiled=True,
    )
    sent_output = fsdp.send(paired_output)
    down_first = fsdp.send([part[:1] for part in paired_down])
    paired_output, sent_output, paired_down, down_first, grad_qkv_w, grad_gate, grad_up = window(
        [hidden_ring],
        paired_output,
        sent_output,
        paired_down,
        down_first,
        grad_qkv_w,
        grad_gate,
        grad_up,
    )
    paired_output, sent_output, paired_down, grad_gate, grad_up = prepare(
        [hidden_ring], paired_output, sent_output, paired_down, grad_gate, grad_up
    )
    total = paired_output[0].astype(F32) + sum(part.astype(F32) for part in sent_output)
    grad_output_w = lax.ppermute(total.astype(BF16), ALL, exchange)
    down_rest = fsdp.send([part[1:] for part in paired_down])

    def corner(array):
        return lax.slice(array, (0,) * array.ndim, (1,) * (array.ndim - 2) + (8, 128))

    grad_gate, grad_up = grad_gate.astype(F32), grad_up.astype(F32)
    corners = [corner(array) for array in (grad_gate, grad_up, layer_out)]
    for step in range(3, ring.steps):
        grad_output_w, paired_down, corners = window(
            [hidden_ring], grad_output_w, paired_down, corners
        )
    grad_output_w, paired_down = prepare([hidden_ring], grad_output_w, paired_down)
    grad_output_w = grad_output_w.astype(F32)
    grad_down = paired_down[0].astype(F32) + sum(
        jnp.concatenate(pair, axis=0).astype(F32) for pair in zip(down_first, down_rest)
    )
    window([hidden_ring], [corner(grad_down), corner(grad_output_w)])
    (grad_tokens,) = by_rows(
        tokens_back_kernel, hidden_ring.landed(), [tokens, grad_middle], [], [BF16]
    )
    grad_query_w, grad_key_w, grad_value_w, grad_gain_a, small = weights_back(
        grad_qkv_w,
        weights_own,
        attn_gain.astype(F32)[:, None],
        held_groups,
        kv_heads,
        head_size,
    )
    gains = small[:4, head_size // 2 :].reshape(2, head_size)
    cut = query_gain.shape[0]
    gains = lax.dynamic_slice(gains, (0, me * cut), (2, cut))
    return (
        layer_out,
        grad_tokens,
        grad_gain_a[:, 0],
        grad_query_w,
        grad_key_w,
        grad_value_w,
        gains[0],
        gains[1],
        grad_output_w,
        small[:, experts_all],
        small[:, :experts_all],
        grad_gate,
        grad_up,
        grad_down,
    )


def solution(mesh):
    rows = P(("fsdp", "seq"), None)
    line = P(("fsdp", "seq"))
    wide = P("seq", "fsdp", None)
    deep = P("seq", None, "fsdp")
    in_specs = (
        rows, rows, rows, line, rows, rows, rows, line, line, rows, line, rows, wide, wide, deep,
    )
    out_specs = (
        rows, rows, line, rows, rows, rows, line, line, rows, line, rows, wide, wide, deep,
    )
    return jax.shard_map(
        on_device, mesh=mesh, in_specs=in_specs, out_specs=out_specs, check_vma=False
    )
```

```python
import math

import jax
import jax.numpy as jnp
import numpy as np
from jax import lax
from jax.experimental import pallas as pl
from jax.experimental.pallas import tpu as pltpu
from jax.sharding import PartitionSpec as P

NORM_EPS = 1e-06
ROPE_BASE = 1000000.0
NEG_LARGE = -1e30
F32 = jnp.float32
BF16 = jnp.bfloat16
ALL = ("fsdp", "seq")
VMEM_LIMIT = 40 * 1024 * 1024
LARGE_LIMIT = 56 * 1024 * 1024
SMALL_LIMIT = 16 * 1024 * 1024


def dot(left, right, left_dim, right_dim):
    return lax.dot_general(
        left, right, (((left_dim,), (right_dim,)), ((), ())), preferred_element_type=F32
    )


def norm_parts(values):
    row_scale = lax.rsqrt(jnp.mean(values * values, axis=-1, keepdims=True) + NORM_EPS)
    return (values * row_scale, row_scale)


def norm_back(grad_normed, normed, row_scale):
    return row_scale * (
        grad_normed - normed * jnp.mean(grad_normed * normed, axis=-1, keepdims=True)
    )


def rotary_tables(positions, head_size):
    half_size = head_size // 2
    frequency = jnp.exp(
        jnp.arange(half_size, dtype=F32) * (-2.0 * math.log(ROPE_BASE) / head_size)
    )
    angles = positions[:, None] * frequency[None, :]
    cosine, sine = jnp.cos(angles), jnp.sin(angles)
    return jnp.concatenate([cosine, cosine], axis=1), jnp.concatenate([-sine, sine], axis=1)


def swap_halves(values):
    return pltpu.roll(values, values.shape[-1] // 2, 1)


def params(limit=VMEM_LIMIT):
    return pltpu.CompilerParams(vmem_limit_bytes=limit)


def take_piece(step, pieces, halved, store):
    last = len(pieces) - (2 if halved else 0)
    for i in range(last):

        @pl.when(step == i)
        def _(i=i):
            store(0, pieces[i][...])

    if halved:

        @pl.when(step == last)
        def _():
            half = pieces[last].shape[0]
            store(0, pieces[last][...])
            store(half, pieces[last + 1][...])


def lay_kernel(count, halved, order_ref, *refs):
    def store(first, rows):
        refs[-1][first : first + rows.shape[0]] = rows

    take_piece(pl.program_id(0), refs[:count], halved, store)


def lay(pieces, order=None):
    halved = order is None
    members = len(pieces) - (1 if halved else 0)
    if halved:
        order = jnp.arange(members, dtype=jnp.int32)
    rows, cols = pieces[0].shape
    return pl.pallas_call(
        lambda *refs: lay_kernel(len(pieces), halved, *refs),
        grid_spec=pltpu.PrefetchScalarGridSpec(
            num_scalar_prefetch=1,
            grid=(members,),
            in_specs=[pl.BlockSpec(piece.shape, lambda i, order: (0, 0)) for piece in pieces],
            out_specs=pl.BlockSpec((rows, cols), lambda i, order: (order[i], 0)),
        ),
        out_shape=jax.ShapeDtypeStruct((members * rows, cols), pieces[0].dtype),
        compiler_params=params(),
        cost_estimate=pl.CostEstimate(
            flops=0, bytes_accessed=4 * members * rows * cols, transcendentals=0
        ),
    )(order, *pieces)


def project_kernel(heads, parts, count, order_ref, *refs):
    pieces, refs = refs[:count], refs[count:]
    weights, refs = refs[:parts], refs[parts:]
    cos_ref, sin_ref, gain_ref, n_ref, pre_ref, q_ref, k_ref, v_ref = refs
    size = cos_ref.shape[1]

    def store(first, rows):
        n_ref[first : first + rows.shape[0]] = norm_parts(rows.astype(F32))[0].astype(BF16)

    take_piece(pl.program_id(0), pieces, True, store)
    depth = weights[0].shape[0]
    projected = 0.0
    for part, w_ref in enumerate(weights):
        columns = pl.ds(pl.multiple_of(order_ref[part] * depth, depth), depth)
        projected += jnp.dot(n_ref[:, columns], w_ref[...], preferred_element_type=F32)
    pre_ref[...] = projected[:, : (heads + 1) * size]
    for head in range(heads + 1):
        row = 0 if head < heads else 1
        scaled = norm_parts(projected[:, head * size : (head + 1) * size])[0] * gain_ref[row : row + 1]
        turned = (scaled * cos_ref[...] + swap_halves(scaled) * sin_ref[...]).astype(BF16)
        if head < heads:
            q_ref[:, head * size : (head + 1) * size] = turned
        else:
            k_ref[...] = turned
    v_ref[...] = projected[:, (heads + 1) * size :].astype(BF16)


def project(pieces, weights, order, width, cos_table, sine_table, gains):
    block, depth = pieces[0].shape
    rows = block * (len(pieces) - 1)
    size = cos_table.shape[1]
    heads = width // size - 2
    spec = lambda cols: pl.BlockSpec((block, cols), lambda i, order: (i, 0))
    whole = lambda shape: pl.BlockSpec(shape, lambda i, order: (0, 0))
    return pl.pallas_call(
        lambda *refs: project_kernel(heads, len(weights), len(pieces), *refs),
        grid_spec=pltpu.PrefetchScalarGridSpec(
            num_scalar_prefetch=1,
            grid=(rows // block,),
            in_specs=[whole(piece.shape) for piece in pieces]
            + [whole((part.shape[0], width)) for part in weights]
            + [spec(size), spec(size), whole(gains.shape)],
            out_specs=[
                spec(depth), spec((heads + 1) * size), spec(heads * size), spec(size), spec(size),
            ],
        ),
        out_shape=[
            jax.ShapeDtypeStruct((rows, depth), BF16),
            jax.ShapeDtypeStruct((rows, (heads + 1) * size), F32),
            jax.ShapeDtypeStruct((rows, heads * size), BF16),
            jax.ShapeDtypeStruct((rows, size), BF16),
            jax.ShapeDtypeStruct((rows, size), BF16),
        ],
        compiler_params=params(LARGE_LIMIT),
        cost_estimate=pl.CostEstimate(
            flops=2 * rows * depth * width, bytes_accessed=16 << 20, transcendentals=0
        ),
    )(order, *pieces, *weights, cos_table, sine_table, gains)


def fetch(arrays, spots, buffers, sems):
    copies = [
        pltpu.make_async_copy(
            array.at[pl.ds(spot * buffer.shape[0], buffer.shape[0])], buffer, sems.at[i]
        )
        for i, (array, spot, buffer) in enumerate(zip(arrays, spots, buffers))
    ]
    for copy in copies:
        copy.start()
    for copy in copies:
        copy.wait()


def ring_add_kernel(spots, up_hbm, down_hbm, left_ref, right_ref, up_ref, down_ref, up_buf, down_buf, sems):
    fetch((up_hbm, down_hbm), spots, (up_buf, down_buf), sems)
    rows, half = up_buf.shape[0], left_ref.shape[0]
    if half == rows:
        up_ref[...] = (up_buf[...].astype(F32) + left_ref[...].astype(F32)).astype(BF16)
        down_ref[...] = (down_buf[...].astype(F32) + right_ref[...].astype(F32)).astype(BF16)
        return
    up_ref[:half] = (up_buf[:half].astype(F32) + left_ref[...].astype(F32)).astype(BF16)
    up_ref[half:] = up_buf[half:]
    down_ref[:half] = down_buf[:half]
    down_ref[half:] = (down_buf[half:].astype(F32) + right_ref[...].astype(F32)).astype(BF16)


HBM = pl.BlockSpec(memory_space=pltpu.HBM)
VMEM = pl.BlockSpec(memory_space=pltpu.VMEM)


def ring_add(mine_up, mine_down, left, right, rows):
    width = left.shape[1]
    return pl.pallas_call(
        lambda *refs: ring_add_kernel((mine_up[1], mine_down[1]), *refs),
        in_specs=[HBM, HBM, VMEM, VMEM],
        out_specs=[VMEM, VMEM],
        out_shape=[jax.ShapeDtypeStruct((rows, width), BF16)] * 2,
        scratch_shapes=[pltpu.VMEM((rows, width), BF16)] * 2 + [pltpu.SemaphoreType.DMA((2,))],
        compiler_params=pltpu.CompilerParams(vmem_limit_bytes=SMALL_LIMIT),
        cost_estimate=pl.CostEstimate(
            flops=2 * rows * width, bytes_accessed=12 * rows * width, transcendentals=0
        ),
    )(mine_up[0], mine_down[0], left, right)


def summed(mine_ref, left_ref, right_ref):
    return mine_ref[...].astype(F32) + left_ref[...].astype(F32) + right_ref[...].astype(F32)


def enter_kernel(mine_ref, left_ref, right_ref, x_ref, gain_ref, middle_ref, mixer_ref):
    middle = x_ref[...].astype(F32) + summed(mine_ref, left_ref, right_ref)
    middle_ref[...] = middle
    mixer_ref[...] = (norm_parts(middle)[0] * gain_ref[...]).astype(BF16)


def mixer_back_kernel(
    mine_ref, left_ref, right_ref, middle_ref, cot_ref, logits_ref, router_ref, gain_ref, *refs
):
    grad_ref, branch_ref, gains_ref = refs
    grad_mixer = summed(mine_ref, left_ref, right_ref) + dot(logits_ref[...], router_ref[...], 1, 1)
    normed, row_scale = norm_parts(middle_ref[...])
    gains_ref[...] = jnp.sum(grad_mixer * normed, axis=0, keepdims=True)
    grad = cot_ref[...].astype(F32) + norm_back(grad_mixer * gain_ref[...], normed, row_scale)
    grad_ref[...] = grad
    branch_ref[...] = grad.astype(BF16)


def tokens_back_kernel(mine_ref, left_ref, right_ref, x_ref, grad_ref, out_ref):
    normed, row_scale = norm_parts(x_ref[...].astype(F32))
    grad = norm_back(summed(mine_ref, left_ref, right_ref), normed, row_scale)
    out_ref[...] = (grad_ref[...] + grad).astype(BF16)


def by_rows(kernel, landed, lines, inputs, outs, sums=()):
    (mine, spot), left, right = landed
    rows, width = left.shape
    count = 1 + len(lines)

    def whole(*refs):
        arrays, refs = refs[:count], refs[count:]
        refs, buffers, sems = refs[: -count - 1], refs[-count - 1 : -1], refs[-1]
        fetch(arrays, (spot,) + (0,) * len(lines), buffers, sems)
        kernel(buffers[0], *refs[:2], *buffers[1:], *refs[2:])

    return pl.pallas_call(
        whole,
        in_specs=[HBM] * count + [VMEM] * (2 + len(inputs)),
        out_specs=[VMEM] * (len(outs) + len(sums)),
        out_shape=[jax.ShapeDtypeStruct((rows, width), kind) for kind in outs]
        + [jax.ShapeDtypeStruct(shape, F32) for shape in sums],
        scratch_shapes=[pltpu.VMEM((rows, array.shape[1]), array.dtype) for array in [mine] + lines]
        + [pltpu.SemaphoreType.DMA((count,))],
        compiler_params=pltpu.CompilerParams(vmem_limit_bytes=SMALL_LIMIT),
        cost_estimate=pl.CostEstimate(
            flops=20 * rows * width, bytes_accessed=16 * rows * width, transcendentals=rows
        ),
    )(mine, *lines, left, right, *inputs)


def weights_back_kernel(held, copies, size, came_ref, own_ref, gain_ref, q_ref, k_ref, v_ref, gains_ref, small_ref):
    groups, rows, _ = came_ref.shape
    width = own_ref.shape[2]
    wide = width - 2 * size
    gains = jnp.zeros((rows, 1), F32)
    small = jnp.zeros(small_ref.shape, F32)
    gain = gain_ref[...]
    seen = set()
    for member, group in enumerate(held):
        came = came_ref[member].astype(F32)
        gains += jnp.sum(
            came[:, :width] * own_ref[member].astype(F32), axis=1, keepdims=True
        )
        small += came[:, width:]
        came = came[:, :width] * gain
        q_ref[:, group * wide : (group + 1) * wide] = came[:, :wide]
        lanes = slice(group // copies * size, (group // copies + 1) * size)
        if group // copies not in seen:
            k_ref[:, lanes] = came[:, wide : wide + size]
            v_ref[:, lanes] = came[:, wide + size :]
        else:
            k_ref[:, lanes] += came[:, wide : wide + size]
            v_ref[:, lanes] += came[:, wide + size :]
        seen.add(group // copies)
    gains_ref[...] = jnp.broadcast_to(gains, gains_ref.shape)
    small_ref[...] = small


def weights_back(came, own, gain, held, kv_heads, size):
    groups, rows, total = came.shape
    width = own.shape[2]
    shape = lambda cols: jax.ShapeDtypeStruct((rows, cols), F32)
    return pl.pallas_call(
        lambda *refs: weights_back_kernel(held, groups // kv_heads, size, *refs),
        out_shape=[
            shape(groups * (width - 2 * size)),
            shape(kv_heads * size),
            shape(kv_heads * size),
            shape(128),
            shape(total - width),
        ],
        compiler_params=params(),
        cost_estimate=pl.CostEstimate(
            flops=4 * groups * rows * width, bytes_accessed=4 << 20, transcendentals=0
        ),
    )(came, own, gain)


def output_back_kernel(count, order_ref, left_ref, *refs):
    pieces, outs, (rows_ref, turned_ref, sum_ref) = refs[:count], refs[count:-3], refs[-3:]

    @pl.when(pl.program_id(0) == 0)
    def _():
        turned_ref[...] = left_ref[...].T

    first = 0
    for piece in pieces:
        rows_ref[first : first + piece.shape[0]] = piece[...]
        first += piece.shape[0]
    sum_ref[...] = jnp.dot(turned_ref[...], rows_ref[...], preferred_element_type=F32)
    for i, out_ref in enumerate(outs):
        rows = out_ref.shape[0]
        first = pl.multiple_of(order_ref[i] * rows, rows)
        out_ref[...] = sum_ref[pl.ds(first, rows), :].astype(BF16)


def output_back(left, pieces, order):
    rows, width = left.shape
    cols = pieces[0].shape[1]
    parts = order.shape[0]
    block = cols // 4
    return pl.pallas_call(
        lambda *refs: output_back_kernel(len(pieces), *refs),
        grid_spec=pltpu.PrefetchScalarGridSpec(
            num_scalar_prefetch=1,
            grid=(4,),
            in_specs=[pl.BlockSpec((rows, width), lambda i, order: (0, 0))]
            + [pl.BlockSpec((piece.shape[0], block), lambda i, order: (0, i)) for piece in pieces],
            out_specs=[pl.BlockSpec((width // parts, block), lambda i, order: (0, i))] * parts,
            scratch_shapes=[
                pltpu.VMEM((rows, block), BF16),
                pltpu.VMEM((width, rows), BF16),
                pltpu.VMEM((width, block), F32),
            ],
        ),
        out_shape=[jax.ShapeDtypeStruct((width // parts, cols), BF16)] * parts,
        compiler_params=params(),
        cost_estimate=pl.CostEstimate(
            flops=2 * rows * width * cols, bytes_accessed=8 << 20, transcendentals=0
        ),
    )(order, left, *pieces)


def project_back_kernel(
    own_rows, place, order_ref, normed_ref, grad_ref, small_ref, line_ref, gains_ref, *outs
):
    width = grad_ref.shape[1]
    part = dot(normed_ref[...], grad_ref[...], 0, 0).astype(BF16)
    small = small_ref[...]
    size = small.shape[1]
    row = lax.broadcasted_iota(jnp.int32, small.shape, 0) % own_rows
    lane = lax.broadcasted_iota(jnp.int32, small.shape, 1)
    small = jnp.where(lane == place, jnp.broadcast_to(line_ref[...], (size, small.shape[0])).T, small)
    upper = lane >= size // 2
    for i in range(2):
        gain = gains_ref[i : i + 1]
        for half, line in enumerate((pltpu.roll(gain, size // 2, 1), gain)):
            small = jnp.where(upper & (row == 2 * i + half), line, small)
    small = small.astype(BF16)
    for i, out_ref in enumerate(outs):

        @pl.when(pl.program_id(0) == i)
        def _(out_ref=out_ref):
            out_ref[:, :width] = part
            out_ref[:, width:] = small


def project_back(normed, grad, small, line, place, gains, own_rows, order):
    rows, depth = normed.shape
    width, extra = grad.shape[1], small.shape[1]
    parts = order.shape[0]
    block = depth // parts
    whole = lambda shape: pl.BlockSpec(shape, lambda i, order: (0, 0))
    return pl.pallas_call(
        lambda *refs: project_back_kernel(own_rows, place, *refs),
        grid_spec=pltpu.PrefetchScalarGridSpec(
            num_scalar_prefetch=1,
            grid=(parts,),
            in_specs=[
                pl.BlockSpec((rows, block), lambda i, order: (0, order[i])),
                whole(grad.shape),
                pl.BlockSpec((block, extra), lambda i, order: (order[i], 0)),
                pl.BlockSpec((1, block), lambda i, order: (0, order[i])),
                whole(gains.shape),
            ],
            out_specs=[whole((block, width + extra))] * parts,
        ),
        out_shape=[jax.ShapeDtypeStruct((block, width + extra), BF16)] * parts,
        compiler_params=params(),
        cost_estimate=pl.CostEstimate(
            flops=2 * rows * depth * width, bytes_accessed=12 << 20, transcendentals=0
        ),
    )(order, normed, grad, small, line, gains)


def row_grads_kernel(first_ref, second_ref, *refs):
    count = len(refs) // 3
    grads, outs = refs[: 2 * count], refs[2 * count :]
    first, second = first_ref[...].T, second_ref[...].T
    for i, out_ref in enumerate(outs):
        for expert in range(out_ref.shape[0]):
            part = dot(first, grads[2 * i][expert], 1, 0)
            part += dot(second, grads[2 * i + 1][expert], 1, 0)
            out_ref[expert] = part.astype(BF16)


def row_grads(rows, *grads):
    experts, _, ff = grads[0][0].shape
    depth = rows[0].shape[1]
    block = depth // 4
    return pl.pallas_call(
        row_grads_kernel,
        grid=(4,),
        in_specs=[pl.BlockSpec((part.shape[0], block), lambda i: (0, i)) for part in rows]
        + [pl.BlockSpec(part.shape, lambda i: (0, 0, 0)) for pair in grads for part in pair],
        out_specs=[pl.BlockSpec((experts, block, ff), lambda i: (0, i, 0))] * len(grads),
        out_shape=[jax.ShapeDtypeStruct((experts, depth, ff), BF16)] * len(grads),
        compiler_params=params(LARGE_LIMIT),
        cost_estimate=pl.CostEstimate(
            flops=2 * len(grads) * experts * sum(part.shape[0] for part in rows) * ff * depth,
            bytes_accessed=24 << 20,
            transcendentals=0,
        ),
    )(*rows, *(part for pair in grads for part in pair))


def down_grads_kernel(order_ref, first_ref, second_ref, cot_ref, *refs):
    outs, turned_ref = refs[:-1], refs[-1]
    expert, step = pl.program_id(0), pl.program_id(1)
    cut = first_ref.shape[1]

    @pl.when(step == 0)
    def _():
        turned_ref[:, :cut] = first_ref[0].T
        turned_ref[:, cut:] = second_ref[0].T

    part = jnp.dot(turned_ref[...], cot_ref[...], preferred_element_type=F32).astype(BF16)
    for i, out_ref in enumerate(outs):

        @pl.when(step == i)
        def _(out_ref=out_ref):
            out_ref[expert] = part


def down_grads(active, cot, order):
    experts, _, ff = active[0].shape
    rows, depth = cot.shape
    parts = order.shape[0]
    block = depth // parts
    return pl.pallas_call(
        down_grads_kernel,
        grid_spec=pltpu.PrefetchScalarGridSpec(
            num_scalar_prefetch=1,
            grid=(experts, parts),
            in_specs=[
                pl.BlockSpec((1,) + part.shape[1:], lambda e, i, order: (e, 0, 0))
                for part in active
            ]
            + [pl.BlockSpec((rows, block), lambda e, i, order: (0, order[i]))],
            out_specs=[pl.BlockSpec((experts, ff, block), lambda e, i, order: (0, 0, 0))] * parts,
            scratch_shapes=[pltpu.VMEM((ff, rows), BF16)],
        ),
        out_shape=[jax.ShapeDtypeStruct((experts, ff, block), BF16)] * parts,
        compiler_params=params(),
        cost_estimate=pl.CostEstimate(
            flops=2 * experts * rows * ff * depth, bytes_accessed=16 << 20, transcendentals=0
        ),
    )(order, *active, cot)


def split_rows(result, outs):
    first = 0
    for out_ref in outs:
        out_ref[...] = result[first : first + out_ref.shape[0]].astype(BF16)
        first += out_ref.shape[0]


def split_shapes(rows, block, cols, halved):
    heights = [block] * (rows // block)
    if halved:
        heights[-1:] = [block // 2, block // 2]
    return [jax.ShapeDtypeStruct((height, cols), BF16) for height in heights]


def rows_dot(left, right, right_dim, block):
    rows, depth = left.shape
    cols = right.shape[1 - right_dim]
    each = cols // 4
    shapes = split_shapes(rows, block, cols, True)
    if right_dim:
        spec = pl.BlockSpec((each, depth), lambda i: (i, 0))
    else:
        spec = pl.BlockSpec((depth, each), lambda i: (0, i))
    return pl.pallas_call(
        lambda left_ref, right_ref, *outs: split_rows(
            dot(left_ref[...], right_ref[...], 1, right_dim), outs
        ),
        grid=(4,),
        in_specs=[pl.BlockSpec((rows, depth), lambda i: (0, 0)), spec],
        out_specs=[pl.BlockSpec((shape.shape[0], each), lambda i: (0, i)) for shape in shapes],
        out_shape=shapes,
        compiler_params=params(),
        cost_estimate=pl.CostEstimate(
            flops=2 * rows * depth * cols, bytes_accessed=8 << 20, transcendentals=0
        ),
    )(left, right)


def entered_kernel(first_ref, second_ref, first_w_ref, second_w_ref, *outs):
    total = 0.0
    for expert in range(first_ref.shape[0]):
        total += dot(first_ref[expert], first_w_ref[expert], 1, 1)
        total += dot(second_ref[expert], second_w_ref[expert], 1, 1)
    split_rows(total, outs)


def entered_rows(first, second, first_w, second_w, block):
    experts, rows, ff = first.shape
    depth = first_w.shape[1]
    each = depth // 4
    whole = pl.BlockSpec(first.shape, lambda i: (0, 0, 0))
    weight = pl.BlockSpec((experts, each, ff), lambda i: (0, i, 0))
    shapes = split_shapes(rows, block, depth, False)
    return pl.pallas_call(
        entered_kernel,
        grid=(4,),
        in_specs=[whole, whole, weight, weight],
        out_specs=[pl.BlockSpec((block, each), lambda i: (0, i))] * len(shapes),
        out_shape=shapes,
        compiler_params=params(LARGE_LIMIT),
        cost_estimate=pl.CostEstimate(
            flops=4 * experts * rows * ff * depth, bytes_accessed=20 << 20, transcendentals=0
        ),
    )(first, second, first_w, second_w)


def stack_heads(array, size):
    return jnp.concatenate(
        [array[:, i * size : (i + 1) * size] for i in range(array.shape[1] // size)], axis=0
    )


def attend_kernel(scale, q_ref, k_ref, v_ref, at_q_ref, at_k_ref, out_ref, p_ref):
    rows, size = q_ref.shape[0], k_ref.shape[1]
    heads = q_ref.shape[1] // size
    scores = dot(k_ref[...], stack_heads(q_ref[...], size), 1, 1) * scale
    at_q = jnp.concatenate([at_q_ref[...]] * heads, axis=1)
    scores = jnp.where(at_k_ref[...] <= at_q, scores, NEG_LARGE)
    grown = jnp.exp(scores - jnp.max(scores, axis=0, keepdims=True))
    probs = (grown * (1.0 / jnp.sum(grown, axis=0, keepdims=True))).astype(BF16)
    p_ref[...] = probs
    output = dot(v_ref[...].T, probs, 1, 0).T.astype(BF16)
    for head in range(heads):
        out_ref[:, head * size : (head + 1) * size] = output[head * rows : (head + 1) * rows]


def attend(query, key, value, places, scale, block):
    rows, width = query.shape
    size = key.shape[1]
    heads = width // size
    whole = lambda shape: pl.BlockSpec(shape, lambda i: (0, 0))
    return pl.pallas_call(
        lambda *refs: attend_kernel(scale, *refs),
        grid=(rows // block,),
        in_specs=[
            pl.BlockSpec((block, width), lambda i: (i, 0)),
            whole((rows, size)),
            whole((rows, size)),
            pl.BlockSpec((1, block), lambda i: (0, i)),
            whole((rows, 1)),
        ],
        out_specs=[
            pl.BlockSpec((block, width), lambda i: (i, 0)),
            pl.BlockSpec((rows, heads * block), lambda i: (0, i)),
        ],
        out_shape=[
            jax.ShapeDtypeStruct((rows, width), BF16),
            jax.ShapeDtypeStruct((rows, heads * rows), BF16),
        ],
        compiler_params=params(LARGE_LIMIT),
        cost_estimate=pl.CostEstimate(
            flops=4 * heads * rows * rows * size,
            bytes_accessed=12 << 20,
            transcendentals=heads * rows * rows,
        ),
    )(query, key, value, places[None, :], places[:, None])


def head_back(grad_turned, pre, gain, cosine, sine):
    grad = grad_turned * cosine - swap_halves(grad_turned) * sine
    normed, row_scale = norm_parts(pre)
    return (
        jnp.sum(grad * normed, axis=0, keepdims=True),
        norm_back(grad * gain, normed, row_scale).astype(BF16),
    )


def attend_back_kernel(scale, count, first, last, offset, *refs):
    pieces, refs = refs[:count], refs[count:]
    w_ref, p_ref, q_ref, k_ref, v_ref, pre_ref, cos_ref, sin_ref, gain_ref = refs[:9]
    refs = refs[9:]
    before, refs = (() if first else refs[:4]), (refs if first else refs[4:])
    out_ref, gains_ref, dk_ref, dv_ref, rows_ref = refs
    step = pl.program_id(0)
    rows, size = q_ref.shape[0], k_ref.shape[1]
    heads = q_ref.shape[1] // size

    def store(first, rows):
        rows_ref[first : first + rows.shape[0]] = rows

    take_piece(step, pieces, last, store)

    @pl.when(step == 0)
    def _():
        if first:
            dk_ref[...] = jnp.zeros_like(dk_ref)
            dv_ref[...] = jnp.zeros_like(dv_ref)
            gains_ref[...] = jnp.zeros_like(gains_ref)
        else:
            for now_ref, before_ref in zip((out_ref, gains_ref, dk_ref, dv_ref), before):
                now_ref[...] = before_ref[...]

    probs = p_ref[...]
    grads = stack_heads(dot(rows_ref[...], w_ref[...], 1, 1).astype(BF16), size)
    dv_ref[...] += dot(probs, grads, 1, 0)
    grad_probs = dot(v_ref[...], grads, 1, 1)
    probs = probs.astype(F32)
    grad_scores = (
        probs * (grad_probs - jnp.sum(probs * grad_probs, axis=0, keepdims=True))
    ).astype(BF16)
    dk_ref[...] += dot(grad_scores, stack_heads(q_ref[...], size), 1, 0)
    grad_query = dot(k_ref[...].T, grad_scores, 1, 0).T * scale
    start = pl.multiple_of((step + offset) * rows, rows)
    here = pl.ds(start, rows)
    cosine, sine = cos_ref[here, :], sin_ref[here, :]
    for head in range(heads):
        lanes = slice(head * size, (head + 1) * size)
        gain_part, part = head_back(
            grad_query[head * rows : (head + 1) * rows],
            pre_ref[here, lanes],
            gain_ref[0:1],
            cosine,
            sine,
        )
        gains_ref[0:1] += gain_part
        out_ref[here, lanes] = part

    if last:

        @pl.when(step == pl.num_programs(0) - 1)
        def _():
            gain_part, part = head_back(
                dk_ref[...] * scale,
                pre_ref[:, heads * size : (heads + 1) * size],
                gain_ref[1:2],
                cos_ref[...],
                sin_ref[...],
            )
            gains_ref[1:2] = gain_part
            out_ref[:, heads * size : (heads + 1) * size] = part
            out_ref[:, (heads + 1) * size :] = dv_ref[...].astype(BF16)


def attend_back(pieces, offset, before, weights, probs, query, key, value, pre, cos_table, sine_table, gains, scale):
    rows, width = query.shape
    size = key.shape[1]
    heads = width // size
    block, depth = pieces[0].shape
    first, last = before is None, before is not None
    steps = len(pieces) - (1 if last else 0)
    whole = lambda shape: pl.BlockSpec(shape, lambda i: (0, 0))
    shapes = [
        jax.ShapeDtypeStruct((rows, (heads + 2) * size), BF16),
        jax.ShapeDtypeStruct((8, size), F32),
        jax.ShapeDtypeStruct((rows, size), F32),
        jax.ShapeDtypeStruct((rows, size), F32),
    ]
    outs = [whole(shape.shape) for shape in shapes]
    return pl.pallas_call(
        lambda *refs: attend_back_kernel(scale, len(pieces), first, last, offset, *refs),
        grid=(steps,),
        in_specs=[whole(piece.shape) for piece in pieces]
        + [
            whole(weights.shape),
            pl.BlockSpec((rows, heads * block), lambda i: (0, i + offset)),
            pl.BlockSpec((block, width), lambda i: (i + offset, 0)),
            whole((rows, size)),
            whole((rows, size)),
            whole((rows, (heads + 1) * size)),
            whole((rows, size)),
            whole((rows, size)),
            whole(gains.shape),
        ]
        + ([] if first else outs),
        out_specs=outs,
        out_shape=shapes,
        scratch_shapes=[pltpu.VMEM((block, depth), BF16)],
        compiler_params=params(),
        cost_estimate=pl.CostEstimate(
            flops=(8 * heads * rows * size + 2 * depth * width) * steps * block,
            bytes_accessed=(3 << 20) * steps,
            transcendentals=0,
        ),
    )(*pieces, weights, probs, query, key, value, pre, cos_table, sine_table, gains, *(before or ()))


def after(value, *others):
    return lax.optimization_barrier((value, *others))[0]


def ring_order(size):
    if size % 4 or size < 8:
        return list(range(size))
    wide = size // 4
    walk = [(0, y) for y in range(wide)]
    for z in range(1, 4):
        walk += [(z, y) for y in (range(wide - 1, 0, -1) if z % 2 else range(1, wide))]
    walk += [(z, 0) for z in (3, 2, 1)]
    return [z * wide + y for z, y in walk]


def together(*values):
    return lax.optimization_barrier(values)


class Ring:
    def __init__(self, size):
        self.size = size
        self.steps = size // 2
        order = ring_order(size)
        self.up = [(order[i], order[(i + 1) % size]) for i in range(size)]
        self.down = [(order[i], order[(i - 1) % size]) for i in range(size)]
        self.offsets = [0]
        for step in range(1, self.steps):
            self.offsets += [-step, step]
        self.offsets += [self.steps]
        near = np.zeros((size, size), np.int32)
        for i, member in enumerate(order):
            near[member] = [order[(i + offset) % size] for offset in self.offsets]
        seat = lax.axis_index("seq")
        self.members = jnp.asarray(near)[seat]
        self.spots = jnp.asarray(np.argsort(near, axis=1).astype(np.int32))[seat]

    def swap(self, up, down):
        return lax.ppermute(up, "seq", self.up), lax.ppermute(down, "seq", self.down)

    def spot(self, offset):
        return self.offsets.index(offset)


class Gather:
    def __init__(self, ring, block):
        self.ring, self.step, self.pieces = ring, 0, [block]
        self.left = self.right = block
        self.ready = None

    def sends(self):
        if self.step + 1 < self.ring.steps:
            return self.left, self.right
        half = self.left.shape[0] // 2
        return self.left[:half], self.right[half:]

    def start(self):
        ready = self.ready or self.sends()
        self.step += 1
        self.ready = None
        return self.ring.swap(*ready)

    def end(self, left, right):
        self.left, self.right = left, right
        self.pieces += [left, right]


class Scatter:
    def __init__(self, ring, piece, rows, far=None):
        self.ring, self.step, self.piece, self.rows, self.far = ring, 0, piece, rows, far
        self.left = self.right = self.ready = None

    def sends(self):
        ring, rows = self.ring, self.rows
        if self.step == 0 and self.far:
            return self.far
        if self.step == 0:
            whole, spot = self.piece(ring.spot(ring.steps))
            start, middle, end = spot * rows, spot * rows + rows // 2, (spot + 1) * rows
            return (
                lax.slice_in_dim(whole, start, middle, axis=0),
                lax.slice_in_dim(whole, middle, end, axis=0),
            )
        place = ring.steps - self.step
        mine_up, mine_down = self.piece(ring.spot(place)), self.piece(ring.spot(-place))
        return ring_add(mine_up, mine_down, self.left, self.right, rows)

    def start(self):
        ready = self.ready or self.sends()
        self.step += 1
        self.ready = None
        return self.ring.swap(*ready)

    def end(self, left, right):
        self.left, self.right = left, right

    def landed(self):
        return self.piece(0), self.left, self.right


def prepare(rings, *values):
    ready, values = together([ring.sends() for ring in rings], values)
    for ring, sends in zip(rings, ready):
        ring.ready = tuple(sends)
    return values


def window(rings, *values):
    moved = [ring.start() for ring in rings]
    moved, values = together(moved, values)
    for ring, (left, right) in zip(rings, moved):
        ring.end(left, right)
    return values


class Fsdp:
    def __init__(self, size):
        self.size = size
        self.across = size // 2

        def blocks(way):
            return np.asarray(
                [
                    [
                        (i // 2 + way * step) % self.across * 2 + (i % 2 ^ flip)
                        for step in range(self.across)
                        for flip in (0, 1)
                    ]
                    for i in range(size)
                ],
                np.int32,
            )

        index = lax.axis_index("fsdp")
        self.blocks = jnp.asarray(blocks(-1))[index]
        self.targets = jnp.asarray(blocks(1))[index]
        self.spots = jnp.asarray(np.argsort(blocks(-1), axis=1).astype(np.int32))[index]

    def swap(self, array):
        return lax.ppermute(array, "fsdp", [(i, i ^ 1) for i in range(self.size)])

    def shift(self, array, step):
        perm = [
            (x * 2 + c, (x + step) % self.across * 2 + c)
            for x in range(self.across)
            for c in (0, 1)
        ]
        return lax.ppermute(array, "fsdp", perm)

    def spread(self, block):
        return [self.shift(block, step) for step in range(1, self.across)]

    def swapped(self, block, others):
        return [part for mine in [block] + others for part in (mine, self.swap(mine))]

    def pair(self, parts):
        return [
            (parts[i].astype(F32) + self.swap(parts[i + 1]).astype(F32)).astype(BF16)
            for i in range(0, self.size, 2)
        ]

    def send(self, paired):
        return [self.shift(part, step) for step, part in enumerate(paired) if step]


def on_device(
    tokens,
    cotangent,
    expert_ids,
    attn_gain,
    w_query,
    w_key,
    w_value,
    query_gain,
    key_gain,
    w_output,
    mlp_gain,
    w_router,
    w_gate,
    w_up,
    w_down,
):
    groups = lax.axis_size("seq")
    splits = lax.axis_size("fsdp")
    counts = groups * splits
    ring, fsdp = Ring(groups), Fsdp(splits)
    seat = lax.axis_index("seq")
    me = lax.axis_index(ALL)
    tok_rows, model_width = tokens.shape
    top_k = expert_ids.shape[1]
    own_rows = w_query.shape[0]
    head_size = query_gain.shape[0] * counts
    heads_all = w_query.shape[1] // head_size
    kv_heads = w_key.shape[1] // head_size
    head_local = heads_all // groups
    copies = groups // kv_heads
    query_width = head_local * head_size
    qkv_width = query_width + 2 * head_size
    experts_all = w_router.shape[1]
    local_experts, _, ff = w_gate.shape
    seq_rows = tok_rows * groups
    scale_qk = 1.0 / math.sqrt(head_size)

    held_groups = [seat % splits * (groups // splits) + seat // splits for seat in range(groups)]
    exchange = [
        (j * groups + part * splits + i, i * groups + part * splits + j)
        for j in range(splits)
        for part in range(groups // splits)
        for i in range(splits)
    ]

    def by_member(weights, group_of):
        width = weights.shape[1] // (max(group_of) + 1)
        return [weights[:, group * width : (group + 1) * width] for group in group_of]

    kv_of = [group // copies for group in held_groups]
    weights_own = jnp.stack(
        [
            jnp.concatenate(parts, axis=1)
            for parts in zip(
                by_member(w_query, held_groups), by_member(w_key, kv_of), by_member(w_value, kv_of)
            )
        ]
    )
    scaled = (weights_own.astype(F32) * attn_gain.astype(F32)[None, :, None]).astype(BF16)

    def placed(gain):
        return lax.dynamic_update_slice(
            jnp.zeros((head_size,), BF16), gain, (me * gain.shape[0],)
        )

    others = jnp.concatenate(
        [mlp_gain, w_router.reshape(-1), expert_ids.T.reshape(-1).astype(BF16)]
    )
    extra = -(-(others.shape[0] + 2 * head_size) // (own_rows * head_size)) * head_size
    spread = jnp.zeros((2, extra), BF16).at[0, :head_size].set(placed(query_gain))
    spread = spread.at[1, :head_size].set(placed(key_gain))
    spare = (own_rows - 2) * extra - others.shape[0]
    others = jnp.pad(others, (0, spare)).reshape(own_rows - 2, extra)
    small = jnp.concatenate([spread, others], axis=0)[None]
    scaled = jnp.concatenate([scaled, jnp.repeat(small, groups, axis=0)], axis=2)
    places = (
        ring.members[:, None] * tok_rows + jnp.arange(tok_rows, dtype=jnp.int32)[None, :]
    ).reshape(seq_rows)
    tables = rotary_tables(places.astype(F32), head_size)

    gate_w = lax.all_gather(w_gate, "fsdp", axis=1, tiled=True)
    token_ring = Gather(ring, tokens)
    (scaled,) = window([token_ring], scaled)
    qkv = lax.all_to_all(scaled, "seq", split_axis=0, concat_axis=0, tiled=True).reshape(
        groups * own_rows, qkv_width + extra
    )
    qkv, w_output = window([token_ring], qkv, w_output)
    part_rows = groups * own_rows // 2
    first_half = fsdp.spread(qkv[:part_rows])
    for step in range(3, ring.steps):
        qkv, first_half, tables, places, w_output = window(
            [token_ring], qkv, first_half, tables, places, w_output
        )
    cos_table, sine_table = tables
    second_half = fsdp.spread(qkv[part_rows:])
    qkv, first_half, second_half, w_output, cotangent_sent = window(
        [token_ring], qkv, first_half, second_half, w_output, cotangent
    )

    cot_ring = Gather(ring, cotangent_sent)
    qkv_parts = fsdp.swapped(
        qkv, [jnp.concatenate(pair, axis=0) for pair in zip(first_half, second_half)]
    )
    gains_qk = sum(
        jnp.sum(
            part.reshape(groups, own_rows, qkv_width + extra)[
                :, :2, qkv_width : qkv_width + head_size
            ].astype(F32),
            axis=0,
        )
        for part in qkv_parts
    )
    projected = project(
        token_ring.pieces, qkv_parts, fsdp.blocks, qkv_width, cos_table, sine_table, gains_qk
    )
    held = lax.ppermute(w_output, ALL, exchange)
    projected, held, qkv_parts = window([cot_ring], projected, held, qkv_parts)
    normed_all, qk_pre, query_seq, key_seq, value_seq = projected
    attended, probs = attend(query_seq, key_seq, value_seq, places, scale_qk, tok_rows)
    held_others = fsdp.spread(held)
    attended, probs, held, held_others, w_up = window(
        [cot_ring], attended, probs, held, held_others, w_up
    )
    up_w = lax.all_gather(w_up, "fsdp", axis=1, tiled=True)
    output_w = lay(fsdp.swapped(held, held_others), fsdp.blocks)
    branch = rows_dot(attended, output_w, 0, tok_rows)
    for step in range(3, ring.steps):
        branch, output_w, gate_w, w_down = window([cot_ring], branch, output_w, gate_w, w_down)
    down_w = lax.all_gather(w_down, "fsdp", axis=2, tiled=True)

    branch_ring = Scatter(ring, lambda spot: (branch[spot], 0), tok_rows, tuple(branch[-2:]))
    (qkv_parts,) = window([branch_ring, cot_ring], qkv_parts)

    def small_arrays(parts):
        small = jnp.stack([part[:, qkv_width:].reshape(groups, -1) for part in parts])
        small = jnp.take(small, fsdp.spots, axis=0)[:, :, 2 * extra :]
        cuts = [own_rows, own_rows * experts_all, tok_rows * top_k]
        ends = [sum(cuts[: i + 1]) for i in range(3)]
        gain_mlp = small[:, :, : ends[0]].reshape(1, model_width).astype(F32)
        router_w = small[:, :, ends[0] : ends[1]].reshape(model_width, experts_all)
        ids_all = parts[0][:, qkv_width:].reshape(groups, -1)[:, 2 * extra :]
        ids_near = jnp.take(ids_all[:, ends[1] : ends[2]], ring.members, axis=0)
        ids_near = ids_near.astype(jnp.int32).reshape(groups, top_k, tok_rows)
        return gain_mlp, router_w, ids_near.transpose(1, 0, 2).reshape(top_k, -1)

    (gain_mlp, router_w, ids_near), qkv_parts, cot_pieces = window(
        [branch_ring], small_arrays(qkv_parts), qkv_parts, cot_ring.pieces
    )
    qkv_w, cot_all = lay(qkv_parts, fsdp.blocks), lay(cot_pieces)
    for step in range(3, ring.steps):
        qkv_w, cot_all = window([branch_ring], qkv_w, cot_all)
    (up_w,) = window([branch_ring], up_w)
    middle, mixer_in = by_rows(
        enter_kernel, branch_ring.landed(), [tokens], [gain_mlp], [F32, BF16]
    )

    def shares(rows_in, ids):
        logits = jnp.dot(rows_in, router_w, preferred_element_type=F32)
        chosen = jnp.sum(
            (ids[:, :, None] == jnp.arange(experts_all, dtype=jnp.int32)).astype(F32), axis=0
        )
        masked = jnp.where(chosen > 0, logits, NEG_LARGE)
        grown = jnp.exp(masked - jnp.max(masked, axis=-1, keepdims=True)) * chosen
        return grown / jnp.sum(grown, axis=-1, keepdims=True)

    def gate_part(rows_in, first):
        last = first + rows_in.shape[0]
        share = lax.dynamic_slice_in_dim(
            shares(rows_in, ids_near[:, first:last]), seat * local_experts, local_experts, 1
        ).T[:, :, None]
        return share, jnp.einsum("td,edf->etf", rows_in, gate_w, preferred_element_type=F32)

    def expert_part(rows_in, first, share, gate_pre):
        last = first + rows_in.shape[0]
        up_pre = jnp.einsum("td,edf->etf", rows_in, up_w, preferred_element_type=F32)
        back = down_back[:, first:last]
        sigmoid = jax.nn.sigmoid(gate_pre)
        silu_gate = gate_pre * sigmoid
        active = silu_gate * up_pre
        grad_share = jnp.sum(active * back, axis=-1)
        active_shared = (active * share).astype(BF16)
        grad_active = back * share
        grad_up_pre = (grad_active * silu_gate).astype(BF16)
        grad_gate_pre = (
            grad_active * up_pre * sigmoid * (1.0 + gate_pre * (1.0 - sigmoid))
        ).astype(BF16)
        return grad_share, active_shared, grad_gate_pre, grad_up_pre

    def entered_part(part):
        entered = jnp.einsum(
            "etf,edf->td", part[2], gate_w, preferred_element_type=F32
        ) + jnp.einsum("etf,edf->td", part[3], up_w, preferred_element_type=F32)
        return entered.astype(BF16)

    cut = ring.steps // 2
    early = (2 * cut + 1) * tok_rows
    mixer_ring = Gather(ring, mixer_in)
    (cot_all,) = window([mixer_ring], cot_all)
    cot_all, down_w = prepare([mixer_ring], cot_all, down_w)
    down_back = jnp.einsum("td,efd->etf", cot_all, down_w, preferred_element_type=F32)
    (down_back,) = window([mixer_ring], down_back)
    for step in range(3, cut + 1):
        window([mixer_ring])
    early_rows = jnp.concatenate(mixer_ring.pieces, axis=0)
    early_share, early_gate = gate_part(early_rows, 0)
    for step in range(cut + 1, ring.steps):
        early_rows, early_share, early_gate = window(
            [mixer_ring], early_rows, early_share, early_gate
        )
    early_part = expert_part(early_rows, 0, early_share, early_gate)
    early_part, early_rows = window([mixer_ring], early_part, early_rows)
    late_rows = jnp.concatenate(mixer_ring.pieces[2 * cut + 1 :], axis=0)
    late_part = expert_part(late_rows, early, *gate_part(late_rows, early))
    late_entered = entered_part(late_part)
    late_entered, late_part, early_part, late_rows, early_rows = together(
        late_entered, late_part, early_part, late_rows, early_rows
    )

    def entered_piece(spot):
        if spot * tok_rows >= early:
            return late_entered, spot - early // tok_rows
        return early_entered[spot], 0

    entered_ring = Scatter(ring, entered_piece, tok_rows)
    grad_share = jnp.concatenate([early_part[0], late_part[0]], axis=1)
    grad_share_own = lax.all_to_all(
        jnp.take(grad_share.reshape(local_experts, groups, tok_rows), ring.spots, axis=1).transpose(
            1, 0, 2
        ),
        "seq",
        split_axis=0,
        concat_axis=0,
        tiled=True,
    )
    early_entered = entered_rows(
        early_part[2], early_part[3], gate_w, up_w, tok_rows
    )
    window([entered_ring])
    early_entered, early_part, late_part, early_rows, late_rows = window(
        [entered_ring], early_entered, early_part, late_part, early_rows, late_rows
    )
    early_part, late_part, early_rows, late_rows = prepare(
        [entered_ring], early_part, late_part, early_rows, late_rows
    )
    (grad_gate,) = row_grads((early_rows, late_rows), (early_part[2], late_part[2]))
    for step in range(3, ring.steps):
        grad_gate, early_part, late_part, early_rows, late_rows, grad_share_own = window(
            [entered_ring], grad_gate, early_part, late_part, early_rows, late_rows, grad_share_own
        )
    grad_gate = lax.psum_scatter(grad_gate, "fsdp", scatter_dimension=1, tiled=True)
    early_part, late_part, early_rows, late_rows, grad_share_own = prepare(
        [entered_ring], early_part, late_part, early_rows, late_rows, grad_share_own
    )
    grad_share_own = grad_share_own.reshape(experts_all, tok_rows).T
    share_own = shares(mixer_in, expert_ids.T)
    grad_logits = (
        share_own
        * (grad_share_own - jnp.sum(share_own * grad_share_own, axis=-1, keepdims=True))
    ).astype(BF16)
    (grad_up,) = row_grads((early_rows, late_rows), (early_part[3], late_part[3]))
    grad_up, grad_logits, early_active, late_active = window(
        [entered_ring], grad_up, grad_logits, early_part[1], late_part[1]
    )
    grad_up = lax.psum_scatter(grad_up, "fsdp", scatter_dimension=1, tiled=True)
    grad_middle, grad_branch, grad_gain_m = by_rows(
        mixer_back_kernel,
        entered_ring.landed(),
        [middle, cotangent],
        [grad_logits, router_w, gain_mlp],
        [F32, BF16],
        [(1, model_width)],
    )

    grads_ring = Gather(ring, grad_branch)
    early_active, late_active = prepare([grads_ring], early_active, late_active)
    produced = [
        jnp.einsum("etf,efd->td", active, down_w, preferred_element_type=F32).astype(BF16)
        for active in (early_active, late_active)
    ]
    produced, early_active, late_active = window(
        [grads_ring], produced, early_active, late_active
    )
    early_active, late_active = prepare([grads_ring], early_active, late_active)
    down_parts = down_grads((early_active, late_active), cot_all, fsdp.targets)
    (down_parts,) = window([grads_ring], down_parts)
    paired_down = fsdp.pair(down_parts)
    for step in range(3, cut + 1):
        window([grads_ring])

    def two_parts(parts):
        def piece(spot):
            if spot * tok_rows >= early:
                return parts[1], spot - early // tok_rows
            return parts[0], spot

        return piece

    def back(pieces, offset, before):
        return attend_back(
            pieces,
            offset,
            before,
            output_w,
            probs,
            query_seq,
            key_seq,
            value_seq,
            qk_pre,
            cos_table,
            sine_table,
            gains_qk,
            scale_qk,
        )

    grads = back(grads_ring.pieces, 0, None)
    grad_small = dot(mixer_in, jnp.pad(grad_logits, ((0, 0), (0, head_size - experts_all))), 0, 0)
    for step in range(cut + 1, ring.steps):
        grad_small, paired_down = window([grads_ring], grad_small, paired_down)
    layer_ring = Scatter(ring, two_parts(produced), tok_rows)
    (grads,) = window([grads_ring, layer_ring], grads)
    grads = back(grads_ring.pieces[2 * cut + 1 :], 2 * cut + 1, grads)
    (grads,) = window([layer_ring], grads)

    grads, grad_small, branch_pieces = prepare(
        [layer_ring], grads, grad_small, grads_ring.pieces
    )
    grad_qkv = grads[0]
    grad_parts = project_back(
        normed_all, grad_qkv, grad_small, grad_gain_m, experts_all, grads[1], own_rows, fsdp.targets
    )
    output_parts = output_back(attended, branch_pieces, fsdp.targets)
    for step in range(3, ring.steps):
        grad_parts, grad_qkv, output_parts = window(
            [layer_ring], grad_parts, grad_qkv, output_parts
        )
    paired = fsdp.pair(grad_parts)
    paired, grad_qkv, output_parts = together(paired, grad_qkv, output_parts)
    sent = fsdp.send(paired)
    paired_output = fsdp.pair(output_parts)
    grad_hidden = rows_dot(grad_qkv, qkv_w, 1, tok_rows)
    grad_hidden, paired_output = window([layer_ring], grad_hidden, paired_output)
    (produced, spot), left, right = layer_ring.landed()
    layer_out = (
        middle
        + lax.slice_in_dim(produced, 0, tok_rows, axis=0).astype(F32)
        + left.astype(F32)
        + right.astype(F32)
    ).astype(BF16)

    hidden_ring = Scatter(
        ring, lambda spot: (grad_hidden[spot], 0), tok_rows, tuple(grad_hidden[-2:])
    )
    paired, sent, paired_output, paired_down = window(
        [hidden_ring], paired, sent, paired_output, paired_down
    )
    paired, sent, paired_output, paired_down = prepare(
        [hidden_ring], paired, sent, paired_output, paired_down
    )
    total = paired[0].astype(F32) + sum(part.astype(F32) for part in sent)
    grad_qkv_w = lax.all_to_all(
        total.astype(BF16).reshape(groups, own_rows, qkv_width + head_size),
        "seq",
        split_axis=0,
        concat_axis=0,
        tiled=True,
    )
    sent_output = fsdp.send(paired_output)
    down_first = fsdp.send([part[:1] for part in paired_down])
    paired_output, sent_output, paired_down, down_first, grad_qkv_w, grad_gate, grad_up = window(
        [hidden_ring],
        paired_output,
        sent_output,
        paired_down,
        down_first,
        grad_qkv_w,
        grad_gate,
        grad_up,
    )
    paired_output, sent_output, paired_down, grad_gate, grad_up = prepare(
        [hidden_ring], paired_output, sent_output, paired_down, grad_gate, grad_up
    )
    total = paired_output[0].astype(F32) + sum(part.astype(F32) for part in sent_output)
    grad_output_w = lax.ppermute(total.astype(BF16), ALL, exchange)
    down_rest = fsdp.send([part[1:] for part in paired_down])

    def corner(array):
        return lax.slice(array, (0,) * array.ndim, (1,) * (array.ndim - 2) + (8, 128))

    grad_gate, grad_up = grad_gate.astype(F32), grad_up.astype(F32)
    corners = [corner(array) for array in (grad_gate, grad_up, layer_out)]
    for step in range(3, ring.steps):
        grad_output_w, paired_down, corners = window(
            [hidden_ring], grad_output_w, paired_down, corners
        )
    grad_output_w, paired_down = prepare([hidden_ring], grad_output_w, paired_down)
    grad_output_w = grad_output_w.astype(F32)
    grad_down = paired_down[0].astype(F32) + sum(
        jnp.concatenate(pair, axis=0).astype(F32) for pair in zip(down_first, down_rest)
    )
    window([hidden_ring], [corner(grad_down), corner(grad_output_w)])
    (grad_tokens,) = by_rows(
        tokens_back_kernel, hidden_ring.landed(), [tokens, grad_middle], [], [BF16]
    )
    grad_query_w, grad_key_w, grad_value_w, grad_gain_a, small = weights_back(
        grad_qkv_w,
        weights_own,
        attn_gain.astype(F32)[:, None],
        held_groups,
        kv_heads,
        head_size,
    )
    gains = small[:4, head_size // 2 :].reshape(2, head_size)
    cut = query_gain.shape[0]
    gains = lax.dynamic_slice(gains, (0, me * cut), (2, cut))
    return (
        layer_out,
        grad_tokens,
        grad_gain_a[:, 0],
        grad_query_w,
        grad_key_w,
        grad_value_w,
        gains[0],
        gains[1],
        grad_output_w,
        small[:, experts_all],
        small[:, :experts_all],
        grad_gate,
        grad_up,
        grad_down,
    )


def solution(mesh):
    rows = P(("fsdp", "seq"), None)
    line = P(("fsdp", "seq"))
    wide = P("seq", "fsdp", None)
    deep = P("seq", None, "fsdp")
    in_specs = (
        rows, rows, rows, line, rows, rows, rows, line, line, rows, line, rows, wide, wide, deep,
    )
    out_specs = (
        rows, rows, line, rows, rows, rows, line, line, rows, line, rows, wide, wide, deep,
    )
    return jax.shard_map(
        on_device, mesh=mesh, in_specs=in_specs, out_specs=out_specs, check_vma=False
    )
```
